512 devices in a mesh: rows: 128 (over y, z, core), rep: 4 (over x).
Axes of the slice: x: 4, y: 4, z: 16, core: 2. Of those that a mesh axis runs over, the one named last changes fastest.
Arguments:
- ratings: bfloat16 [8192, 128, 128], P(('rows', 'rep'))
- observed: int32 [8192, 16, 128], P(('rows', 'rep')), may hold values from 0 to 255
- user_start: bfloat16 [64, 524288], P(None, ('rows', 'rep')), may hold values from -2 to 2
- item_start: bfloat16 [64, 131072], P(None, ('rows', 'rep')), may hold values from -2 to 2
- exposure: int32 [131072], P(('rows', 'rep')), may hold values from 1 to 15
- serve_list: int32 [65536], P(('rows', 'rep')), may hold values from 0 to 2, as said below
- tile_slot: int32 [8192], P(('rows', 'rep')), may hold values from 0 to 127, as said below
- tile_user: int32 [8192], P(('rows', 'rep')), may hold values from 0 to 31
Outputs:
- user_factor: bfloat16 [64, 524288], P(None, ('rows', 'rep'))
- item_factor: bfloat16 [64, 131072], P(None, ('rows', 'rep'))
The draws below stay inside these ranges and needn't reach their ends.
Inputs may be any that keep to these rules, and one draw needn't show every extreme that they name: serve_list holds 2 where the requesting rows index needs no block of that owner; each device needs at most one item block from each owner of its rep group, and some owner's block in every draw. `tile_slot`: every tile points to an owner whose serve_list entry for the tile's rows index is a real block.
All inputs are finite; a program needn't handle non-finite values.
Results may differ from the reference program's by a relative error of at most 0.0068.
Values may be sent and summed in bfloat16 or wider, within the bound.
A program may use at most 64 MiB of HBM per device.

```python
import math
import jax
import jax.numpy as jnp
from jax import lax

RANK = 64
BLK = 128
LEVELS = 16
ITERS = 2
USER_BLOCKS = 8
ITEM_BLOCKS = 2
TILES_DEV = 16
NTILES = 8192
USERS = 524288
ITEMS = 131072
WORDS = 16
N_ROWS = 128
N_REP = 4


def occupancy(key):
    base_key = jax.random.fold_in(key, 7)
    split_keys = jax.random.split(base_key, 5)
    used_slot = jax.random.randint(split_keys[0], (N_ROWS, N_REP, N_ROWS), 0, 2).astype(jnp.int32)
    forced = jax.random.randint(split_keys[1], (N_ROWS, N_REP, 1), 0, N_ROWS)
    positions = jnp.arange(N_ROWS, dtype=jnp.int32)[None, None, :]
    used_slot = jnp.maximum(used_slot, (positions == forced).astype(jnp.int32))
    picked = jax.random.randint(split_keys[2], (N_ROWS, N_REP, N_ROWS), 0, ITEM_BLOCKS)
    serve_table = jnp.where(used_slot == 1, picked, ITEM_BLOCKS).astype(jnp.int32)
    serve_flat = jnp.transpose(serve_table, (2, 1, 0)).reshape(-1)
    slot_order = jnp.argsort(1 - used_slot, axis=2, stable=True).astype(jnp.int32)
    used_total = jnp.sum(used_slot, axis=2)
    chosen = jax.random.randint(split_keys[3], (N_ROWS, N_REP, TILES_DEV), 0, used_total[:, :, None])
    slot_flat = jnp.take_along_axis(slot_order, chosen, axis=2).reshape(-1).astype(jnp.int32)
    user_flat = jax.random.randint(split_keys[4], (N_ROWS * N_REP * TILES_DEV,), 0, N_REP * USER_BLOCKS).astype(jnp.int32)
    return (serve_flat, slot_flat, user_flat)


def draw_serve_list(key, part):
    return occupancy(key)[0]


def draw_tile_slot(key, part):
    return occupancy(key)[1]


def draw_tile_user(key, part):
    return occupancy(key)[2]


def draw_exposure(key, part):
    base_key = jax.random.fold_in(key, 23)
    owners = N_ROWS * N_REP
    owner_index = jnp.arange(ITEMS, dtype=jnp.int32) // (ITEM_BLOCKS * BLK)
    lowest = 1 + 3 * (owners - 1 - owner_index) // max(owners - 1, 1)
    return jax.random.randint(base_key, (ITEMS,), lowest, LEVELS).astype(jnp.int32)


def draw_ratings(key, part):
    base_key = jax.random.fold_in(key, 11)
    split_keys = jax.random.split(base_key, 2)
    tile_shape = (NTILES, BLK, BLK)
    rising = 1.0 + 2.0 * jnp.arange(NTILES, dtype=jnp.float32)[:, None, None] / NTILES
    drawn = jax.random.normal(split_keys[0], tile_shape, jnp.float32)
    row_scale = jnp.exp(jax.random.uniform(split_keys[1], (NTILES, BLK, 1), jnp.float32, 0.0, math.log(10.0)))
    rating_values = drawn * row_scale * rising / 3.0
    return rating_values.astype(jnp.bfloat16)


def set_ends(entries, own_key, least, high):
    longest = entries.shape.index(max(entries.shape))
    spots = []
    for shift in (0, 1):
        where = [jax.random.randint(jax.random.fold_in(own_key, axis), (), 0, length) for axis, length in enumerate(entries.shape)]
        where[longest] = (where[longest] + shift) % entries.shape[longest]
        spots.append(tuple(where))
    return entries.at[spots[0]].set(least).at[spots[1]].set(high)


def steps_of(stream_key, extent, cuts, least, largest):
    loudness, own = 1.0, jax.random.fold_in(stream_key, 6)
    for axis_at, blocks in cuts:
        draws = jnp.exp(jax.random.uniform(jax.random.fold_in(own, axis_at), (blocks,), jnp.float32, least / len(cuts), largest / len(cuts)))
        loudness = loudness * jnp.repeat(draws, extent[axis_at] // blocks).reshape([-1 if axis == axis_at else 1 for axis in range(len(extent))])
    return loudness


def scatter_about(own_key, shape, scale, bound, cuts=(), kind=jnp.bfloat16):
    result = scale * jax.random.normal(own_key, shape, jnp.float32)
    if cuts:
        result = result * steps_of(own_key, shape, cuts, -0.22, 0.18)
    return jnp.clip(result, -bound, bound).astype(kind)


def setup_inputs(seed: int = 0) -> dict:
    splits = jax.random.split(jax.random.key(seed), 9)
    return {
        "ratings": draw_ratings(jax.random.fold_in(splits[8], 71), 0),
        "observed": set_ends(jax.random.randint(splits[1], (NTILES, WORDS, BLK), 0, 256), jax.random.fold_in(splits[1], 1), 0, 255).astype(jnp.int32),
        "user_start": scatter_about(splits[2], (RANK, USERS), 0.35, 2.0, ((1, 512),)),
        "item_start": scatter_about(splits[3], (RANK, ITEMS), 0.35, 2.0, ((1, 512),)),
        "exposure": draw_exposure(jax.random.fold_in(splits[8], 71), 0),
        "serve_list": draw_serve_list(jax.random.fold_in(splits[8], 71), 0),
        "tile_slot": draw_tile_slot(jax.random.fold_in(splits[8], 71), 0),
        "tile_user": draw_tile_user(jax.random.fold_in(splits[8], 71), 0),
    }


def unpack_mask(packed_words):
    bit_shifts = jnp.arange(8, dtype=jnp.int32)
    bit_values = jnp.bitwise_and(jnp.right_shift(packed_words[:, :, :, None], bit_shifts), 1)
    bit_values = jnp.transpose(bit_values, (0, 2, 1, 3))
    return bit_values.reshape(packed_words.shape[0], packed_words.shape[2], packed_words.shape[1] * 8).astype(jnp.float32)

def residual_block(rating_part, word_part, user_part, item_part, weight_part):
    predicted = jnp.einsum('gku,gki->gui', user_part.astype(jnp.float32), item_part.astype(jnp.float32))
    deviation = rating_part.astype(jnp.float32) - predicted
    observed_mask = unpack_mask(word_part)
    return (observed_mask * weight_part[:, None, :].astype(jnp.float32) * deviation).astype(jnp.bfloat16)

def orthonormal(raw_factor, row_count):
    gram_total = jnp.dot(raw_factor, raw_factor.T, precision=lax.Precision.HIGHEST)
    cholesky_factor = jnp.linalg.cholesky(gram_total / row_count)
    return jax.scipy.linalg.solve_triangular(cholesky_factor, raw_factor, lower=True).astype(jnp.bfloat16)

def to_blocks(factor, tile_side):
    return jnp.transpose(factor.reshape(factor.shape[0], -1, tile_side), (1, 0, 2))

def from_blocks(blocks):
    return jnp.transpose(blocks, (1, 0, 2)).reshape(blocks.shape[1], -1)

def reference(ratings, observed, user_start, item_start, exposure, serve_list, tile_slot, tile_user):
    tile_count = ratings.shape[0]
    tile_side = ratings.shape[2]
    tile_ids = jnp.arange(tile_count, dtype=jnp.int32)
    device = tile_ids // TILES_DEV
    row_index = device // N_REP
    rep_index = device % N_REP
    user_block = (row_index * (N_REP * USER_BLOCKS) + tile_user).astype(jnp.int32)
    owner_index = (tile_slot * N_REP + rep_index).astype(jnp.int32)
    item_block = (owner_index * ITEM_BLOCKS + serve_list[owner_index * N_ROWS + row_index]).astype(jnp.int32)
    weight = ((LEVELS + 1.0) / (exposure.astype(jnp.float32) + 1.0)).astype(jnp.bfloat16).reshape(-1, tile_side)
    user_blocks = to_blocks(user_start, tile_side)
    item_blocks = to_blocks(item_start, tile_side)
    group_size = math.gcd(tile_count, 512)
    block_count = tile_count // group_size
    pieces = (ratings.reshape(block_count, group_size, tile_side, tile_side), observed.reshape(block_count, group_size, observed.shape[1], tile_side), user_block.reshape(block_count, group_size), item_block.reshape(block_count, group_size))
    rank_size = user_start.shape[0]

    def user_half(query_blocks):

        def advance(running, piece):
            rating_part, word_part, user_idx, item_idx = piece
            residual = residual_block(rating_part, word_part, user_blocks[user_idx], item_blocks[item_idx], weight[item_idx])
            contrib = jnp.einsum('gki,gui->gku', query_blocks[item_idx].astype(jnp.float32), residual.astype(jnp.float32))
            return (running.at[user_idx].add(contrib), None)
        start_sum = jnp.zeros((user_blocks.shape[0], rank_size, tile_side), jnp.float32)
        return from_blocks(lax.scan(advance, start_sum, pieces)[0])

    def item_half(new_users):

        def advance(running, piece):
            rating_part, word_part, user_idx, item_idx = piece
            residual = residual_block(rating_part, word_part, user_blocks[user_idx], item_blocks[item_idx], weight[item_idx])
            contrib = jnp.einsum('gku,gui->gki', new_users[user_idx].astype(jnp.float32), residual.astype(jnp.float32))
            return (running.at[item_idx].add(contrib), None)
        start_sum = jnp.zeros((item_blocks.shape[0], rank_size, tile_side), jnp.float32)
        return from_blocks(lax.scan(advance, start_sum, pieces)[0])
    query_blocks = item_blocks
    user_factor = user_start
    item_factor = item_start
    for sweep_index in range(ITERS):
        raw_user = user_half(query_blocks)
        user_factor = orthonormal(raw_user, raw_user.shape[1] * 1.0)
        raw_item = item_half(to_blocks(user_factor, tile_side))
        item_factor = orthonormal(raw_item, raw_item.shape[1] * 1.0)
        query_blocks = to_blocks(item_factor, tile_side)
    return (user_factor, item_factor)
```

```python
import functools

import jax
import jax.numpy as jnp
from jax import lax
from jax.experimental import pallas as pl
from jax.experimental.pallas import tpu as pltpu
from jax.sharding import PartitionSpec as P

LEVELS = 16
ITERS = 2
MESH = pl.DeviceIdType.MESH
BF = jnp.bfloat16
F32 = jnp.float32
STRIP = 16
VMEM_LIMIT = 48 * 1024 * 1024


class Grid:
    def __init__(self, rows, rep):
        self.c = 2
        self.x = rep
        self.y = 4 if rows % 16 == 0 else 2
        self.z = rows // (self.c * self.y)


def place(grid):
    r = lax.axis_index("rows")
    x = lax.axis_index("rep")
    y = r // (grid.z * grid.c)
    z = (r // grid.c) % grid.z
    return x, y, z, r % grid.c


def row_of(grid, y, z, c):
    return (y * grid.z + z) * grid.c + c


def remote(src, dst, send_sem, recv_sem, r, x):
    return pltpu.make_async_remote_copy(
        src_ref=src,
        dst_ref=dst,
        send_sem=send_sem,
        recv_sem=recv_sem,
        device_id=(r, x),
        device_id_type=MESH,
    )


def greet(targets):
    barrier = pltpu.get_barrier_semaphore()
    for r, x in targets:
        pl.semaphore_signal(barrier, inc=1, device_id=(r, x), device_id_type=MESH)
    pl.semaphore_wait(barrier, len(targets))


def peers_x(grid, r, x):
    return [(r, (x + i) % grid.x) for i in range(1, grid.x)]


def peers_yc(grid, x, y, z, c):
    out = []
    for i in range(grid.y):
        for j in range(grid.c):
            if i or j:
                out.append((row_of(grid, (y + i) % grid.y, z, (c + j) % 2), x))
    return out


def peers_z(grid, x, y, z, c):
    return [(row_of(grid, y, (z + i) % grid.z, c), x) for i in range(1, grid.z)]


def plane_gather(grid, place_, buf, y_send, y_recv, z_send, z_recv, c_send, c_recv):
    x, y, z, c = place_
    half = grid.y // 2
    steps = grid.z // 2
    mine = row_of(grid, y, z, c)

    def y_copy(to, slot):
        block = buf.at[c, z, slot]
        return remote(block, block, y_send.at[to], y_recv.at[slot], row_of(grid, to, z, c), x)

    for i in range(1, grid.y):
        y_copy((y + i) % grid.y, y).start()

    def part(zz, h):
        return buf.at[c, zz, pl.ds(h * half, half)]

    def z_copy(s, h, way):
        zz = (z - s + grid.z) % grid.z if way == 0 else (z + s) % grid.z
        to = (z + 1) % grid.z if way == 0 else (z - 1 + grid.z) % grid.z
        return remote(
            part(zz, h),
            part(zz, h),
            z_send.at[way, s, h],
            z_recv.at[way, s, h],
            row_of(grid, y, to, c),
            x,
        )

    def c_copy(zz, h):
        return remote(
            part(zz, h),
            part(zz, h),
            c_send.at[zz, h],
            c_recv.at[zz, h],
            row_of(grid, y, z, 1 - c),
            x,
        )

    def c_arrival(zz, h):
        there = buf.at[1 - c, zz, pl.ds(h * half, half)]
        return remote(there, there, c_send.at[zz, h], c_recv.at[zz, h], row_of(grid, y, z, 1 - c), x)

    for i in range(1, grid.y):
        y_copy((y + i) % grid.y, (y + i) % grid.y).wait_recv()

    for h in range(2):
        for way in range(2):
            z_copy(0, h, way).start()
        c_copy(z, h).start()

    @pl.loop(1, steps)
    def _(s):
        for h in range(2):
            for way in range(2):
                z_copy(s - 1, h, way).wait_recv()
            zr = (z - s + grid.z) % grid.z
            zl = (z + s) % grid.z

            @pl.when((s < steps - 1) | (h == 0))
            def _():
                z_copy(s, h, 0).start()

            @pl.when((s < steps - 1) | (h == 1))
            def _():
                z_copy(s, h, 1).start()

            c_copy(zr, h).start()
            c_copy(zl, h).start()

    far = (z + steps) % grid.z
    last = steps - 1
    z_copy(last, 0, 0).wait_recv()
    c_copy(far, 0).start()
    z_copy(last, 1, 1).wait_recv()
    c_copy(far, 1).start()

    for i in range(1, grid.y):
        y_copy((y + i) % grid.y, y).wait_send()

    @pl.loop(0, steps)
    def _(s):
        for h in range(2):

            @pl.when((s < steps - 1) | (h == 0))
            def _():
                z_copy(s, h, 0).wait_send()

            @pl.when((s < steps - 1) | (h == 1))
            def _():
                z_copy(s, h, 1).wait_send()

    @pl.loop(0, grid.z)
    def _(zz):
        for h in range(2):
            c_copy(zz, h).wait_send()
            c_arrival(zz, h).wait_recv()


def plane_sems(grid):
    return [
        pltpu.SemaphoreType.DMA((grid.y,)),
        pltpu.SemaphoreType.DMA((grid.y,)),
        pltpu.SemaphoreType.DMA((2, grid.z // 2, 2)),
        pltpu.SemaphoreType.DMA((2, grid.z // 2, 2)),
        pltpu.SemaphoreType.DMA((grid.z, 2)),
        pltpu.SemaphoreType.DMA((grid.z, 2)),
    ]


def plane_targets(grid, x, y, z, c):
    out = [(row_of(grid, (y + i) % grid.y, z, c), x) for i in range(1, grid.y)]
    out += [(row_of(grid, y, (z + 1) % grid.z, c), x), (row_of(grid, y, (z - 1 + grid.z) % grid.z, c), x)]
    return out + [(row_of(grid, y, z, 1 - c), x)]


def x_gather(grid, place_, users, send, recv):
    x, y, z, c = place_
    r = row_of(grid, y, z, c)

    per = users.shape[0] // grid.x

    def copy(to, slot):
        block = users.at[pl.ds(slot * per, per)]
        return remote(block, block, send.at[to], recv.at[slot], r, to)

    def start():
        for i in range(1, grid.x):
            copy((x + i) % grid.x, x).start()

    def finish():
        for i in range(1, grid.x):
            copy((x + i) % grid.x, (x + i) % grid.x).wait_recv()
        for i in range(1, grid.x):
            copy((x + i) % grid.x, x).wait_send()

    return start, finish


def first_gather_kernel(grid, chunk, own_users, buf, users, x_send, x_recv, *sems):
    place_ = x, y, z, c = place(grid)
    buf[c, z, y] = chunk[...]
    users[pl.ds(x * own_users.shape[0], own_users.shape[0])] = own_users[...]
    greet(plane_targets(grid, x, y, z, c) + peers_x(grid, row_of(grid, y, z, c), x))
    start, finish = x_gather(grid, place_, users, x_send, x_recv)
    start()
    plane_gather(grid, place_, buf, *sems)
    finish()


def first_gather(grid, chunk, own_users):
    return pl.pallas_call(
        functools.partial(first_gather_kernel, grid),
        out_shape=(
            jax.ShapeDtypeStruct((2, grid.z, grid.y) + chunk.shape, BF),
            jax.ShapeDtypeStruct((grid.x * own_users.shape[0],) + own_users.shape[1:], BF),
        ),
        in_specs=[pl.BlockSpec(memory_space=pltpu.VMEM)] * 2,
        out_specs=(pl.BlockSpec(memory_space=pltpu.VMEM),) * 2,
        scratch_shapes=[pltpu.SemaphoreType.DMA((grid.x,))] * 2 + plane_sems(grid),
        compiler_params=pltpu.CompilerParams(
            collective_id=0, has_side_effects=True, vmem_limit_bytes=VMEM_LIMIT
        ),
    )(chunk, own_users)


def item_gather_kernel(grid, chunk, buf, *sems):
    place_ = x, y, z, c = place(grid)
    buf[c, z, y] = chunk[...]
    greet(plane_targets(grid, x, y, z, c))
    plane_gather(grid, place_, buf, *sems)


def item_gather(grid, chunk):
    return pl.pallas_call(
        functools.partial(item_gather_kernel, grid),
        out_shape=jax.ShapeDtypeStruct((2, grid.z, grid.y) + chunk.shape, BF),
        in_specs=[pl.BlockSpec(memory_space=pltpu.VMEM)],
        out_specs=pl.BlockSpec(memory_space=pltpu.VMEM),
        scratch_shapes=plane_sems(grid),
        compiler_params=pltpu.CompilerParams(
            collective_id=1, has_side_effects=True, vmem_limit_bytes=VMEM_LIMIT
        ),
    )(chunk)


def gram_sum(grid, place_, gram, part, first, second, third, whole, sems):
    x, y, z, c = place_
    r = row_of(grid, y, z, c)
    s1, r1, s2, r2, s3, r3, s4, r4 = sems
    k = gram.shape[0]
    rows = k // grid.x
    low = rows // 2
    for p in range(grid.x):
        part[p] = jnp.concatenate(
            [gram[p * rows : p * rows + low], gram[p * rows + low : (p + 1) * rows]], axis=1
        )

    def one(to, slot):
        return remote(part.at[to], first.at[slot], s1.at[to], r1.at[slot], r, to)

    first[x] = part[x]
    for i in range(1, grid.x):
        one((x + i) % grid.x, x).start()
    for i in range(1, grid.x):
        one((x + i) % grid.x, (x + i) % grid.x).wait_recv()
    total = first[0]
    for i in range(1, grid.x):
        total = total + first[i]

    here = y * grid.c + c
    second[here] = total

    def two(to, slot):
        return remote(
            second.at[here],
            second.at[slot],
            s2.at[to],
            r2.at[slot],
            row_of(grid, to // grid.c, z, to % grid.c),
            x,
        )

    group = grid.y * grid.c
    for i in range(1, group):
        two((here + i) % group, here).start()
    for i in range(1, group):
        two((here + i) % group, (here + i) % group).wait_recv()
    total = second[0]
    for i in range(1, group):
        total = total + second[i]

    third[z] = total

    def three(to, slot):
        return remote(third.at[z], third.at[slot], s3.at[to], r3.at[slot], row_of(grid, y, to, c), x)

    for i in range(1, grid.z):
        three((z + i) % grid.z, z).start()
    for i in range(1, grid.z):
        three((z + i) % grid.z, (z + i) % grid.z).wait_recv()
    total = third[0]
    for i in range(1, grid.z):
        total = total + third[i]

    whole[x] = total

    def four(to, slot):
        return remote(whole.at[x], whole.at[slot], s4.at[to], r4.at[slot], r, to)

    for i in range(1, grid.x):
        four((x + i) % grid.x, x).start()
    for i in range(1, grid.x):
        four((x + i) % grid.x, (x + i) % grid.x).wait_recv()
    for i in range(1, grid.x):
        one((x + i) % grid.x, x).wait_send()
        four((x + i) % grid.x, x).wait_send()
    for i in range(1, group):
        two((here + i) % group, here).wait_send()
    for i in range(1, grid.z):
        three((z + i) % grid.z, z).wait_send()
    pieces = []
    for p in range(grid.x):
        pieces += [whole[p][:, :k], whole[p][:, k:]]
    return jnp.concatenate(pieces, axis=0)


def gram_scratch(grid, rank):
    low = rank // grid.x // 2
    shape = (low, 2 * rank)
    return [
        pltpu.VMEM((grid.x,) + shape, F32),
        pltpu.VMEM((grid.x,) + shape, F32),
        pltpu.VMEM((grid.y * grid.c,) + shape, F32),
        pltpu.VMEM((grid.z,) + shape, F32),
        pltpu.VMEM((grid.x,) + shape, F32),
    ] + [
        pltpu.SemaphoreType.DMA((n,))
        for n in (grid.x, grid.x, grid.y * grid.c, grid.y * grid.c, grid.z, grid.z, grid.x, grid.x)
    ]


def block_gram(raw, blocks):
    total = None
    for i in range(blocks):
        value = raw[i]
        one = lax.dot_general(
            value,
            value,
            (((1,), (1,)), ((), ())),
            precision=lax.Precision.HIGHEST,
            preferred_element_type=F32,
        )
        total = one if total is None else total + one
    return total


def strips_at(buf, at, count):
    return jnp.concatenate([buf[at + i] for i in range(count)], axis=0)


def residual_kernel(chunk_at, pick, user_at, buf, users, ratings, observed, out, out_t, *, rank):
    side = ratings.shape[1]
    strips = rank // STRIP

    @pl.loop(0, ratings.shape[0])
    def _(t):
        b = pick[t]
        base = chunk_at[t] * (2 * strips + 1)
        items = strips_at(buf, base + b * strips, strips)
        meta = buf[base + 2 * strips].astype(F32)
        line = lax.broadcasted_iota(jnp.int32, meta.shape, 0)
        weight = jnp.sum(jnp.where(line == b, meta, 0.0), axis=0, keepdims=True)
        guess = lax.dot_general(
            users[user_at[t]], items, (((0,), (0,)), ((), ())), preferred_element_type=F32
        )
        words = observed[t]
        spread = jnp.broadcast_to(words[:, None, :], (words.shape[0], 8, side)).reshape(side, side)
        shift = lax.broadcasted_iota(jnp.int32, (side, side), 0) % 8
        mask = ((spread >> shift) & 1).astype(F32).T
        value = mask * weight * (ratings[t].astype(F32) - guess)
        out[t] = value.astype(BF)
        out_t[t] = value.T.astype(BF)


def residual_call(rank, chunk_at, pick, user_at, buf, users, ratings, observed):
    shape = jax.ShapeDtypeStruct(ratings.shape, BF)
    return pl.pallas_call(
        functools.partial(residual_kernel, rank=rank),
        out_shape=(shape, shape),
        in_specs=[pl.BlockSpec(memory_space=pltpu.SMEM)] * 3
        + [pl.BlockSpec(memory_space=pltpu.VMEM)] * 4,
        out_specs=(pl.BlockSpec(memory_space=pltpu.VMEM),) * 2,
        compiler_params=pltpu.CompilerParams(vmem_limit_bytes=VMEM_LIMIT),
    )(chunk_at, pick, user_at, buf, users, ratings, observed)


def user_half_kernel(
    grid, rank, query_at, before, last, buf, res_t, raw, gram, sums, stage, got, send, recv, *rest
):
    place_ = x, y, z, c = place(grid)
    r = row_of(grid, y, z, c)
    per = raw.shape[0]
    greet(peers_x(grid, r, x) + peers_yc(grid, x, y, z, c) + peers_z(grid, x, y, z, c))
    sums[0] = jnp.zeros_like(sums[0])

    @pl.loop(0, res_t.shape[0])
    def _(t):
        query = strips_at(buf, query_at[t], rank // STRIP)
        product = jnp.dot(query, res_t[t], preferred_element_type=F32)
        sums[t + 1] = product + sums[before[t]]

    def copy(to, slot):
        return remote(stage.at[to], got.at[slot], send.at[to], recv.at[slot], r, to)

    for i in range(1, grid.x):
        to = (x + i) % grid.x

        @pl.loop(0, per)
        def _(j):
            stage[to, j] = sums[last[to * per + j]]

        copy(to, x).start()

    @pl.loop(0, per)
    def _(j):
        raw[j] = sums[last[x * per + j]]

    for i in range(1, grid.x):
        copy((x + i) % grid.x, (x + i) % grid.x).wait_recv()

    @pl.loop(0, per)
    def _(j):
        total = raw[j]
        for i in range(1, grid.x):
            total = total + got[(x + i) % grid.x, j]
        raw[j] = total

    gram[...] = gram_sum(grid, place_, block_gram(raw, per), *rest[:5], rest[5:])
    for i in range(1, grid.x):
        copy((x + i) % grid.x, x).wait_send()


def user_half(grid, rank, per, number, tables, buf, res_t):
    side = res_t.shape[1]
    return pl.pallas_call(
        functools.partial(user_half_kernel, grid, rank),
        out_shape=(
            jax.ShapeDtypeStruct((per, rank, side), F32),
            jax.ShapeDtypeStruct((rank, rank), F32),
        ),
        in_specs=[pl.BlockSpec(memory_space=pltpu.SMEM)] * 3
        + [pl.BlockSpec(memory_space=pltpu.VMEM)] * 2,
        out_specs=(pl.BlockSpec(memory_space=pltpu.VMEM),) * 2,
        scratch_shapes=[
            pltpu.VMEM((res_t.shape[0] + 1, rank, side), F32),
            pltpu.VMEM((grid.x, per, rank, side), F32),
            pltpu.VMEM((grid.x, per, rank, side), F32),
            pltpu.SemaphoreType.DMA((grid.x,)),
            pltpu.SemaphoreType.DMA((grid.x,)),
        ]
        + gram_scratch(grid, rank),
        compiler_params=pltpu.CompilerParams(
            collective_id=number, has_side_effects=True, vmem_limit_bytes=VMEM_LIMIT
        ),
    )(*tables, buf, res_t)


def item_half_kernel(
    grid,
    user_at,
    before,
    table,
    own_users,
    res,
    raw,
    gram,
    users,
    sums,
    near,
    stage,
    got,
    x_send,
    x_recv,
    y_send,
    y_recv,
    c_send,
    c_recv,
    z_send,
    z_recv,
    *rest,
):
    place_ = x, y, z, c = place(grid)
    r = row_of(grid, y, z, c)
    tiles = res.shape[0]
    per = own_users.shape[0]
    users[pl.ds(x * per, per)] = own_users[...]
    greet(peers_x(grid, r, x) + peers_yc(grid, x, y, z, c) + peers_z(grid, x, y, z, c))
    start, finish = x_gather(grid, place_, users, x_send, x_recv)
    start()
    sums[0] = jnp.zeros_like(sums[0])
    for cc in range(grid.c):
        for yy in range(grid.y):
            near[cc, yy, 0] = jnp.zeros(near.shape[3:], BF)
    finish()

    @pl.loop(0, tiles)
    def _(t):
        product = jnp.dot(users[user_at[t]], res[t], preferred_element_type=F32)
        total = product + sums[before[t]]
        sums[t + 1] = total
        near[c, y, t + 1] = total.astype(BF)

    def y_copy(to, slot):
        block = near.at[c, slot, pl.ds(1, tiles)]
        return remote(block, block, y_send.at[to], y_recv.at[slot], row_of(grid, to, z, c), x)

    def c_copy(core, slot):
        block = near.at[core, slot, pl.ds(1, tiles)]
        return remote(block, block, c_send.at[slot], c_recv.at[slot], row_of(grid, y, z, 1 - c), x)

    for i in range(1, grid.y):
        y_copy((y + i) % grid.y, y).start()
    c_copy(c, y).start()
    for i in range(1, grid.y):
        slot = (y + i) % grid.y
        y_copy(slot, slot).wait_recv()
        c_copy(c, slot).start()
    for i in range(grid.y):
        c_copy(1 - c, (y + i) % grid.y).wait_recv()

    def z_copy(to, slot):
        return remote(stage.at[to], got.at[slot], z_send.at[to], z_recv.at[slot], row_of(grid, y, to, c), x)

    def gathered(zz, b):
        total = None
        for cc in range(grid.c):
            for yy in range(grid.y):
                at = table[((cc * grid.y + yy) * grid.z + zz) * 2 + b]
                value = near[cc, yy, at].astype(F32)
                total = value if total is None else total + value
        return total

    @pl.loop(1, grid.z)
    def _(i):
        to = (z + i) % grid.z
        for b in range(2):
            stage[to, b] = gathered(to, b).astype(BF)
        z_copy(to, z).start()

    for b in range(2):
        raw[b] = gathered(z, b)

    @pl.loop(1, grid.z)
    def _(i):
        slot = (z - i + grid.z) % grid.z
        z_copy(slot, slot).wait_recv()
        for b in range(2):
            raw[b] = raw[b] + got[slot, b].astype(F32)

    gram[...] = gram_sum(grid, place_, block_gram(raw, 2), *rest[:5], rest[5:])
    for i in range(1, grid.y):
        y_copy((y + i) % grid.y, y).wait_send()
    for i in range(grid.y):
        c_copy(c, (y + i) % grid.y).wait_send()

    @pl.loop(1, grid.z)
    def _(i):
        z_copy((z + i) % grid.z, z).wait_send()


def item_half(grid, rank, tables, own_users, res):
    tiles, side = res.shape[:2]
    return pl.pallas_call(
        functools.partial(item_half_kernel, grid),
        out_shape=(
            jax.ShapeDtypeStruct((2, rank, side), F32),
            jax.ShapeDtypeStruct((rank, rank), F32),
        ),
        in_specs=[pl.BlockSpec(memory_space=pltpu.SMEM)] * 3
        + [pl.BlockSpec(memory_space=pltpu.VMEM)] * 2,
        out_specs=(pl.BlockSpec(memory_space=pltpu.VMEM),) * 2,
        scratch_shapes=[
            pltpu.VMEM((grid.x * own_users.shape[0],) + own_users.shape[1:], BF),
            pltpu.VMEM((tiles + 1, rank, side), F32),
            pltpu.VMEM((grid.c, grid.y, tiles + 1, rank, side), BF),
            pltpu.VMEM((grid.z, 2, rank, side), BF),
            pltpu.VMEM((grid.z, 2, rank, side), BF),
        ]
        + [
            pltpu.SemaphoreType.DMA((n,))
            for n in (grid.x, grid.x, grid.y, grid.y, grid.y, grid.y, grid.z, grid.z)
        ]
        + gram_scratch(grid, rank),
        compiler_params=pltpu.CompilerParams(
            collective_id=3, has_side_effects=True, vmem_limit_bytes=VMEM_LIMIT
        ),
    )(*tables, own_users, res)


def orthonormal(raw_blocks, gram_total, row_count):
    rank = gram_total.shape[0]
    factor = jnp.linalg.cholesky(gram_total / row_count)
    raw = jnp.transpose(raw_blocks, (1, 0, 2)).reshape(rank, -1)
    return jax.scipy.linalg.solve_triangular(factor, raw, lower=True).astype(BF)


def to_blocks(factor, side):
    return jnp.transpose(factor.reshape(factor.shape[0], -1, side), (1, 0, 2))


def links(ids):
    n = ids.shape[0]
    at = jnp.arange(n, dtype=jnp.int32)
    same = (ids[:, None] == ids[None, :]) & (at[None, :] < at[:, None])
    return jnp.max(jnp.where(same, at[None, :] + 1, 0), axis=1)


def local(grid, ratings, observed, user_start, item_start, exposure, serve_list, tile_slot, tile_user):
    side = ratings.shape[2]
    rank, own_users = user_start.shape
    tiles = ratings.shape[0]
    owners = grid.y * grid.z * grid.c
    user_count = own_users * owners * grid.x * 1.0
    item_count = item_start.shape[1] * owners * grid.x * 1.0
    per = own_users // side
    x, y, z, c = place(grid)

    weight = ((LEVELS + 1.0) / (exposure.astype(F32) + 1.0)).astype(BF).reshape(2, side)
    meta = jnp.zeros((16, side), BF)
    meta = meta.at[0:2].set(weight)
    meta = meta.at[2, :owners].set(serve_list.astype(BF))
    meta = meta.at[3, :tiles].set(tile_slot.astype(BF))
    chunk = jnp.concatenate([to_blocks(item_start, side).reshape(-1, STRIP, side), meta[None]], 0)
    buf, users = first_gather(grid, chunk, to_blocks(user_start, side))

    notes = buf[:, :, :, 2 * rank // STRIP, 2:4, :].astype(jnp.int32)
    group = lax.dynamic_index_in_dim(notes, z, 1, keepdims=False)[:, :, 1, :tiles]
    slots = group.reshape(grid.c * grid.y, tiles)
    serves = notes[:, :, :, 0, :owners].reshape(owners, grid.y, grid.z, grid.c)
    serves = lax.dynamic_index_in_dim(serves, z, 2, keepdims=False)
    serves = jnp.transpose(serves, (2, 1, 0)).reshape(grid.c * grid.y, owners)
    sy = slots // (grid.z * grid.c)
    sz = (slots // grid.c) % grid.z
    sc = slots % grid.c
    where = (sc * grid.z + sz) * grid.y + sy
    hit = where[:, :, None] == jnp.arange(owners, dtype=jnp.int32)
    picks = jnp.sum(jnp.where(hit, serves[:, None, :], 0), axis=2)
    own = c * grid.y + y
    chunk_at = lax.dynamic_index_in_dim(where, own, 0, keepdims=False)
    pick = lax.dynamic_index_in_dim(picks, own, 0, keepdims=False)
    before_item = links(chunk_at * 2 + pick)
    place_of = jnp.where((sy == y) & (sc == c), sz * 2 + picks, -1)
    table = jnp.max(
        jnp.where(
            place_of[:, None, :] == jnp.arange(2 * grid.z, dtype=jnp.int32)[None, :, None],
            jnp.arange(1, tiles + 1, dtype=jnp.int32),
            0,
        ),
        axis=2,
    ).reshape(-1)
    before_user = links(tile_user)
    last_user = jnp.max(
        jnp.where(
            tile_user[None, :] == jnp.arange(grid.x * per, dtype=jnp.int32)[:, None],
            jnp.arange(1, tiles + 1, dtype=jnp.int32),
            0,
        ),
        axis=1,
    )

    strips = rank // STRIP
    flat = buf.reshape(-1, STRIP, side)
    query_at = chunk_at * (2 * strips + 1) + pick * strips
    res, res_t = residual_call(
        rank, chunk_at, pick, tile_user, flat, users, ratings, observed
    )
    query = flat
    for sweep in range(ITERS):
        raw_user, gram_user = user_half(
            grid, rank, per, 2 if sweep == 0 else 4, (query_at, before_user, last_user), query, res_t
        )
        user_factor = orthonormal(raw_user, gram_user, user_count)
        raw_item, gram_item = item_half(
            grid, rank, (tile_user, before_item, table), to_blocks(user_factor, side), res
        )
        item_factor = orthonormal(raw_item, gram_item, item_count)
        if sweep + 1 < ITERS:
            chunk = to_blocks(item_factor, side).reshape(-1, STRIP, side)
            query = item_gather(grid, chunk).reshape(-1, STRIP, side)
            query_at = (chunk_at * 2 + pick) * strips
    return user_factor, item_factor


def solution(mesh):
    grid = Grid(mesh.shape["rows"], mesh.shape["rep"])
    both = P(("rows", "rep"))
    second = P(None, ("rows", "rep"))
    return jax.shard_map(
        functools.partial(local, grid),
        mesh=mesh,
        in_specs=(both, both, second, second, both, both, both, both),
        out_specs=(second, second),
        check_vma=False,
    )
```

```python
import functools

import jax
import jax.numpy as jnp
from jax import lax
from jax.experimental import pallas as pl
from jax.experimental.pallas import tpu as pltpu
from jax.sharding import PartitionSpec as P

LEVELS = 16
ITERS = 2
MESH = pl.DeviceIdType.MESH
BF = jnp.bfloat16
F32 = jnp.float32
HIGHEST = lax.Precision.HIGHEST
VMEM_LIMIT = 48 * 1024 * 1024


class Grid:
    def __init__(self, rows, rep):
        self.c = 2
        self.x = rep
        self.y = 4
        self.z = rows // (self.c * self.y)


class Here:
    def __init__(self, grid):
        r = lax.axis_index("rows")
        self.grid = grid
        self.r = r
        self.x = lax.axis_index("rep")
        self.y = r // (grid.z * grid.c)
        self.z = (r // grid.c) % grid.z
        self.c = r % grid.c

    def along_x(self, to):
        return self.r, to

    def along_y(self, to):
        return (to * self.grid.z + self.z) * self.grid.c + self.c, self.x

    def along_z(self, to):
        return (self.y * self.grid.z + to) * self.grid.c + self.c, self.x

    def along_yc(self, to):
        y, c = to // self.grid.c, to % self.grid.c
        return (y * self.grid.z + self.z) * self.grid.c + c, self.x

    def other_core(self):
        return (self.y * self.grid.z + self.z) * self.grid.c + 1 - self.c, self.x

    def z_off(self, by):
        return (self.z + by + 2 * self.grid.z) % self.grid.z

    def far_z(self):
        return [4 * k for k in range(1, self.grid.z // 4)]

    def greet(self):
        grid = self.grid
        targets = [self.along_x((self.x + i) % grid.x) for i in range(1, grid.x)]
        for i in range(grid.y):
            for j in range(grid.c):
                if i or j:
                    to = ((self.y + i) % grid.y) * grid.c + (self.c + j) % 2
                    targets.append(self.along_yc(to))
        offsets = {o % grid.z for o in [1, 2, 3, -1, -2, -3] + self.far_z()} - {0}
        targets += [self.along_z(self.z_off(o)) for o in sorted(offsets)]
        barrier = pltpu.get_barrier_semaphore()
        for target in targets:
            pl.semaphore_signal(barrier, inc=1, device_id=target, device_id_type=MESH)
        pl.semaphore_wait(barrier, len(targets))


def remote(src, dst, send_sem, recv_sem, device):
    return pltpu.make_async_remote_copy(
        src_ref=src,
        dst_ref=dst,
        send_sem=send_sem,
        recv_sem=recv_sem,
        device_id=device,
        device_id_type=MESH,
    )


def sems(*shape):
    return pltpu.SemaphoreType.DMA(shape)


def spread_x(here, buf, per, send, recv):
    n = here.grid.x

    def copy(to, slot):
        block = buf.at[pl.ds(slot * per, per)]
        return remote(block, block, send.at[to], recv.at[slot], here.along_x(to))

    for i in range(1, n):
        copy((here.x + i) % n, here.x).start()
    yield
    for i in range(1, n):
        copy((here.x + i) % n, (here.x + i) % n).wait_recv()
    yield
    for i in range(1, n):
        copy((here.x + i) % n, here.x).wait_send()
    yield


def spread_z_sems(grid):
    far = grid.z // 4
    return [sems(far), sems(far), sems(far, 4), sems(far, 4), sems(1), sems(1)]


def spread_z(here, buf, n, far_send, far_recv, near_send, near_recv, c_send, c_recv):
    grid = here.grid
    half = n // 2
    far = grid.z // 4

    def chunk(core, zz, start=0, count=n):
        return buf.at[pl.ds((core * grid.z + zz) * n + start, count)]

    def far_copy(k):
        block = chunk(here.c, here.z)
        return remote(block, block, far_send.at[k], far_recv.at[k], here.along_z(here.z_off(4 * k)))

    def far_arrival(k):
        block = chunk(here.c, here.z_off(-4 * k))
        return remote(block, block, far_send.at[k], far_recv.at[k], here.along_z(here.z_off(-4 * k)))

    ways = [(1, 0, n), (-1, 0, n), (-2, 0, half), (2, half, half)]

    def near_copy(k, way):
        by, start, count = ways[way]
        block = chunk(here.c, here.z_off(-4 * k), start, count)
        return remote(
            block, block, near_send.at[k, way], near_recv.at[k, way], here.along_z(here.z_off(by))
        )

    def near_arrival(k, way):
        by, start, count = ways[way]
        block = chunk(here.c, here.z_off(-by - 4 * k), start, count)
        return remote(
            block, block, near_send.at[k, way], near_recv.at[k, way], here.along_z(here.z_off(-by))
        )

    for k in range(1, far):
        far_copy(k).start()
    for way in range(4):
        near_copy(0, way).start()
    yield
    for k in range(1, far):
        far_arrival(k).wait_recv()
        for way in range(4):
            near_copy(k, way).start()
    yield
    for k in range(far):
        for way in range(4):
            near_arrival(k, way).wait_recv()
    line = buf.at[pl.ds(here.c * grid.z * n, grid.z * n)]
    swap = remote(line, line, c_send.at[0], c_recv.at[0], here.other_core())
    swap.start()
    yield
    line = buf.at[pl.ds((1 - here.c) * grid.z * n, grid.z * n)]
    remote(line, line, c_send.at[0], c_recv.at[0], here.other_core()).wait_recv()
    yield
    swap.wait_send()
    for k in range(far):
        if k:
            far_copy(k).wait_send()
        for way in range(4):
            near_copy(k, way).wait_send()
    yield


def exchange(n, me, device, put, take, send, recv):
    def copy(to):
        return remote(put(to), take(me), send.at[to], recv.at[me], device(to))

    def arrival(slot):
        return remote(put(slot), take(slot), send.at[slot], recv.at[slot], device(slot))

    for i in range(1, n):
        copy((me + i) % n).start()
    yield
    for i in range(1, n):
        arrival((me + i) % n).wait_recv()
    yield
    for i in range(1, n):
        copy((me + i) % n).wait_send()
    yield


def add_up(ref, n):
    total = ref[0]
    for i in range(1, n):
        total = total + ref[i]
    return total


def gram_scratch(grid, rank):
    shape = (rank // grid.x // 2, 2 * rank)
    counts = [grid.x, grid.y * grid.c, 4, grid.z // 4, grid.x]
    buffers = [pltpu.VMEM((n,) + shape, F32) for n in [grid.x] + counts]
    return buffers + [sems(n) for n in counts for _ in range(2)] + [pltpu.VMEM((rank, 2 * rank), F32)]


def gram_steps(here, raw, blocks, row_count, scratch):
    grid = here.grid
    part, first, second, third, fourth, whole = scratch[:6]
    pairs = [scratch[6 + 2 * i : 8 + 2 * i] for i in range(5)]
    work = scratch[-1]
    total = None
    for i in range(blocks):
        value = raw[i]
        one = lax.dot_general(
            value, value, (((1,), (1,)), ((), ())), precision=HIGHEST, preferred_element_type=F32
        )
        total = one if total is None else total + one
    k = total.shape[0]
    rows = k // grid.x
    low = rows // 2
    for p in range(grid.x):
        part[p] = jnp.concatenate(
            [total[p * rows : p * rows + low], total[p * rows + low : (p + 1) * rows]], axis=1
        )
    x, z = here.x, here.z
    group = here.y * grid.c + here.c
    level, across = z // 4, z % 4
    first[x] = part[x]
    ends = []

    def run(n, me, device, put, ref, pair):
        steps = exchange(n, me, device, put, lambda slot: ref.at[slot], *pair)
        next(steps)
        ends.append(steps)
        return steps

    steps = run(grid.x, x, here.along_x, lambda to: part.at[to], first, pairs[0])
    yield
    next(steps)
    second[group] = add_up(first, grid.x)
    mine = second.at[group]
    steps = run(grid.y * grid.c, group, here.along_yc, lambda to: mine, second, pairs[1])
    yield
    next(steps)
    third[across] = add_up(second, grid.y * grid.c)
    mine = third.at[across]
    steps = run(4, across, lambda to: here.along_z(level * 4 + to), lambda to: mine, third, pairs[2])
    yield
    next(steps)
    fourth[level] = add_up(third, 4)
    mine = fourth.at[level]
    steps = run(
        grid.z // 4, level, lambda to: here.along_z(to * 4 + across), lambda to: mine, fourth, pairs[3]
    )
    yield
    next(steps)
    whole[x] = add_up(fourth, grid.z // 4)
    mine = whole.at[x]
    steps = run(grid.x, x, here.along_x, lambda to: mine, whole, pairs[4])
    yield
    next(steps)
    row = lax.broadcasted_iota(jnp.int32, (low, k), 0)
    lane = lax.broadcasted_iota(jnp.int32, (low, k), 1)
    for p in range(grid.x):
        for h in range(2):
            at = p * rows + h * low
            unit = jnp.where(row + at == lane, 1.0, 0.0).astype(F32)
            value = whole[p][:, h * k : (h + 1) * k] * (1.0 / row_count)
            work[at : at + low, :] = jnp.concatenate([value, unit], axis=1)
    for steps in ends:
        next(steps)
    yield
    row = lax.broadcasted_iota(jnp.int32, (k, 2 * k), 0)
    lane = lax.broadcasted_iota(jnp.int32, (k, 2 * k), 1)

    @pl.loop(0, k)
    def _(i):
        value = work[...]
        pivot_row = work[pl.ds(i, 1), :]
        pivot = jnp.sum(jnp.where(lane[:1] == i, pivot_row, 0.0), axis=1, keepdims=True)
        column = jnp.sum(jnp.where(lane == i, value, 0.0), axis=1, keepdims=True)
        factor = jnp.where(row[:, :1] > i, column * (1.0 / pivot), 0.0)
        work[...] = value - factor * pivot_row

    value = work[...]
    diagonal = jnp.sum(jnp.where(lane == row, value, 0.0), axis=1, keepdims=True)
    work[...] = value * lax.rsqrt(diagonal)
    yield


def apply_inverse(work, value):
    k = work.shape[0]
    return jnp.dot(work[:, k:], value, precision=HIGHEST, preferred_element_type=F32)


def first_kernel(grid, chunk, note, own_users, line, notes, users, x_send, x_recv, y_send, y_recv, *rest):
    here = Here(grid)
    per = own_users.shape[0]
    n = chunk.shape[0]
    line[pl.ds((here.c * grid.z + here.z) * n, n)] = chunk[...]
    base = (here.c * grid.z + here.z) * grid.y
    notes[base + here.y] = note[...]
    users[pl.ds(here.x * per, per)] = own_users[...]
    here.greet()
    mine = notes.at[base + here.y]
    note_y = exchange(
        grid.y, here.y, here.along_y, lambda to: mine, lambda slot: notes.at[base + slot], y_send, y_recv
    )
    next(note_y)
    items = spread_z(here, line, n, *rest[:6])
    next(items)
    people = spread_x(here, users, per, x_send, x_recv)
    next(people)
    next(note_y)
    note_z = spread_z(here, notes, grid.y, *rest[6:])
    next(note_z)
    next(items)
    next(note_z)
    next(items)
    next(note_z)
    for steps in (items, note_z, people):
        next(steps)
    for steps in (items, note_z, people, note_y):
        next(steps)


def first_gather(grid, chunk, note, own_users):
    lines = 2 * grid.z
    return pl.pallas_call(
        functools.partial(first_kernel, grid),
        out_shape=(
            jax.ShapeDtypeStruct((lines * chunk.shape[0],) + chunk.shape[1:], BF),
            jax.ShapeDtypeStruct((lines * grid.y,) + note.shape, BF),
            jax.ShapeDtypeStruct((grid.x * own_users.shape[0],) + own_users.shape[1:], BF),
        ),
        in_specs=[pl.BlockSpec(memory_space=pltpu.VMEM)] * 3,
        out_specs=(pl.BlockSpec(memory_space=pltpu.VMEM),) * 3,
        scratch_shapes=[sems(grid.x)] * 2 + [sems(grid.y)] * 2 + spread_z_sems(grid) * 2,
        compiler_params=pltpu.CompilerParams(
            collective_id=0, has_side_effects=True, vmem_limit_bytes=VMEM_LIMIT
        ),
    )(chunk, note, own_users)


def residual_tiles(tables, query, notes, users, ratings, observed, out, out_t):
    tiles, side = ratings.shape[:2]

    @pl.loop(0, tiles)
    def _(t):
        meta = notes[tables["note_at"][t]].astype(F32)
        line = lax.broadcasted_iota(jnp.int32, meta.shape, 0)
        weight = jnp.sum(jnp.where(line == tables["pick"][t], meta, 0.0), axis=0, keepdims=True)
        guess = lax.dot_general(
            users[tables["user_at"][t]],
            query[tables["query_at"][t]],
            (((0,), (0,)), ((), ())),
            preferred_element_type=F32,
        )
        words = observed[t]
        spread = jnp.broadcast_to(words[:, None, :], (words.shape[0], 8, side)).reshape(side, side)
        shift = lax.broadcasted_iota(jnp.int32, (side, side), 0) % 8
        mask = ((spread >> shift) & 1).astype(F32).T
        value = mask * weight * (ratings[t].astype(F32) - guess)
        out[t] = value.astype(BF)
        out_t[t] = value.T.astype(BF)


TABLES = ("user_at", "query_at", "note_at", "pick", "ask", "user_before", "user_last", "item_before", "item_table")


def main_kernel(grid, counts, names, *refs):
    refs = list(refs)
    tables = {name: refs.pop(0) for name in TABLES}
    line, notes, users, ratings, observed, user_out, item_out = (refs.pop(0) for _ in range(7))
    scratch = {name: refs.pop(0) for name in names}
    here = Here(grid)
    tiles, side = ratings.shape[:2]
    per = user_out.shape[1] // side
    rank = user_out.shape[0]
    x, y, z, c = here.x, here.y, here.z, here.c
    res, res_t, sums = scratch["res"], scratch["res_t"], scratch["sums"]
    near_rows = tiles + 1
    far = grid.z // 4

    def of(prefix, it):
        start = f"{prefix}{it}_"
        return [ref for name, ref in scratch.items() if name.startswith(start)]

    here.greet()
    sums[0] = jnp.zeros_like(sums[0])
    for it in range(ITERS):
        near = scratch[f"near{it}"]
        for s in range(grid.c * grid.y):
            near[s * near_rows] = jnp.zeros(near.shape[1:], BF)
    ends = []
    gram_item = None
    for it in range(ITERS):
        sel, query, stage_x, got_x, raw_u, new_users, near, stage, got, fars, got_far, raw_i = (
            scratch[f"{name}{it}"]
            for name in (
                "sel",
                "query",
                "stage_x",
                "got_x",
                "raw_u",
                "users",
                "near",
                "stage",
                "got",
                "fars",
                "got_far",
                "raw_i",
            )
        )
        for i in range(grid.y):
            to = (y + i) % grid.y

            @pl.loop(0, tiles)
            def _(t):
                sel[to * tiles + t] = line[tables["ask"][to * tiles + t]]

        asked = exchange(
            grid.y,
            y,
            here.along_y,
            lambda to: sel.at[pl.ds(to * tiles, tiles)],
            lambda slot: query.at[pl.ds(slot * tiles, tiles)],
            *of("ysel", it),
        )
        next(asked)
        query[pl.ds(y * tiles, tiles)] = sel[pl.ds(y * tiles, tiles)]
        if gram_item is not None:
            next(gram_item)
        next(asked)
        ends.append(asked)
        if it == 0:
            residual_tiles(tables, query, notes, users, ratings, observed, res, res_t)

        @pl.loop(0, tiles)
        def _(t):
            product = jnp.dot(query[tables["query_at"][t]], res_t[t], preferred_element_type=F32)
            sums[t + 1] = product + sums[tables["user_before"][t]]

        for i in range(grid.x):
            to = (x + i) % grid.x

            @pl.loop(0, per)
            def _(j):
                stage_x[to * per + j] = sums[tables["user_last"][to * per + j]]

        parts = exchange(
            grid.x,
            x,
            here.along_x,
            lambda to: stage_x.at[pl.ds(to * per, per)],
            lambda slot: got_x.at[pl.ds(slot * per, per)],
            *of("xsum", it),
        )
        next(parts)
        if gram_item is not None:
            for _ in range(3):
                next(gram_item)
        next(parts)
        ends.append(parts)

        @pl.loop(0, per)
        def _(j):
            total = stage_x[x * per + j]
            for i in range(1, grid.x):
                total = total + got_x[((x + i) % grid.x) * per + j]
            if it:
                total = apply_inverse(scratch[f"gitem{it - 1}_work"], total)
            raw_u[j] = total
            new_users[x * per + j] = total.astype(BF)

        people = spread_x(here, new_users, per, *of("xall", it))
        next(people)
        gram_user = gram_steps(here, raw_u, per, counts[0], of("guser", it))
        next(gram_user)
        next(people)
        next(gram_user)
        ends.append(people)

        @pl.loop(0, tiles)
        def _(t):
            product = jnp.dot(new_users[tables["user_at"][t]], res[t], preferred_element_type=F32)
            total = product + sums[tables["item_before"][t]]
            sums[t + 1] = total
            near[(c * grid.y + y) * near_rows + 1 + t] = total.astype(BF)

        def rows_of(core, slot):
            return near.at[pl.ds((core * grid.y + slot) * near_rows + 1, tiles)]

        along = exchange(
            grid.y, y, here.along_y, lambda to: rows_of(c, y), lambda slot: rows_of(c, slot), *of("ynear", it)
        )
        next(along)
        c_send, c_recv = of("cnear", it)

        def c_copy(core, slot):
            block = rows_of(core, slot)
            return remote(block, block, c_send.at[slot], c_recv.at[slot], here.other_core())

        c_copy(c, y).start()
        next(gram_user)
        next(along)
        ends.append(along)
        for i in range(1, grid.y):
            c_copy(c, (y + i) % grid.y).start()
        next(gram_user)
        for i in range(grid.y):
            c_copy(1 - c, (y + i) % grid.y).wait_recv()

        def gathered(zz, b):
            total = None
            for s in range(grid.c * grid.y):
                at = tables["item_table"][(s * grid.z + zz) * 2 + b]
                value = near[at].astype(F32)
                total = value if total is None else total + value
            return total

        z_send, z_recv = of("znear", it)
        ways = [(1, (0, 1)), (-1, (0, 1)), (-2, (0,)), (2, (1,))]
        starts = [0, 2 * far, 4 * far, 5 * far]

        def near_z(way, arrival=False):
            by, parts_ = ways[way]
            count = len(parts_) * far
            to = here.along_z(here.z_off(-by if arrival else by))
            return remote(
                stage.at[pl.ds(starts[way], count)],
                got.at[pl.ds(starts[way], count)],
                z_send.at[way],
                z_recv.at[way],
                to,
            )

        for way, (by, parts_) in enumerate(ways):

            @pl.loop(0, far)
            def _(k):
                for j, b in enumerate(parts_):
                    zz = here.z_off(by + 4 * k)
                    stage[starts[way] + len(parts_) * k + j] = gathered(zz, b).astype(BF)

            near_z(way).start()
        next(gram_user)
        for k in range(far):
            for b in range(2):
                fars[2 * k + b] = gathered(here.z_off(4 * k), b)
        next(gram_user)
        for way in range(4):
            near_z(way, True).wait_recv()
        f_send, f_recv = of("zfar", it)
        far_stage = scratch[f"far_stage{it}"]

        def far_copy(k):
            return remote(
                far_stage.at[pl.ds(2 * k, 2)],
                got_far.at[pl.ds(2 * k, 2)],
                f_send.at[k],
                f_recv.at[k],
                here.along_z(here.z_off(4 * k)),
            )

        for k in list(range(1, far)) + [0]:
            for b in range(2):
                total = (
                    fars[2 * k + b]
                    + got[starts[0] + 2 * k + b].astype(F32)
                    + got[starts[1] + 2 * k + b].astype(F32)
                    + got[starts[2 + b] + k].astype(F32)
                )
                if k:
                    far_stage[2 * k + b] = total.astype(BF)
                else:
                    raw_i[b] = total
            if k:
                far_copy(k).start()
        next(gram_user)
        for k in range(1, far):
            far_copy(k).wait_recv()
        for b in range(2):
            total = raw_i[b]
            for k in range(1, far):
                total = total + got_far[2 * k + b].astype(F32)
            raw_i[b] = apply_inverse(scratch[f"guser{it}_work"], total)
        gram_item = gram_steps(here, raw_i, 2, counts[1], of("gitem", it))
        if it + 1 < ITERS:
            line = scratch["line"]
            for b in range(2):
                line[(c * grid.z + z) * 2 + b] = raw_i[b].astype(BF)
            items = spread_z(here, line, 2, *of("zall", it))
            next(items)
            next(gram_item)
            next(items)
            next(gram_item)
            next(items)
            next(gram_item)
            next(items)
            ends.append(items)
        else:
            next(gram_item)
            for j in range(per):
                user_out[:, j * side : (j + 1) * side] = apply_inverse(
                    scratch[f"guser{it}_work"], raw_u[j]
                ).astype(BF)
            for _ in range(6):
                next(gram_item)
            for b in range(2):
                item_out[:, b * side : (b + 1) * side] = apply_inverse(
                    scratch[f"gitem{it}_work"], raw_i[b]
                ).astype(BF)
        for i in range(grid.y):
            c_copy(c, (y + i) % grid.y).wait_send()
        for way in range(4):
            near_z(way).wait_send()
        for k in range(1, far):
            far_copy(k).wait_send()
    for steps in ends:
        next(steps)


def main_scratch(grid, rank, side, tiles, per):
    far = grid.z // 4
    block = (rank, side)

    def vmem(n, kind=BF):
        return pltpu.VMEM((n,) + block, kind)

    out = {
        "res": pltpu.VMEM((tiles, side, side), BF),
        "res_t": pltpu.VMEM((tiles, side, side), BF),
        "sums": vmem(tiles + 1, F32),
        "line": vmem(2 * grid.z * 2),
    }
    for it in range(ITERS):
        out[f"sel{it}"] = vmem(grid.y * tiles)
        out[f"query{it}"] = vmem(grid.y * tiles)
        out[f"stage_x{it}"] = vmem(grid.x * per, F32)
        out[f"got_x{it}"] = vmem(grid.x * per, F32)
        out[f"raw_u{it}"] = vmem(per, F32)
        out[f"users{it}"] = vmem(grid.x * per)
        out[f"near{it}"] = vmem(grid.c * grid.y * (tiles + 1))
        out[f"stage{it}"] = vmem(6 * far)
        out[f"got{it}"] = vmem(6 * far)
        out[f"fars{it}"] = vmem(2 * far, F32)
        out[f"far_stage{it}"] = vmem(2 * far)
        out[f"got_far{it}"] = vmem(2 * far)
        out[f"raw_i{it}"] = vmem(2, F32)
        for name, n in (
            ("ysel", grid.y),
            ("xsum", grid.x),
            ("xall", grid.x),
            ("ynear", grid.y),
            ("cnear", grid.y),
            ("znear", 4),
            ("zfar", far),
        ):
            out[f"{name}{it}_send"] = sems(n)
            out[f"{name}{it}_recv"] = sems(n)
        for i, shape in enumerate(spread_z_sems(grid)):
            out[f"zall{it}_{i}"] = shape
        for name in ("guser", "gitem"):
            shapes = gram_scratch(grid, rank)
            for i, shape in enumerate(shapes):
                out[f"{name}{it}_" + ("work" if i + 1 == len(shapes) else str(i))] = shape
    return out


def main_call(grid, counts, tables, line, notes, users, ratings, observed):
    tiles, side = ratings.shape[:2]
    rank = line.shape[1]
    per = users.shape[0] // grid.x
    scratch = main_scratch(grid, rank, side, tiles, per)
    return pl.pallas_call(
        functools.partial(main_kernel, grid, counts, tuple(scratch)),
        out_shape=(
            jax.ShapeDtypeStruct((rank, per * side), BF),
            jax.ShapeDtypeStruct((rank, 2 * side), BF),
        ),
        in_specs=[pl.BlockSpec(memory_space=pltpu.SMEM)] * len(TABLES)
        + [pl.BlockSpec(memory_space=pltpu.VMEM)] * 5,
        out_specs=(pl.BlockSpec(memory_space=pltpu.VMEM),) * 2,
        scratch_shapes=list(scratch.values()),
        compiler_params=pltpu.CompilerParams(
            collective_id=1, has_side_effects=True, vmem_limit_bytes=VMEM_LIMIT
        ),
    )(*(tables[name] for name in TABLES), line, notes, users, ratings, observed)


def to_blocks(factor, side):
    return jnp.transpose(factor.reshape(factor.shape[0], -1, side), (1, 0, 2))


def links(ids):
    at = jnp.arange(ids.shape[0], dtype=jnp.int32)
    same = (ids[:, None] == ids[None, :]) & (at[None, :] < at[:, None])
    return jnp.max(jnp.where(same, at[None, :] + 1, 0), axis=1)


def lasts(ids, n):
    tiles = ids.shape[-1]
    same = ids[..., None, :] == jnp.arange(n, dtype=jnp.int32)[:, None]
    return jnp.max(jnp.where(same, jnp.arange(1, tiles + 1, dtype=jnp.int32), 0), axis=-1)


def local(grid, ratings, observed, user_start, item_start, exposure, serve_list, tile_slot, tile_user):
    side = ratings.shape[2]
    own_users = user_start.shape[1]
    tiles = ratings.shape[0]
    owners = grid.y * grid.z * grid.c
    counts = (own_users * owners * grid.x * 1.0, item_start.shape[1] * owners * grid.x * 1.0)
    per = own_users // side
    r = lax.axis_index("rows")
    y, z, c = r // (grid.z * grid.c), (r // grid.c) % grid.z, r % grid.c

    weight = ((LEVELS + 1.0) / (exposure.astype(F32) + 1.0)).astype(BF).reshape(2, side)
    serve = jnp.zeros((1, side), BF).at[0, :owners].set(serve_list.astype(BF))
    slot = jnp.zeros((1, side), BF).at[0, :tiles].set(tile_slot.astype(BF))
    note = jnp.concatenate([weight, serve, slot, jnp.zeros((12, side), BF)], 0)
    line, notes, users = first_gather(grid, to_blocks(item_start, side), note, to_blocks(user_start, side))

    known = notes.reshape(grid.c, grid.z, grid.y, 16, side)[:, :, :, 2:4].astype(jnp.int32)
    slots = lax.dynamic_index_in_dim(known, z, 1, keepdims=False)[:, :, 1, :tiles]
    slots = slots.reshape(grid.c * grid.y, tiles)
    serves = known[:, :, :, 0, :owners].reshape(owners, grid.y, grid.z, grid.c)
    serves = lax.dynamic_index_in_dim(serves, z, 2, keepdims=False)
    serves = jnp.transpose(serves, (2, 1, 0)).reshape(grid.c * grid.y, owners)
    sy, sz, sc = slots // (grid.z * grid.c), (slots // grid.c) % grid.z, slots % grid.c
    where = (sc * grid.z + sz) * grid.y + sy
    hit = where[:, :, None] == jnp.arange(owners, dtype=jnp.int32)
    picks = jnp.sum(jnp.where(hit, serves[:, None, :], 0), axis=2)
    in_line = (sc * grid.z + sz) * 2 + picks
    asks = jnp.where(sy == y, in_line, 0).reshape(grid.c, grid.y, tiles)
    own = c * grid.y + y

    def mine(value):
        return lax.dynamic_index_in_dim(value, own, 0, keepdims=False)

    note_at, pick = mine(where), mine(picks)
    last = lasts(jnp.where((sy == y) & (sc == c), sz * 2 + picks, -1), 2 * grid.z)
    first_row = jnp.arange(grid.c * grid.y, dtype=jnp.int32)[:, None] * (tiles + 1)
    tables = {
        "user_at": tile_user,
        "query_at": mine(sy) * tiles + jnp.arange(tiles, dtype=jnp.int32),
        "note_at": note_at,
        "pick": pick,
        "ask": lax.dynamic_index_in_dim(asks, c, 0, keepdims=False).reshape(-1),
        "user_before": links(tile_user),
        "user_last": lasts(tile_user, grid.x * per),
        "item_before": links(note_at * 2 + pick),
        "item_table": (last + first_row).reshape(-1),
    }
    return main_call(grid, counts, tables, line, notes, users, ratings, observed)


def solution(mesh):
    grid = Grid(mesh.shape["rows"], mesh.shape["rep"])
    both = P(("rows", "rep"))
    second = P(None, ("rows", "rep"))
    return jax.shard_map(
        functools.partial(local, grid),
        mesh=mesh,
        in_specs=(both, both, second, second, both, both, both, both),
        out_specs=(second, second),
        check_vma=False,
    )
```

```python
import functools

import jax
import jax.numpy as jnp
from jax import lax
from jax.experimental import pallas as pl
from jax.experimental.pallas import tpu as pltpu
from jax.sharding import PartitionSpec as P

LEVELS = 16
ITERS = 2
MESH = pl.DeviceIdType.MESH
BF = jnp.bfloat16
F32 = jnp.float32
HIGHEST = lax.Precision.HIGHEST
VMEM_LIMIT = 48 * 1024 * 1024


class Grid:
    def __init__(self, rows, rep):
        self.c = 2
        self.x = rep
        self.y = 4
        self.z = rows // (self.c * self.y)


class Here:
    def __init__(self, grid):
        r = lax.axis_index("rows")
        self.grid = grid
        self.r = r
        self.x = lax.axis_index("rep")
        self.y = r // (grid.z * grid.c)
        self.z = (r // grid.c) % grid.z
        self.c = r % grid.c

    def along_x(self, to):
        return self.r, to

    def along_y(self, to):
        return (to * self.grid.z + self.z) * self.grid.c + self.c, self.x

    def along_z(self, to):
        return (self.y * self.grid.z + to) * self.grid.c + self.c, self.x

    def along_yc(self, to):
        y, c = to // self.grid.c, to % self.grid.c
        return (y * self.grid.z + self.z) * self.grid.c + c, self.x

    def other_core(self):
        return (self.y * self.grid.z + self.z) * self.grid.c + 1 - self.c, self.x

    def z_off(self, by):
        return (self.z + by + 2 * self.grid.z) % self.grid.z

    def greet(self):
        grid = self.grid
        targets = [self.along_x((self.x + i) % grid.x) for i in range(1, grid.x)]
        for i in range(grid.y):
            for j in range(grid.c):
                if i or j:
                    to = ((self.y + i) % grid.y) * grid.c + (self.c + j) % 2
                    targets.append(self.along_yc(to))
        targets += [self.along_z(self.z_off(o)) for o in range(1, grid.z)]
        barrier = pltpu.get_barrier_semaphore()
        for target in targets:
            pl.semaphore_signal(barrier, inc=1, device_id=target, device_id_type=MESH)
        pl.semaphore_wait(barrier, len(targets))


def remote(src, dst, send_sem, recv_sem, device):
    return pltpu.make_async_remote_copy(
        src_ref=src,
        dst_ref=dst,
        send_sem=send_sem,
        recv_sem=recv_sem,
        device_id=device,
        device_id_type=MESH,
    )


def sems(*shape):
    return pltpu.SemaphoreType.DMA(shape)


def spread_x(here, buf, per, send, recv):
    n = here.grid.x

    def copy(to, slot):
        block = buf.at[pl.ds(slot * per, per)]
        return remote(block, block, send.at[to], recv.at[slot], here.along_x(to))

    for i in range(1, n):
        copy((here.x + i) % n, here.x).start()
    yield
    for i in range(1, n):
        copy((here.x + i) % n, (here.x + i) % n).wait_recv()
    yield
    for i in range(1, n):
        copy((here.x + i) % n, here.x).wait_send()
    yield


def spread_z_sems(grid):
    far = grid.z // 4
    return [sems(far), sems(far), sems(far, 4), sems(far, 4), sems(1), sems(1)]


def spread_z(here, buf, n, far_send, far_recv, near_send, near_recv, c_send, c_recv):
    grid = here.grid
    half = n // 2
    far = grid.z // 4

    def chunk(core, zz, start=0, count=n):
        return buf.at[pl.ds((core * grid.z + zz) * n + start, count)]

    def far_copy(k):
        block = chunk(here.c, here.z)
        return remote(block, block, far_send.at[k], far_recv.at[k], here.along_z(here.z_off(4 * k)))

    def far_arrival(k):
        block = chunk(here.c, here.z_off(-4 * k))
        return remote(block, block, far_send.at[k], far_recv.at[k], here.along_z(here.z_off(-4 * k)))

    ways = [(1, 0, n), (-1, 0, n), (-2, 0, half), (2, half, half)]

    def near_copy(k, way):
        by, start, count = ways[way]
        block = chunk(here.c, here.z_off(-4 * k), start, count)
        return remote(
            block, block, near_send.at[k, way], near_recv.at[k, way], here.along_z(here.z_off(by))
        )

    def near_arrival(k, way):
        by, start, count = ways[way]
        block = chunk(here.c, here.z_off(-by - 4 * k), start, count)
        return remote(
            block, block, near_send.at[k, way], near_recv.at[k, way], here.along_z(here.z_off(-by))
        )

    for k in range(1, far):
        far_copy(k).start()
    for way in range(4):
        near_copy(0, way).start()
    yield
    for k in range(1, far):
        far_arrival(k).wait_recv()
        for way in range(4):
            near_copy(k, way).start()
    yield
    for k in range(far):
        for way in range(4):
            near_arrival(k, way).wait_recv()
    line = buf.at[pl.ds(here.c * grid.z * n, grid.z * n)]
    swap = remote(line, line, c_send.at[0], c_recv.at[0], here.other_core())
    swap.start()
    yield
    line = buf.at[pl.ds((1 - here.c) * grid.z * n, grid.z * n)]
    remote(line, line, c_send.at[0], c_recv.at[0], here.other_core()).wait_recv()
    yield
    swap.wait_send()
    for k in range(far):
        if k:
            far_copy(k).wait_send()
        for way in range(4):
            near_copy(k, way).wait_send()
    yield


def exchange(n, me, device, put, take, send, recv):
    def copy(to):
        return remote(put(to), take(me), send.at[to], recv.at[me], device(to))

    def arrival(slot):
        return remote(put(slot), take(slot), send.at[slot], recv.at[slot], device(slot))

    for i in range(1, n):
        copy((me + i) % n).start()
    yield
    for i in range(1, n):
        arrival((me + i) % n).wait_recv()
    yield
    for i in range(1, n):
        copy((me + i) % n).wait_send()
    yield


def add_up(ref, n):
    total = ref[0]
    for i in range(1, n):
        total = total + ref[i]
    return total


def gram_scratch(grid, rank):
    shape = (rank // grid.x // 2, 2 * rank)
    counts = [grid.x, grid.y * grid.c, grid.z, grid.x]
    buffers = [pltpu.VMEM((n,) + shape, F32) for n in [grid.x] + counts]
    return buffers + [sems(n) for n in counts for _ in range(2)] + [pltpu.VMEM((rank, 2 * rank), F32)]


def gram_steps(here, raw, blocks, row_count, scratch):
    grid = here.grid
    part, first, second, third, whole = scratch[:5]
    pairs = [scratch[5 + 2 * i : 7 + 2 * i] for i in range(4)]
    work = scratch[-1]
    total = None
    for i in range(blocks):
        value = raw[i]
        one = lax.dot_general(
            value, value, (((1,), (1,)), ((), ())), precision=HIGHEST, preferred_element_type=F32
        )
        total = one if total is None else total + one
    k = total.shape[0]
    rows = k // grid.x
    low = rows // 2
    for p in range(grid.x):
        part[p] = jnp.concatenate(
            [total[p * rows : p * rows + low], total[p * rows + low : (p + 1) * rows]], axis=1
        )
    x, z = here.x, here.z
    group = here.y * grid.c + here.c
    first[x] = part[x]
    ends = []

    def run(n, me, device, put, ref, pair):
        steps = exchange(n, me, device, put, lambda slot: ref.at[slot], *pair)
        next(steps)
        ends.append(steps)
        return steps

    steps = run(grid.x, x, here.along_x, lambda to: part.at[to], first, pairs[0])
    yield
    next(steps)
    second[group] = add_up(first, grid.x)
    mine = second.at[group]
    steps = run(grid.y * grid.c, group, here.along_yc, lambda to, mine=mine: mine, second, pairs[1])
    yield
    next(steps)
    third[z] = add_up(second, grid.y * grid.c)
    mine = third.at[z]
    steps = run(grid.z, z, here.along_z, lambda to, mine=mine: mine, third, pairs[2])
    yield
    next(steps)
    whole[x] = add_up(third, grid.z)
    mine = whole.at[x]
    steps = run(grid.x, x, here.along_x, lambda to, mine=mine: mine, whole, pairs[3])
    yield
    next(steps)
    row = lax.broadcasted_iota(jnp.int32, (low, k), 0)
    lane = lax.broadcasted_iota(jnp.int32, (low, k), 1)
    for p in range(grid.x):
        for h in range(2):
            at = p * rows + h * low
            unit = jnp.where(row + at == lane, 1.0, 0.0).astype(F32)
            value = whole[p][:, h * k : (h + 1) * k] * (1.0 / row_count)
            work[at : at + low, :] = jnp.concatenate([value, unit], axis=1)
    for steps in ends:
        next(steps)
    yield
    row = lax.broadcasted_iota(jnp.int32, (k, 2 * k), 0)
    lane = lax.broadcasted_iota(jnp.int32, (k, 2 * k), 1)

    def lane_sum(value, at):
        return jnp.sum(jnp.where(lane[: value.shape[0]] == at, value, 0.0), axis=1, keepdims=True)

    @pl.loop(0, k // 2)
    def _(i):
        at = 2 * i
        value = work[...]
        upper = work[pl.ds(at, 1), :]
        lower = work[pl.ds(at + 1, 1), :]
        inverse = 1.0 / lane_sum(upper, at)
        cross = lane_sum(upper, at + 1)
        left = lane_sum(value, at) * inverse
        lower = lower - (cross * inverse) * upper
        right = lane_sum(value, at + 1) - left * cross
        right = right * (1.0 / (lane_sum(lower, at + 1)))
        left = jnp.where(row[:, :1] > at, left, 0.0)
        right = jnp.where(row[:, :1] > at + 1, right, 0.0)
        work[...] = value - left * upper - right * lower

    value = work[...]
    diagonal = jnp.sum(jnp.where(lane == row, value, 0.0), axis=1, keepdims=True)
    work[...] = value * lax.rsqrt(diagonal)
    yield


def apply_inverse(work, value):
    k = work.shape[0]
    return jnp.dot(work[:, k:], value, precision=HIGHEST, preferred_element_type=F32)


def slots_of(grid, value):
    return value // (grid.z * grid.c), (value // grid.c) % grid.z, value % grid.c


def work_out_tables(here, tiles, notes, serves, column_table, item_table):
    grid = here.grid
    group = grid.c * grid.y
    n = group * tiles
    owners = grid.c * grid.z * grid.y
    side = notes.shape[2]

    @pl.loop(0, owners)
    def _(i):
        serves[pl.ds(i, 1), :] = notes[i][2:3].astype(F32)

    row = lax.broadcasted_iota(jnp.int32, (n, side), 0)
    lane = lax.broadcasted_iota(jnp.int32, (n, side), 1)
    tile, member = row % tiles, row // tiles
    asked = []
    for core in range(grid.c):
        for y in range(grid.y):
            line = notes[(core * grid.z + here.z) * grid.y + y][3:4].astype(F32)
            asked.append(jnp.broadcast_to(line, (tiles, side)))
    asked = jnp.concatenate(asked, axis=0)

    def column(value):
        return jnp.sum(value, axis=1, keepdims=True)

    slot = column(jnp.where(lane == tile, asked, 0.0)).astype(jnp.int32)
    sy, sz, sc = slots_of(grid, slot)
    where = (sc * grid.z + sz) * grid.y + sy
    hot = jnp.where(lane == where, 1.0, 0.0).astype(BF)[:, :owners]
    served = jnp.dot(hot, serves[...].astype(BF), preferred_element_type=F32)
    asker = ((member % grid.y) * grid.z + here.z) * grid.c + member // grid.y
    pick = column(jnp.where(lane == asker, served, 0.0)).astype(jnp.int32)
    line_at = (sc * grid.z + sz) * 2 + pick
    ask = jnp.where(sy == here.y, line_at, 0)
    ids = where * 2 + pick
    across = jnp.broadcast_to(ids.astype(F32), (n, side)).T.astype(jnp.int32)[:n]
    square_lane, square_row = lane[:, :n], row[:, :n]
    same = (across == ids) & (square_lane // tiles == square_row // tiles) & (square_lane < square_row)
    before = jnp.max(jnp.where(same, square_lane % tiles + 1, 0).astype(F32), axis=1, keepdims=True)
    columns = jnp.where(
        lane == 0, ask.astype(F32), jnp.where(lane == 1, pick.astype(F32), jnp.where(lane == 2, before, 0.0))
    )
    column_table[...] = columns.T[:8].astype(jnp.int32)
    mine = jnp.where((sy == here.y) & (sc == here.c), sz * 2 + pick, -1)
    number = jnp.where(mine == lane, tile + 1, 0).astype(F32)
    for g in range(group):
        last = jnp.max(number[g * tiles : (g + 1) * tiles], axis=0, keepdims=True)
        item_table[g : g + 1, :] = last.astype(jnp.int32) + g * (tiles + 1)


def within(at, ref):
    return jnp.minimum(jnp.maximum(at, 0), ref.shape[0] - 1)


def unpack_masks(observed, masks):
    side = masks.shape[1]

    @pl.loop(0, masks.shape[0])
    def _(t):
        words = observed[t]
        spread = jnp.broadcast_to(words[:, None, :], (words.shape[0], 8, side)).reshape(side, side)
        shift = lax.broadcasted_iota(jnp.int32, (side, side), 0) % 8
        masks[t] = ((spread >> shift) & 1).astype(F32).T.astype(BF)


def residual_tiles(tables, own, query, notes, users, ratings, masks, out, out_t):
    tiles = ratings.shape[0]

    @pl.loop(0, tiles, unroll=4)
    def _(t):
        meta = notes[tables["note_at"][t]].astype(F32)
        line = lax.broadcasted_iota(jnp.int32, meta.shape, 0)
        pick = tables["column"][1, own * tiles + t]
        weight = jnp.sum(jnp.where(line == pick, meta, 0.0), axis=0, keepdims=True)
        guess = lax.dot_general(
            users[tables["user_at"][t]],
            query[tables["query_at"][t]],
            (((0,), (0,)), ((), ())),
            preferred_element_type=F32,
        )
        value = masks[t].astype(F32) * weight * (ratings[t].astype(F32) - guess)
        out[t] = value.astype(BF)
        out_t[t] = value.T.astype(BF)


TABLES = ("user_at", "query_at", "note_at", "user_before", "user_last")


def main_kernel(grid, counts, names, *refs):
    refs = list(refs)
    tables = {name: refs.pop(0) for name in TABLES}
    facts, item_start, user_start, ratings, observed, user_out, item_out = (refs.pop(0) for _ in range(7))
    scratch = {name: refs.pop(0) for name in names}
    here = Here(grid)
    tiles, side = ratings.shape[:2]
    per = user_out.shape[1] // side
    rank = user_out.shape[0]
    x, y, z, c = here.x, here.y, here.z, here.c
    res, res_t, sums = scratch["res"], scratch["res_t"], scratch["sums"]
    near_rows = tiles + 1
    far = grid.z // 4

    def of(prefix, it):
        start = f"{prefix}{it}_"
        return [ref for name, ref in scratch.items() if name.startswith(start)]

    line, notes, users = scratch["line"], scratch["notes"], scratch["users"]
    ends = []

    for b in range(2):
        line[(c * grid.z + z) * 2 + b] = item_start[:, b * side : (b + 1) * side]
    for j in range(per):
        users[x * per + j] = user_start[:, j * side : (j + 1) * side]
    facts_f = facts[...].astype(F32)
    weight = (LEVELS + 1.0) / (facts_f + 1.0)
    facts_row = lax.broadcasted_iota(jnp.int32, facts.shape, 0)
    note_at = (c * grid.z + z) * grid.y + y
    first_rows = jnp.where(facts_row < 2, weight, facts_f)
    notes[note_at] = jnp.concatenate([first_rows, jnp.zeros_like(first_rows)], axis=0).astype(BF)
    here.greet()
    mine = notes.at[note_at]
    note_y = exchange(
        grid.y,
        y,
        here.along_y,
        lambda to: mine,
        lambda slot: notes.at[(c * grid.z + z) * grid.y + slot],
        *of("note", "y"),
    )
    items = spread_z(here, line, 2, *of("line", "z"))
    people = spread_x(here, users, per, *of("users", "x"))
    note_z = spread_z(here, notes, grid.y, *of("note", "z"))
    next(note_y)
    next(items)
    next(people)
    sums[0] = jnp.zeros_like(sums[0])
    for it in range(ITERS):
        near = scratch[f"near{it}"]
        for s in range(grid.c * grid.y):
            near[s * near_rows] = jnp.zeros(near.shape[1:], BF)
    next(note_y)
    next(note_z)
    unpack_masks(observed, scratch["masks"])
    next(note_z)
    next(items)
    next(note_z)
    next(note_z)
    work_out_tables(here, tiles, notes, scratch["serves"], scratch["column_v"], scratch["item_v"])
    copies = [
        pltpu.make_async_copy(scratch[f"{name}_v"], scratch[f"{name}_s"], scratch[f"{name}_sem"].at[0])
        for name in ("column", "item")
    ]
    for copy in copies:
        copy.start()
    next(items)
    for copy in copies:
        copy.wait()
    tables["column"] = scratch["column_s"]
    own = c * grid.y + y
    next(items)
    next(people)
    ends += [note_y, items, people, note_z]
    gram_item = None
    for it in range(ITERS):
        sel, query, stage_x, got_x, raw_u, new_users, near, stage, got, fars, got_far, raw_i = (
            scratch[f"{name}{it}"]
            for name in (
                "sel",
                "query",
                "stage_x",
                "got_x",
                "raw_u",
                "users",
                "near",
                "stage",
                "got",
                "fars",
                "got_far",
                "raw_i",
            )
        )
        for i in range(grid.y):
            to = (y + i) % grid.y

            @pl.loop(0, tiles)
            def _(t):
                at = tables["column"][0, (c * grid.y + to) * tiles + t]
                sel[to * tiles + t] = line[within(at, line)]

        asked = exchange(
            grid.y,
            y,
            here.along_y,
            lambda to: sel.at[pl.ds(to * tiles, tiles)],
            lambda slot: query.at[pl.ds(slot * tiles, tiles)],
            *of("ysel", it),
        )
        next(asked)
        query[pl.ds(y * tiles, tiles)] = sel[pl.ds(y * tiles, tiles)]
        if gram_item is not None:
            next(gram_item)
        next(asked)
        ends.append(asked)
        if it == 0:
            residual_tiles(tables, own, query, notes, users, ratings, scratch["masks"], res, res_t)

        @pl.loop(0, tiles, unroll=4)
        def _(t):
            product = jnp.dot(query[tables["query_at"][t]], res_t[t], preferred_element_type=F32)
            sums[t + 1] = product + sums[tables["user_before"][t]]

        for i in range(grid.x):
            to = (x + i) % grid.x

            @pl.loop(0, per)
            def _(j):
                total = sums[tables["user_last"][to * per + j]]
                if i:
                    stage_x[to * per + j] = total.astype(BF)
                else:
                    raw_u[j] = total

        parts = exchange(
            grid.x,
            x,
            here.along_x,
            lambda to: stage_x.at[pl.ds(to * per, per)],
            lambda slot: got_x.at[pl.ds(slot * per, per)],
            *of("xsum", it),
        )
        next(parts)
        if gram_item is not None:
            for _ in range(2):
                next(gram_item)
        next(parts)
        ends.append(parts)

        @pl.loop(0, per)
        def _(j):
            total = raw_u[j]
            for i in range(1, grid.x):
                total = total + got_x[((x + i) % grid.x) * per + j].astype(F32)
            if it:
                total = apply_inverse(scratch[f"gitem{it - 1}_work"], total)
            raw_u[j] = total
            new_users[x * per + j] = total.astype(BF)

        people = spread_x(here, new_users, per, *of("xall", it))
        next(people)
        gram_user = gram_steps(here, raw_u, per, counts[0], of("guser", it))
        next(gram_user)
        next(people)
        next(gram_user)
        ends.append(people)

        @pl.loop(0, tiles, unroll=4)
        def _(t):
            product = jnp.dot(new_users[tables["user_at"][t]], res[t], preferred_element_type=F32)
            total = product + sums[within(tables["column"][2, own * tiles + t], sums)]
            sums[t + 1] = total
            near[(c * grid.y + y) * near_rows + 1 + t] = total.astype(BF)

        def rows_of(core, slot):
            return near.at[pl.ds((core * grid.y + slot) * near_rows + 1, tiles)]

        along = exchange(
            grid.y, y, here.along_y, lambda to: rows_of(c, y), lambda slot: rows_of(c, slot), *of("ynear", it)
        )
        next(along)
        c_send, c_recv = of("cnear", it)

        def c_copy(core, slot):
            block = rows_of(core, slot)
            return remote(block, block, c_send.at[slot], c_recv.at[slot], here.other_core())

        c_copy(c, y).start()
        next(gram_user)
        next(along)
        ends.append(along)
        for i in range(1, grid.y):
            c_copy(c, (y + i) % grid.y).start()
        next(gram_user)
        for i in range(grid.y):
            c_copy(1 - c, (y + i) % grid.y).wait_recv()

        def gathered(zz, b):
            total = None
            for s in range(grid.c * grid.y):
                at = scratch["item_s"][s, zz * 2 + b]
                value = near[within(at, near)].astype(F32)
                total = value if total is None else total + value
            return total

        z_send, z_recv = of("znear", it)
        ways = [(1, (0, 1)), (-1, (0, 1)), (-2, (0,)), (2, (1,))]
        starts = [0, 2 * far, 4 * far, 5 * far]

        def near_z(way, arrival=False):
            by, parts_ = ways[way]
            count = len(parts_) * far
            to = here.along_z(here.z_off(-by if arrival else by))
            return remote(
                stage.at[pl.ds(starts[way], count)],
                got.at[pl.ds(starts[way], count)],
                z_send.at[way],
                z_recv.at[way],
                to,
            )

        for way, (by, parts_) in enumerate(ways):

            @pl.loop(0, far)
            def _(k):
                for j, b in enumerate(parts_):
                    zz = here.z_off(by + 4 * k)
                    stage[starts[way] + len(parts_) * k + j] = gathered(zz, b).astype(BF)

            near_z(way).start()
        for k in range(far):
            for b in range(2):
                fars[2 * k + b] = gathered(here.z_off(4 * k), b)
        next(gram_user)
        for way in range(4):
            near_z(way, True).wait_recv()
        f_send, f_recv = of("zfar", it)
        far_stage = scratch[f"far_stage{it}"]

        def far_copy(k):
            return remote(
                far_stage.at[pl.ds(2 * k, 2)],
                got_far.at[pl.ds(2 * k, 2)],
                f_send.at[k],
                f_recv.at[k],
                here.along_z(here.z_off(4 * k)),
            )

        for k in list(range(1, far)) + [0]:
            for b in range(2):
                total = (
                    fars[2 * k + b]
                    + got[starts[0] + 2 * k + b].astype(F32)
                    + got[starts[1] + 2 * k + b].astype(F32)
                    + got[starts[2 + b] + k].astype(F32)
                )
                if k:
                    far_stage[2 * k + b] = total.astype(BF)
                else:
                    raw_i[b] = total
            if k:
                far_copy(k).start()
        next(gram_user)
        for k in range(1, far):
            far_copy(k).wait_recv()
        for b in range(2):
            total = raw_i[b]
            for k in range(1, far):
                total = total + got_far[2 * k + b].astype(F32)
            raw_i[b] = apply_inverse(scratch[f"guser{it}_work"], total)
        gram_item = gram_steps(here, raw_i, 2, counts[1], of("gitem", it))
        if it + 1 < ITERS:
            line = scratch["next_line"]
            for b in range(2):
                line[(c * grid.z + z) * 2 + b] = raw_i[b].astype(BF)
            items = spread_z(here, line, 2, *of("zall", it))
            next(items)
            next(gram_item)
            next(items)
            next(gram_item)
            next(items)
            next(gram_item)
            next(items)
            ends.append(items)
        else:
            next(gram_item)
            for j in range(per):
                user_out[:, j * side : (j + 1) * side] = apply_inverse(
                    scratch[f"guser{it}_work"], raw_u[j]
                ).astype(BF)
            for _ in range(5):
                next(gram_item)
            for b in range(2):
                item_out[:, b * side : (b + 1) * side] = apply_inverse(
                    scratch[f"gitem{it}_work"], raw_i[b]
                ).astype(BF)
        for i in range(grid.y):
            c_copy(c, (y + i) % grid.y).wait_send()
        for way in range(4):
            near_z(way).wait_send()
        for k in range(1, far):
            far_copy(k).wait_send()
    for steps in ends:
        next(steps)


def main_scratch(grid, rank, side, tiles, per):
    far = grid.z // 4
    block = (rank, side)

    def vmem(n, kind=BF):
        return pltpu.VMEM((n,) + block, kind)

    out = {
        "res": pltpu.VMEM((tiles, side, side), BF),
        "res_t": pltpu.VMEM((tiles, side, side), BF),
        "sums": vmem(tiles + 1, F32),
        "line": vmem(2 * grid.z * 2),
        "next_line": vmem(2 * grid.z * 2),
        "users": vmem(grid.x * per),
        "notes": pltpu.VMEM((2 * grid.z * grid.y, 16, side), BF),
        "masks": pltpu.VMEM((tiles, side, side), BF),
        "serves": pltpu.VMEM((2 * grid.z * grid.y, side), F32),
        "column_v": pltpu.VMEM((8, grid.c * grid.y * tiles), jnp.int32),
        "column_s": pltpu.SMEM((8, grid.c * grid.y * tiles), jnp.int32),
        "column_sem": sems(1),
        "item_v": pltpu.VMEM((grid.c * grid.y, side), jnp.int32),
        "item_s": pltpu.SMEM((grid.c * grid.y, side), jnp.int32),
        "item_sem": sems(1),
        "notey_send": sems(grid.y),
        "notey_recv": sems(grid.y),
        "usersx_send": sems(grid.x),
        "usersx_recv": sems(grid.x),
    }
    for prefix in ("linez", "notez"):
        for i, shape in enumerate(spread_z_sems(grid)):
            out[f"{prefix}_{i}"] = shape
    for it in range(ITERS):
        out[f"sel{it}"] = vmem(grid.y * tiles)
        out[f"query{it}"] = vmem(grid.y * tiles)
        out[f"stage_x{it}"] = vmem(grid.x * per)
        out[f"got_x{it}"] = vmem(grid.x * per)
        out[f"raw_u{it}"] = vmem(per, F32)
        out[f"users{it}"] = vmem(grid.x * per)
        out[f"near{it}"] = vmem(grid.c * grid.y * (tiles + 1))
        out[f"stage{it}"] = vmem(6 * far)
        out[f"got{it}"] = vmem(6 * far)
        out[f"fars{it}"] = vmem(2 * far, F32)
        out[f"far_stage{it}"] = vmem(2 * far)
        out[f"got_far{it}"] = vmem(2 * far)
        out[f"raw_i{it}"] = vmem(2, F32)
        for name, n in (
            ("ysel", grid.y),
            ("xsum", grid.x),
            ("xall", grid.x),
            ("ynear", grid.y),
            ("cnear", grid.y),
            ("znear", 4),
            ("zfar", far),
        ):
            out[f"{name}{it}_send"] = sems(n)
            out[f"{name}{it}_recv"] = sems(n)
        for i, shape in enumerate(spread_z_sems(grid)):
            out[f"zall{it}_{i}"] = shape
        for name in ("guser", "gitem"):
            shapes = gram_scratch(grid, rank)
            for i, shape in enumerate(shapes):
                out[f"{name}{it}_" + ("work" if i + 1 == len(shapes) else str(i))] = shape
    return out


def main_call(grid, counts, tables, facts, item_start, user_start, ratings, observed):
    tiles, side = ratings.shape[:2]
    rank = item_start.shape[0]
    per = user_start.shape[1] // side
    scratch = main_scratch(grid, rank, side, tiles, per)
    return pl.pallas_call(
        functools.partial(main_kernel, grid, counts, tuple(scratch)),
        out_shape=(
            jax.ShapeDtypeStruct((rank, per * side), BF),
            jax.ShapeDtypeStruct((rank, 2 * side), BF),
        ),
        in_specs=[pl.BlockSpec(memory_space=pltpu.SMEM)] * len(TABLES)
        + [pl.BlockSpec(memory_space=pltpu.VMEM)] * 5,
        out_specs=(pl.BlockSpec(memory_space=pltpu.VMEM),) * 2,
        scratch_shapes=list(scratch.values()),
        compiler_params=pltpu.CompilerParams(
            collective_id=1, has_side_effects=True, vmem_limit_bytes=VMEM_LIMIT
        ),
    )(*(tables[name] for name in TABLES), facts, item_start, user_start, ratings, observed)


def links(ids):
    at = jnp.arange(ids.shape[0], dtype=jnp.int32)
    same = (ids[:, None] == ids[None, :]) & (at[None, :] < at[:, None])
    return jnp.max(jnp.where(same, at[None, :] + 1, 0), axis=1)


def lasts(ids, n):
    tiles = ids.shape[-1]
    same = ids[..., None, :] == jnp.arange(n, dtype=jnp.int32)[:, None]
    return jnp.max(jnp.where(same, jnp.arange(1, tiles + 1, dtype=jnp.int32), 0), axis=-1)


def local(grid, ratings, observed, user_start, item_start, exposure, serve_list, tile_slot, tile_user):
    side = ratings.shape[2]
    own_users = user_start.shape[1]
    tiles = ratings.shape[0]
    owners = grid.y * grid.z * grid.c
    counts = (own_users * owners * grid.x * 1.0, item_start.shape[1] * owners * grid.x * 1.0)
    per = own_users // side
    sy, sz, sc = slots_of(grid, tile_slot)
    tables = {
        "user_at": tile_user,
        "query_at": sy * tiles + jnp.arange(tiles, dtype=jnp.int32),
        "note_at": (sc * grid.z + sz) * grid.y + sy,
        "user_before": links(tile_user),
        "user_last": lasts(tile_user, grid.x * per),
    }
    rows = [exposure, jnp.pad(serve_list, (0, side - owners)), jnp.pad(tile_slot, (0, side - tiles))]
    facts = jnp.concatenate(rows + [jnp.zeros((4 * side,), jnp.int32)]).reshape(8, side)
    return main_call(grid, counts, tables, facts, item_start, user_start, ratings, observed)


def solution(mesh):
    grid = Grid(mesh.shape["rows"], mesh.shape["rep"])
    both = P(("rows", "rep"))
    second = P(None, ("rows", "rep"))
    return jax.shard_map(
        functools.partial(local, grid),
        mesh=mesh,
        in_specs=(both, both, second, second, both, both, both, both),
        out_specs=(second, second),
        check_vma=False,
    )
```

```python
import functools

import jax
import jax.numpy as jnp
from jax import lax
from jax.experimental import pallas as pl
from jax.experimental.pallas import tpu as pltpu
from jax.sharding import PartitionSpec as P

LEVELS = 16
ITERS = 2
MESH = pl.DeviceIdType.MESH
BF = jnp.bfloat16
F32 = jnp.float32
HIGHEST = lax.Precision.HIGHEST
VMEM_LIMIT = 48 * 1024 * 1024


class Grid:
    def __init__(self, rows, rep):
        self.c = 2
        self.x = rep
        self.y = 4
        self.z = rows // (self.c * self.y)


class Names:
    def __init__(self, **named):
        self.__dict__.update(named)


def named(tree):
    if isinstance(tree, dict):
        return Names(**{key: named(value) for key, value in tree.items()})
    return [named(value) for value in tree] if isinstance(tree, (list, tuple)) else tree


class Here:
    def __init__(self, grid):
        r = lax.axis_index("rows")
        self.grid = grid
        self.r = r
        self.x = lax.axis_index("rep")
        self.y = r // (grid.z * grid.c)
        self.z = (r // grid.c) % grid.z
        self.c = r % grid.c

    def along_x(self, to):
        return self.r, to

    def along_y(self, to):
        return (to * self.grid.z + self.z) * self.grid.c + self.c, self.x

    def along_z(self, to):
        return (self.y * self.grid.z + to) * self.grid.c + self.c, self.x

    def along_yc(self, to):
        y, c = to // self.grid.c, to % self.grid.c
        return (y * self.grid.z + self.z) * self.grid.c + c, self.x

    def other_core(self):
        return (self.y * self.grid.z + self.z) * self.grid.c + 1 - self.c, self.x

    def z_off(self, by):
        return (self.z + by + 2 * self.grid.z) % self.grid.z

    def greet(self):
        grid = self.grid
        targets = [self.along_x((self.x + i) % grid.x) for i in range(1, grid.x)]
        for i in range(grid.y):
            for j in range(grid.c):
                if i or j:
                    to = ((self.y + i) % grid.y) * grid.c + (self.c + j) % 2
                    targets.append(self.along_yc(to))
        targets += [self.along_z(self.z_off(o)) for o in range(1, grid.z)]
        barrier = pltpu.get_barrier_semaphore()
        for target in targets:
            pl.semaphore_signal(barrier, inc=1, device_id=target, device_id_type=MESH)
        yield
        pl.semaphore_wait(barrier, len(targets))
        yield


def remote(src, dst, send_sem, recv_sem, device):
    return pltpu.make_async_remote_copy(
        src_ref=src,
        dst_ref=dst,
        send_sem=send_sem,
        recv_sem=recv_sem,
        device_id=device,
        device_id_type=MESH,
    )


def sems(*shape):
    return pltpu.SemaphoreType.DMA(shape)


def spread_x(here, buf, per, send, recv):
    n = here.grid.x

    def copy(to, slot):
        block = buf.at[pl.ds(slot * per, per)]
        return remote(block, block, send.at[to], recv.at[slot], here.along_x(to))

    for i in range(1, n):
        copy((here.x + i) % n, here.x).start()
    yield
    for i in range(1, n):
        copy((here.x + i) % n, (here.x + i) % n).wait_recv()
    yield
    for i in range(1, n):
        copy((here.x + i) % n, here.x).wait_send()
    yield


def spread_z_sems(grid):
    far = grid.z // 4
    return [sems(far), sems(far), sems(far, 4), sems(far, 4), sems(1), sems(1)]


def spread_z(here, buf, n, far_send, far_recv, near_send, near_recv, c_send, c_recv):
    grid = here.grid
    half = n // 2
    far = grid.z // 4

    def chunk(core, zz, start=0, count=n):
        return buf.at[pl.ds((core * grid.z + zz) * n + start, count)]

    def far_copy(k):
        block = chunk(here.c, here.z)
        return remote(block, block, far_send.at[k], far_recv.at[k], here.along_z(here.z_off(4 * k)))

    def far_arrival(k):
        block = chunk(here.c, here.z_off(-4 * k))
        return remote(block, block, far_send.at[k], far_recv.at[k], here.along_z(here.z_off(-4 * k)))

    ways = [(1, 0, n), (-1, 0, n), (-2, 0, half), (2, half, half)]

    def near_copy(k, way):
        by, start, count = ways[way]
        block = chunk(here.c, here.z_off(-4 * k), start, count)
        return remote(
            block, block, near_send.at[k, way], near_recv.at[k, way], here.along_z(here.z_off(by))
        )

    def near_arrival(k, way):
        by, start, count = ways[way]
        block = chunk(here.c, here.z_off(-by - 4 * k), start, count)
        return remote(
            block, block, near_send.at[k, way], near_recv.at[k, way], here.along_z(here.z_off(-by))
        )

    for k in range(1, far):
        far_copy(k).start()
    for way in range(4):
        near_copy(0, way).start()
    yield
    for k in range(1, far):
        far_arrival(k).wait_recv()
        for way in range(4):
            near_copy(k, way).start()
    yield
    for k in range(far):
        for way in range(4):
            near_arrival(k, way).wait_recv()
    line = buf.at[pl.ds(here.c * grid.z * n, grid.z * n)]
    swap = remote(line, line, c_send.at[0], c_recv.at[0], here.other_core())
    swap.start()
    yield
    line = buf.at[pl.ds((1 - here.c) * grid.z * n, grid.z * n)]
    remote(line, line, c_send.at[0], c_recv.at[0], here.other_core()).wait_recv()
    yield
    swap.wait_send()
    for k in range(far):
        if k:
            far_copy(k).wait_send()
        for way in range(4):
            near_copy(k, way).wait_send()
    yield


def exchange(n, me, device, put, take, send, recv):
    def copy(to):
        return remote(put(to), take(me), send.at[to], recv.at[me], device(to))

    def arrival(slot):
        return remote(put(slot), take(slot), send.at[slot], recv.at[slot], device(slot))

    for i in range(1, n):
        copy((me + i) % n).start()
    yield
    for i in range(1, n):
        arrival((me + i) % n).wait_recv()
    yield
    for i in range(1, n):
        copy((me + i) % n).wait_send()
    yield


def add_up(ref, n):
    total = ref[0]
    for i in range(1, n):
        total = total + ref[i]
    return total


def gram_scratch(grid, rank):
    shape = (rank // grid.x // 2, 2 * rank)
    counts = [grid.x, grid.y * grid.c, grid.z, grid.x]
    buffers = [pltpu.VMEM((n,) + shape, F32) for n in [grid.x] + counts]
    return buffers + [sems(n) for n in counts for _ in range(2)] + [pltpu.VMEM((rank, 2 * rank), F32)]


def gram_steps(here, block, blocks, row_count, scratch):
    grid = here.grid
    part, first, second, third, whole = scratch[:5]
    pairs = [scratch[5 + 2 * i : 7 + 2 * i] for i in range(4)]
    work = scratch[-1]
    total = None
    for i in range(blocks):
        value = block(i)
        one = lax.dot_general(
            value, value, (((1,), (1,)), ((), ())), precision=HIGHEST, preferred_element_type=F32
        )
        total = one if total is None else total + one
    k = total.shape[0]
    rows = k // grid.x
    low = rows // 2
    for p in range(grid.x):
        part[p] = jnp.concatenate(
            [total[p * rows : p * rows + low], total[p * rows + low : (p + 1) * rows]], axis=1
        )
    x, z = here.x, here.z
    group = here.y * grid.c + here.c
    first[x] = part[x]
    ends = []

    def run(n, me, device, put, ref, pair):
        steps = exchange(n, me, device, put, lambda slot: ref.at[slot], *pair)
        next(steps)
        ends.append(steps)
        return steps

    steps = run(grid.x, x, here.along_x, lambda to: part.at[to], first, pairs[0])
    yield
    next(steps)
    second[group] = add_up(first, grid.x)
    mine = second.at[group]
    steps = run(grid.y * grid.c, group, here.along_yc, lambda to, mine=mine: mine, second, pairs[1])
    yield
    next(steps)
    third[z] = add_up(second, grid.y * grid.c)
    mine = third.at[z]
    steps = run(grid.z, z, here.along_z, lambda to, mine=mine: mine, third, pairs[2])
    yield
    next(steps)
    whole[x] = add_up(third, grid.z)
    mine = whole.at[x]
    steps = run(grid.x, x, here.along_x, lambda to, mine=mine: mine, whole, pairs[3])
    yield
    next(steps)
    row = lax.broadcasted_iota(jnp.int32, (low, k), 0)
    lane = lax.broadcasted_iota(jnp.int32, (low, k), 1)
    for p in range(grid.x):
        for h in range(2):
            at = p * rows + h * low
            unit = jnp.where(row + at == lane, 1.0, 0.0).astype(F32)
            value = whole[p][:, h * k : (h + 1) * k] * (1.0 / row_count)
            work[at : at + low, :] = jnp.concatenate([value, unit], axis=1)
    for steps in ends:
        next(steps)
    yield
    row = lax.broadcasted_iota(jnp.int32, (k, 2 * k), 0)
    lane = lax.broadcasted_iota(jnp.int32, (k, 2 * k), 1)

    eliminate(work)
    value = work[...]
    diagonal = jnp.sum(jnp.where(lane == row, value, 0.0), axis=1, keepdims=True)
    work[...] = value * lax.rsqrt(diagonal)
    yield


def eliminate(work, width=4):
    k = work.shape[0]
    row = lax.broadcasted_iota(jnp.int32, (k, 1), 0)
    lane = lax.broadcasted_iota(jnp.int32, work.shape, 1)

    def lane_sum(value, at):
        return jnp.sum(jnp.where(lane[: value.shape[0]] == at, value, 0.0), axis=1, keepdims=True)

    @pl.loop(0, k // width)
    def _(i):
        at = i * width
        value = work[...]
        rows = [work[pl.ds(at + a, 1), :] for a in range(width)]
        columns = [lane_sum(value, at + a) for a in range(width)]
        block = [[lane_sum(rows[a], at + b) for b in range(width)] for a in range(width)]
        for a in range(width):
            inverse = 1.0 / block[a][a]
            left = columns[a] * inverse
            for b in range(a + 1, width):
                factor = block[a][b] * inverse
                rows[b] = rows[b] - factor * rows[a]
                columns[b] = columns[b] - left * block[a][b]
                for d in range(b, width):
                    block[b][d] = block[b][d] - factor * block[a][d]
            value = value - jnp.where(row > at + a, left, 0.0) * rows[a]
        work[...] = value


def apply_inverse(work, value, first=0):
    k = work.shape[0]
    rows = work[first:, k:] if first else work[: value.shape[0], k : k + value.shape[0]]
    return jnp.dot(rows, value, precision=HIGHEST, preferred_element_type=F32)


def slots_of(grid, value):
    return value // (grid.z * grid.c), (value // grid.c) % grid.z, value % grid.c


def work_out_tables(here, tiles, notes, serves, column_table, item_table):
    grid = here.grid
    group = grid.c * grid.y
    n = group * tiles
    owners = grid.c * grid.z * grid.y
    side = notes.shape[2]

    @pl.loop(0, owners)
    def _(i):
        serves[pl.ds(i, 1), :] = notes[i][2:3].astype(F32)

    row = lax.broadcasted_iota(jnp.int32, (n, side), 0)
    lane = lax.broadcasted_iota(jnp.int32, (n, side), 1)
    tile, member = row % tiles, row // tiles
    asked = []
    for core in range(grid.c):
        for y in range(grid.y):
            line = notes[(core * grid.z + here.z) * grid.y + y][3:4].astype(F32)
            asked.append(jnp.broadcast_to(line, (tiles, side)))
    asked = jnp.concatenate(asked, axis=0)

    def column(value):
        return jnp.sum(value, axis=1, keepdims=True)

    slot = column(jnp.where(lane == tile, asked, 0.0)).astype(jnp.int32)
    sy, sz, sc = slots_of(grid, slot)
    where = (sc * grid.z + sz) * grid.y + sy
    hot = jnp.where(lane == where, 1.0, 0.0).astype(BF)[:, :owners]
    served = jnp.dot(hot, serves[...].astype(BF), preferred_element_type=F32)
    asker = ((member % grid.y) * grid.z + here.z) * grid.c + member // grid.y
    pick = column(jnp.where(lane == asker, served, 0.0)).astype(jnp.int32)
    line_at = (sc * grid.z + sz) * 2 + pick
    ask = jnp.where(sy == here.y, line_at, 0)
    ids = where * 2 + pick
    across = jnp.broadcast_to(ids.astype(F32), (n, side)).T.astype(jnp.int32)[:n]
    square_lane, square_row = lane[:, :n], row[:, :n]
    same = (across == ids) & (square_lane // tiles == square_row // tiles) & (square_lane < square_row)
    before = jnp.max(jnp.where(same, square_lane % tiles + 1, 0).astype(F32), axis=1, keepdims=True)
    columns = jnp.where(
        lane == 0, ask.astype(F32), jnp.where(lane == 1, pick.astype(F32), jnp.where(lane == 2, before, 0.0))
    )
    column_table[...] = columns.T[:8].astype(jnp.int32)
    mine = jnp.where((sy == here.y) & (sc == here.c), sz * 2 + pick, -1)
    number = jnp.where(mine == lane, tile + 1, 0).astype(F32)
    for g in range(group):
        last = jnp.max(number[g * tiles : (g + 1) * tiles], axis=0, keepdims=True)
        item_table[g : g + 1, :] = last.astype(jnp.int32) + g * (tiles + 1)


def within(at, ref):
    return jnp.minimum(jnp.maximum(at, 0), ref.shape[0] - 1)


def unpack_masks(observed, masks):
    side = masks.shape[1]

    @pl.loop(0, masks.shape[0])
    def _(t):
        words = observed[t]
        spread = jnp.broadcast_to(words[:, None, :], (words.shape[0], 8, side)).reshape(side, side)
        shift = lax.broadcasted_iota(jnp.int32, (side, side), 0) % 8
        masks[t] = ((spread >> shift) & 1).astype(F32).T.astype(BF)


def residual_tiles(tables, own, query, notes, users, ratings, masks, out, out_t):
    tiles = ratings.shape[0]

    @pl.loop(0, tiles, unroll=4)
    def _(t):
        meta = notes[tables.note_at[t]].astype(F32)
        line = lax.broadcasted_iota(jnp.int32, meta.shape, 0)
        pick = tables.column[1, own * tiles + t]
        weight = jnp.sum(jnp.where(line == pick, meta, 0.0), axis=0, keepdims=True)
        items = jnp.concatenate([part[tables.query_at[t]] for part in query], axis=0)
        guess = lax.dot_general(
            users[tables.user_at[t]], items, (((0,), (0,)), ((), ())), preferred_element_type=F32
        )
        value = masks[t].astype(F32) * weight * (ratings[t].astype(F32) - guess)
        out[t] = value.astype(BF)
        out_t[t] = value.T.astype(BF)


def main_kernel(grid, counts, tree, *refs):
    refs = list(refs)
    tables = Names()
    tables.user_at, tables.query_at, tables.note_at, tables.user_before, tables.user_last = (
        refs.pop(0) for _ in range(5)
    )
    facts, item_start, user_start, ratings_far, observed_far, user_out, item_out = (refs.pop(0) for _ in range(7))
    scratch = named(jax.tree.unflatten(tree, refs))
    here = Here(grid)
    ratings, observed = scratch.ratings, scratch.observed
    loads = [
        pltpu.make_async_copy(observed_far, observed, scratch.load_sem.at[0]),
        pltpu.make_async_copy(ratings_far, ratings, scratch.load_sem.at[1]),
    ]
    for load in loads:
        load.start()
    tiles, side = ratings.shape[:2]
    per = user_out.shape[1] // side
    rank = user_out.shape[0]
    x, y, z, c = here.x, here.y, here.z, here.c
    half = rank // 2
    res, res_t = scratch.res, scratch.res_t
    near_rows = tiles + 1
    far = grid.z // 4

    line, notes, users = scratch.line, scratch.notes, scratch.users
    ends = []
    greeting = here.greet()
    next(greeting)

    for b in range(2):
        line[(c * grid.z + z) * 2 + b] = item_start[:, b * side : (b + 1) * side]
    for j in range(per):
        users[x * per + j] = user_start[:, j * side : (j + 1) * side]
    facts_f = facts[...].astype(F32)
    weight = (LEVELS + 1.0) / (facts_f + 1.0)
    facts_row = lax.broadcasted_iota(jnp.int32, facts.shape, 0)
    note_at = (c * grid.z + z) * grid.y + y
    first_rows = jnp.where(facts_row < 2, weight, facts_f)
    notes[note_at] = jnp.concatenate([first_rows, jnp.zeros_like(first_rows)], axis=0).astype(BF)
    for h in range(2):
        scratch.sums[h][0] = jnp.zeros((half, side), F32)
        for it in range(ITERS):
            near = scratch.half[it][h].near
            for s in range(grid.c * grid.y):
                near[s * near_rows] = jnp.zeros((half, side), BF)
    for load in loads:
        load.wait()
    unpack_masks(observed, scratch.masks)
    next(greeting)
    mine = notes.at[note_at]
    note_y = exchange(
        grid.y,
        y,
        here.along_y,
        lambda to: mine,
        lambda slot: notes.at[(c * grid.z + z) * grid.y + slot],
        *scratch.note_y,
    )
    items = spread_z(here, line, 2, *scratch.line_z)
    people = spread_x(here, users, per, *scratch.users_x)
    note_z = spread_z(here, notes, grid.y, *scratch.note_z)
    next(note_y)
    next(items)
    next(people)
    next(note_y)
    next(note_z)
    next(note_z)
    next(items)
    next(note_z)
    next(items)
    next(note_z)
    work_out_tables(here, tiles, notes, scratch.serves, scratch.column_v, scratch.item_v)
    copies = [
        pltpu.make_async_copy(scratch.column_v, scratch.column_s, scratch.table_sem.at[0]),
        pltpu.make_async_copy(scratch.item_v, scratch.item_s, scratch.table_sem.at[1]),
    ]
    for copy in copies:
        copy.start()
    for copy in copies:
        copy.wait()
    tables.column = scratch.column_s
    own = c * grid.y + y
    next(items)
    next(people)
    ends += [note_y, items, people, note_z]

    def chain(h):
        rows = slice(h * half, (h + 1) * half)
        sums = scratch.sums[h]
        for it in range(ITERS):
            mine, low = scratch.half[it][h], scratch.half[it][0]
            sel, query, stage_x, got_x, pre_u, raw_u = (
                mine.sel,
                mine.query,
                mine.stage_x,
                mine.got_x,
                mine.pre_u,
                mine.raw_u,
            )
            new_users, near, stage, got, fars, got_far, pre_i, raw_i = (
                mine.users,
                mine.near,
                mine.stage,
                mine.got,
                mine.fars,
                mine.got_far,
                mine.pre_i,
                mine.raw_i,
            )
            for i in range(grid.y):
                to = (y + i) % grid.y

                @pl.loop(0, tiles, unroll=4)
                def _(t):
                    at = tables.column[0, (c * grid.y + to) * tiles + t]
                    if it:
                        block = scratch.lines[h][within(at, line)]
                    else:
                        block = line[within(at, line)][rows]
                    sel[to * tiles + t] = block

            asked = exchange(
                grid.y,
                y,
                here.along_y,
                lambda to, sel=sel: sel.at[pl.ds(to * tiles, tiles)],
                lambda slot, query=query: query.at[pl.ds(slot * tiles, tiles)],
                *mine.ysel,
            )
            next(asked)
            query[pl.ds(y * tiles, tiles)] = sel[pl.ds(y * tiles, tiles)]
            yield
            next(asked)
            ends.append(asked)
            if it == 0:
                yield

            @pl.loop(0, tiles, unroll=4)
            def _(t):
                product = jnp.dot(query[tables.query_at[t]], res_t[t], preferred_element_type=F32)
                sums[t + 1] = product + sums[tables.user_before[t]]

            for i in range(1, grid.x + 1):
                to = (x + i) % grid.x

                @pl.loop(0, per, unroll=4)
                def _(j):
                    total = sums[tables.user_last[to * per + j]]
                    if i < grid.x:
                        stage_x[to * per + j] = total.astype(BF)
                    else:
                        pre_u[j] = total

            parts = exchange(
                grid.x,
                x,
                here.along_x,
                lambda to, stage_x=stage_x: stage_x.at[pl.ds(to * per, per)],
                lambda slot, got_x=got_x: got_x.at[pl.ds(slot * per, per)],
                *mine.xsum,
            )
            next(parts)
            yield
            next(parts)
            ends.append(parts)

            @pl.loop(0, per, unroll=4)
            def _(j):
                total = pre_u[j]
                for i in range(1, grid.x):
                    total = total + got_x[((x + i) % grid.x) * per + j].astype(F32)
                if it:
                    pre_u[j] = total
                    work = scratch.gram_item[it - 1][-1]
                    if h:
                        total = apply_inverse(
                            work, jnp.concatenate([low.pre_u[j], total], axis=0), half
                        )
                    else:
                        total = apply_inverse(work, total)
                raw_u[j] = total
                new_users[x * per + j] = total.astype(BF)

            people = spread_x(here, new_users, per, *mine.xall)
            next(people)
            yield
            next(people)
            ends.append(people)

            @pl.loop(0, tiles, unroll=4)
            def _(t):
                product = jnp.dot(new_users[tables.user_at[t]], res[t], preferred_element_type=F32)
                total = product + sums[within(tables.column[2, own * tiles + t], sums)]
                sums[t + 1] = total
                near[own * near_rows + 1 + t] = total.astype(BF)

            def rows_of(core, slot, near=near):
                return near.at[pl.ds((core * grid.y + slot) * near_rows + 1, tiles)]

            along = exchange(
                grid.y, y, here.along_y, lambda to, f=rows_of: f(c, y), lambda slot, f=rows_of: f(c, slot), *mine.ynear
            )
            next(along)
            c_send, c_recv = mine.cnear

            def c_copy(core, slot):
                block = rows_of(core, slot)
                return remote(block, block, c_send.at[slot], c_recv.at[slot], here.other_core())

            c_copy(c, y).start()
            yield
            next(along)
            ends.append(along)
            for i in range(1, grid.y):
                c_copy(c, (y + i) % grid.y).start()
            yield
            for i in range(grid.y):
                c_copy(1 - c, (y + i) % grid.y).wait_recv()

            def gathered(zz, b):
                total = None
                for s in range(grid.c * grid.y):
                    at = scratch.item_s[s, zz * 2 + b]
                    value = near[within(at, near)].astype(F32)
                    total = value if total is None else total + value
                return total

            z_send, z_recv = mine.znear
            ways = [(1, (0, 1)), (-1, (0, 1)), (-2, (0,)), (2, (1,))]
            starts = [0, 2 * far, 4 * far, 5 * far]

            def near_z(way, arrival=False):
                by, parts_ = ways[way]
                count = len(parts_) * far
                to = here.along_z(here.z_off(-by if arrival else by))
                return remote(
                    stage.at[pl.ds(starts[way], count)],
                    got.at[pl.ds(starts[way], count)],
                    z_send.at[way],
                    z_recv.at[way],
                    to,
                )

            for way in (3, 2, 1, 0):
                by, parts_ = ways[way]

                @pl.loop(0, far)
                def _(k):
                    for j, b in enumerate(parts_):
                        zz = here.z_off(by + 4 * k)
                        stage[starts[way] + len(parts_) * k + j] = gathered(zz, b).astype(BF)

                near_z(way).start()

            @pl.loop(0, far)
            def _(k):
                for b in range(2):
                    fars[2 * k + b] = gathered(here.z_off(4 * k), b)

            yield
            for way in range(4):
                near_z(way, True).wait_recv()
            f_send, f_recv = mine.zfar
            far_stage = mine.far_stage

            def far_copy(k):
                return remote(
                    far_stage.at[pl.ds(2 * k, 2)],
                    got_far.at[pl.ds(2 * k, 2)],
                    f_send.at[k],
                    f_recv.at[k],
                    here.along_z(here.z_off(4 * k)),
                )

            for k in list(range(1, far)) + [0]:
                for b in range(2):
                    total = (
                        fars[2 * k + b]
                        + got[starts[0] + 2 * k + b].astype(F32)
                        + got[starts[1] + 2 * k + b].astype(F32)
                        + got[starts[2 + b] + k].astype(F32)
                    )
                    if k:
                        far_stage[2 * k + b] = total.astype(BF)
                    else:
                        pre_i[b] = total
                if k:
                    far_copy(k).start()
            yield
            for k in range(1, far):
                far_copy(k).wait_recv()
            work = scratch.gram_user[it][-1]
            for b in range(2):
                total = pre_i[b]
                for k in range(1, far):
                    total = total + got_far[2 * k + b].astype(F32)
                pre_i[b] = total
                if h:
                    raw_i[b] = apply_inverse(
                        work, jnp.concatenate([low.pre_i[b], total], axis=0), half
                    )
                else:
                    raw_i[b] = apply_inverse(work, total)
            if it + 1 < ITERS:
                next_line = scratch.lines[h]
                for b in range(2):
                    next_line[(c * grid.z + z) * 2 + b] = raw_i[b].astype(BF)
                items = spread_z(here, next_line, 2, *mine.zall)
                ends.append(items)
                for _ in range(3):
                    next(items)
                    yield
                next(items)
            for i in range(grid.y):
                c_copy(c, (y + i) % grid.y).wait_send()
            for way in range(4):
                near_z(way).wait_send()
            for k in range(1, far):
                far_copy(k).wait_send()
        yield

    def whole_of(low, high):
        return lambda i: jnp.concatenate([low[i], high[i]], axis=0)

    chains = [chain(0), chain(1)]

    def step():
        for one in chains:
            next(one)

    gram_item = None
    for it in range(ITERS):
        if it == 0:
            step()
            step()
            query = [one.query for one in scratch.half[0]]
            residual_tiles(tables, own, query, notes, users, ratings, scratch.masks, res, res_t)
            step()
        else:
            step()
            next(gram_item)
            step()
            next(gram_item)
            next(gram_item)
        step()
        gram_user = gram_steps(here, whole_of(*(one.raw_u for one in scratch.half[it])), per, counts[0], scratch.gram_user[it])
        next(gram_user)
        step()
        next(gram_user)
        step()
        next(gram_user)
        step()
        next(gram_user)
        step()
        next(gram_user)
        next(gram_user)
        step()
        gram_item = gram_steps(here, whole_of(*(one.raw_i for one in scratch.half[it])), 2, counts[1], scratch.gram_item[it])
        next(gram_item)
        if it + 1 < ITERS:
            step()
            next(gram_item)
            step()
            next(gram_item)
    users_of = whole_of(*(one.raw_u for one in scratch.half[-1]))
    items_of = whole_of(*(one.raw_i for one in scratch.half[-1]))
    for j in range(per):
        user_out[:, j * side : (j + 1) * side] = apply_inverse(
            scratch.gram_user[ITERS - 1][-1], users_of(j)
        ).astype(BF)
    for _ in range(5):
        next(gram_item)
    for b in range(2):
        item_out[:, b * side : (b + 1) * side] = apply_inverse(
            scratch.gram_item[ITERS - 1][-1], items_of(b)
        ).astype(BF)
    for steps in ends:
        next(steps)


def main_scratch(grid, rank, side, tiles, per):
    far = grid.z // 4
    asked = grid.c * grid.y * tiles

    def vmem(n, kind=BF, rows=rank // 2):
        return pltpu.VMEM((n, rows, side), kind)

    def pair(n):
        return [sems(n), sems(n)]

    def half():
        return dict(
            sel=vmem(grid.y * tiles),
            query=vmem(grid.y * tiles),
            stage_x=vmem(grid.x * per),
            got_x=vmem(grid.x * per),
            pre_u=vmem(per, F32),
            raw_u=vmem(per, F32),
            users=vmem(grid.x * per),
            near=vmem(grid.c * grid.y * (tiles + 1)),
            stage=vmem(6 * far),
            got=vmem(6 * far),
            fars=vmem(2 * far, F32),
            far_stage=vmem(2 * far),
            got_far=vmem(2 * far),
            pre_i=vmem(2, F32),
            raw_i=vmem(2, F32),
            ysel=pair(grid.y),
            xsum=pair(grid.x),
            xall=pair(grid.x),
            ynear=pair(grid.y),
            cnear=pair(grid.y),
            znear=pair(4),
            zfar=pair(far),
            zall=spread_z_sems(grid),
        )

    return dict(
        ratings=pltpu.VMEM((tiles, side, side), BF),
        observed=pltpu.VMEM((tiles, side // 8, side), jnp.int32),
        load_sem=sems(2),
        res=pltpu.VMEM((tiles, side, side), BF),
        res_t=pltpu.VMEM((tiles, side, side), BF),
        sums=[vmem(tiles + 1, F32) for _ in range(2)],
        line=vmem(2 * grid.z * 2, BF, rank),
        lines=[vmem(2 * grid.z * 2) for _ in range(2)],
        users=vmem(grid.x * per, BF, rank),
        notes=pltpu.VMEM((2 * grid.z * grid.y, 16, side), BF),
        masks=pltpu.VMEM((tiles, side, side), BF),
        serves=pltpu.VMEM((2 * grid.z * grid.y, side), F32),
        column_v=pltpu.VMEM((8, asked), jnp.int32),
        column_s=pltpu.SMEM((8, asked), jnp.int32),
        item_v=pltpu.VMEM((grid.c * grid.y, side), jnp.int32),
        item_s=pltpu.SMEM((grid.c * grid.y, side), jnp.int32),
        table_sem=sems(2),
        note_y=pair(grid.y),
        users_x=pair(grid.x),
        line_z=spread_z_sems(grid),
        note_z=spread_z_sems(grid),
        half=[[half() for _ in range(2)] for _ in range(ITERS)],
        gram_user=[gram_scratch(grid, rank) for _ in range(ITERS)],
        gram_item=[gram_scratch(grid, rank) for _ in range(ITERS)],
    )


def main_call(grid, counts, tables, facts, item_start, user_start, ratings, observed):
    tiles, side = ratings.shape[:2]
    rank = item_start.shape[0]
    per = user_start.shape[1] // side
    scratch, tree = jax.tree.flatten(main_scratch(grid, rank, side, tiles, per))
    return pl.pallas_call(
        functools.partial(main_kernel, grid, counts, tree),
        out_shape=(
            jax.ShapeDtypeStruct((rank, per * side), BF),
            jax.ShapeDtypeStruct((rank, 2 * side), BF),
        ),
        in_specs=[pl.BlockSpec(memory_space=pltpu.SMEM)] * len(tables)
        + [pl.BlockSpec(memory_space=pltpu.VMEM)] * 3
        + [pl.BlockSpec(memory_space=pltpu.HBM)] * 2,
        out_specs=(pl.BlockSpec(memory_space=pltpu.VMEM),) * 2,
        scratch_shapes=scratch,
        compiler_params=pltpu.CompilerParams(
            collective_id=1, has_side_effects=True, vmem_limit_bytes=VMEM_LIMIT
        ),
    )(*tables, facts, item_start, user_start, ratings, observed)


def links(ids):
    at = jnp.arange(ids.shape[0], dtype=jnp.int32)
    same = (ids[:, None] == ids[None, :]) & (at[None, :] < at[:, None])
    return jnp.max(jnp.where(same, at[None, :] + 1, 0), axis=1)


def lasts(ids, n):
    tiles = ids.shape[-1]
    same = ids[..., None, :] == jnp.arange(n, dtype=jnp.int32)[:, None]
    return jnp.max(jnp.where(same, jnp.arange(1, tiles + 1, dtype=jnp.int32), 0), axis=-1)


def local(grid, ratings, observed, user_start, item_start, exposure, serve_list, tile_slot, tile_user):
    side = ratings.shape[2]
    own_users = user_start.shape[1]
    tiles = ratings.shape[0]
    owners = grid.y * grid.z * grid.c
    counts = (own_users * owners * grid.x * 1.0, item_start.shape[1] * owners * grid.x * 1.0)
    per = own_users // side
    sy, sz, sc = slots_of(grid, tile_slot)
    tables = (
        tile_user,
        sy * tiles + jnp.arange(tiles, dtype=jnp.int32),
        (sc * grid.z + sz) * grid.y + sy,
        links(tile_user),
        lasts(tile_user, grid.x * per),
    )
    rows = [exposure, jnp.pad(serve_list, (0, side - owners)), jnp.pad(tile_slot, (0, side - tiles))]
    facts = jnp.concatenate(rows + [jnp.zeros((4 * side,), jnp.int32)]).reshape(8, side)
    return main_call(grid, counts, tables, facts, item_start, user_start, ratings, observed)


def solution(mesh):
    grid = Grid(mesh.shape["rows"], mesh.shape["rep"])
    both = P(("rows", "rep"))
    second = P(None, ("rows", "rep"))
    return jax.shard_map(
        functools.partial(local, grid),
        mesh=mesh,
        in_specs=(both, both, second, second, both, both, both, both),
        out_specs=(second, second),
        check_vma=False,
    )
```

```python
import functools

import jax
import jax.numpy as jnp
from jax import lax
from jax.experimental import pallas as pl
from jax.experimental.pallas import tpu as pltpu
from jax.sharding import PartitionSpec as P

LEVELS = 16
ITERS = 2
MESH = pl.DeviceIdType.MESH
BF = jnp.bfloat16
F32 = jnp.float32
HIGHEST = lax.Precision.HIGHEST
VMEM_LIMIT = 62 * 1024 * 1024


class Grid:
    def __init__(self, rows, rep):
        self.c = 2
        self.x = rep
        self.y = 4
        self.z = rows // (self.c * self.y)


class Names:
    def __init__(self, **named):
        self.__dict__.update(named)


def named(tree):
    if isinstance(tree, dict):
        return Names(**{key: named(value) for key, value in tree.items()})
    return [named(value) for value in tree] if isinstance(tree, (list, tuple)) else tree


class Here:
    def __init__(self, grid):
        r = lax.axis_index("rows")
        self.grid = grid
        self.r = r
        self.x = lax.axis_index("rep")
        self.y = r // (grid.z * grid.c)
        self.z = (r // grid.c) % grid.z
        self.c = r % grid.c

    def along_x(self, to):
        return self.r, to

    def along_y(self, to):
        return (to * self.grid.z + self.z) * self.grid.c + self.c, self.x

    def along_z(self, to):
        return (self.y * self.grid.z + to) * self.grid.c + self.c, self.x

    def along_yc(self, to):
        y, c = to // self.grid.c, to % self.grid.c
        return (y * self.grid.z + self.z) * self.grid.c + c, self.x

    def other_core(self):
        return (self.y * self.grid.z + self.z) * self.grid.c + 1 - self.c, self.x

    def z_off(self, by):
        return (self.z + by + 2 * self.grid.z) % self.grid.z

    def greet(self):
        grid = self.grid
        targets = [self.along_x((self.x + i) % grid.x) for i in range(1, grid.x)]
        for i in range(grid.y):
            for j in range(grid.c):
                if i or j:
                    to = ((self.y + i) % grid.y) * grid.c + (self.c + j) % 2
                    targets.append(self.along_yc(to))
        targets += [self.along_z(self.z_off(o)) for o in range(1, grid.z)]
        barrier = pltpu.get_barrier_semaphore()
        for target in targets:
            pl.semaphore_signal(barrier, inc=1, device_id=target, device_id_type=MESH)
        yield
        pl.semaphore_wait(barrier, len(targets))
        yield


def remote(src, dst, send_sem, recv_sem, device):
    return pltpu.make_async_remote_copy(
        src_ref=src,
        dst_ref=dst,
        send_sem=send_sem,
        recv_sem=recv_sem,
        device_id=device,
        device_id_type=MESH,
    )


def sems(*shape):
    return pltpu.SemaphoreType.DMA(shape)


def spread_x(here, buf, per, send, recv):
    n = here.grid.x

    def copy(to, slot):
        block = buf.at[pl.ds(slot * per, per)]
        return remote(block, block, send.at[to], recv.at[slot], here.along_x(to))

    for i in range(1, n):
        copy((here.x + i) % n, here.x).start()
    yield
    for i in range(1, n):
        copy((here.x + i) % n, (here.x + i) % n).wait_recv()
    yield
    for i in range(1, n):
        copy((here.x + i) % n, here.x).wait_send()
    yield


def spread_z_sems(grid):
    far = grid.z // 4
    return [sems(far), sems(far), sems(far, 4), sems(far, 4), sems(1), sems(1)]


def spread_z(here, buf, n, far_send, far_recv, near_send, near_recv, c_send, c_recv):
    grid = here.grid
    half = n // 2
    far = grid.z // 4

    def chunk(core, zz, start=0, count=n):
        return buf.at[pl.ds((core * grid.z + zz) * n + start, count)]

    def far_copy(k):
        block = chunk(here.c, here.z)
        return remote(block, block, far_send.at[k], far_recv.at[k], here.along_z(here.z_off(4 * k)))

    def far_arrival(k):
        block = chunk(here.c, here.z_off(-4 * k))
        return remote(block, block, far_send.at[k], far_recv.at[k], here.along_z(here.z_off(-4 * k)))

    ways = [(1, 0, n), (-1, 0, n), (-2, 0, half), (2, half, half)]

    def near_copy(k, way):
        by, start, count = ways[way]
        block = chunk(here.c, here.z_off(-4 * k), start, count)
        return remote(
            block, block, near_send.at[k, way], near_recv.at[k, way], here.along_z(here.z_off(by))
        )

    def near_arrival(k, way):
        by, start, count = ways[way]
        block = chunk(here.c, here.z_off(-by - 4 * k), start, count)
        return remote(
            block, block, near_send.at[k, way], near_recv.at[k, way], here.along_z(here.z_off(-by))
        )

    for k in range(1, far):
        far_copy(k).start()
    for way in range(4):
        near_copy(0, way).start()
    yield
    for k in range(1, far):
        far_arrival(k).wait_recv()
        for way in range(4):
            near_copy(k, way).start()
    yield
    for k in range(far):
        for way in range(4):
            near_arrival(k, way).wait_recv()
    line = buf.at[pl.ds(here.c * grid.z * n, grid.z * n)]
    swap = remote(line, line, c_send.at[0], c_recv.at[0], here.other_core())
    swap.start()
    yield
    line = buf.at[pl.ds((1 - here.c) * grid.z * n, grid.z * n)]
    remote(line, line, c_send.at[0], c_recv.at[0], here.other_core()).wait_recv()
    yield
    swap.wait_send()
    for k in range(far):
        if k:
            far_copy(k).wait_send()
        for way in range(4):
            near_copy(k, way).wait_send()
    yield


def exchange(n, me, device, put, take, send, recv):
    def copy(to):
        return remote(put(to), take(me), send.at[to], recv.at[me], device(to))

    def arrival(slot):
        return remote(put(slot), take(slot), send.at[slot], recv.at[slot], device(slot))

    for i in range(1, n):
        copy((me + i) % n).start()
    yield
    for i in range(1, n):
        arrival((me + i) % n).wait_recv()
    yield
    for i in range(1, n):
        copy((me + i) % n).wait_send()
    yield


def add_up(ref, n):
    total = ref[0]
    for i in range(1, n):
        total = total + ref[i]
    return total


def gram_scratch(grid, rank):
    shape = (rank // grid.x // 2, 2 * rank)
    counts = [grid.x, grid.y * grid.c, grid.z, grid.x]
    buffers = [pltpu.VMEM((n,) + shape, F32) for n in [grid.x] + counts]
    return buffers + [sems(n) for n in counts for _ in range(2)] + [pltpu.VMEM((rank, 2 * rank), F32)]


def gram_steps(here, block, blocks, row_count, scratch, scale_only=False):
    grid = here.grid
    part, first, second, third, whole = scratch[:5]
    pairs = [scratch[5 + 2 * i : 7 + 2 * i] for i in range(4)]
    work = scratch[-1]
    total = None
    for i in range(blocks):
        value = block(i)
        one = lax.dot_general(
            value, value, (((1,), (1,)), ((), ())), precision=HIGHEST, preferred_element_type=F32
        )
        total = one if total is None else total + one
    k = total.shape[0]
    rows = k // grid.x
    low = rows // 2
    for p in range(grid.x):
        part[p] = jnp.concatenate(
            [total[p * rows : p * rows + low], total[p * rows + low : (p + 1) * rows]], axis=1
        )
    x, z = here.x, here.z
    group = here.y * grid.c + here.c
    first[x] = part[x]
    ends = []

    def run(n, me, device, put, ref, pair):
        steps = exchange(n, me, device, put, lambda slot: ref.at[slot], *pair)
        next(steps)
        ends.append(steps)
        return steps

    steps = run(grid.x, x, here.along_x, lambda to: part.at[to], first, pairs[0])
    yield
    next(steps)
    second[group] = add_up(first, grid.x)
    mine = second.at[group]
    steps = run(grid.y * grid.c, group, here.along_yc, lambda to, mine=mine: mine, second, pairs[1])
    yield
    next(steps)
    third[z] = add_up(second, grid.y * grid.c)
    mine = third.at[z]
    steps = run(grid.z, z, here.along_z, lambda to, mine=mine: mine, third, pairs[2])
    yield
    next(steps)
    whole[x] = add_up(third, grid.z)
    mine = whole.at[x]
    steps = run(grid.x, x, here.along_x, lambda to, mine=mine: mine, whole, pairs[3])
    yield
    next(steps)
    row = lax.broadcasted_iota(jnp.int32, (low, k), 0)
    lane = lax.broadcasted_iota(jnp.int32, (low, k), 1)
    for p in range(grid.x):
        for h in range(2):
            at = p * rows + h * low
            unit = jnp.where(row + at == lane, 1.0, 0.0).astype(F32)
            value = whole[p][:, h * k : (h + 1) * k] * (1.0 / row_count)
            work[at : at + low, :] = jnp.concatenate([value, unit], axis=1)
    for steps in ends:
        next(steps)
    yield
    row = lax.broadcasted_iota(jnp.int32, (k, 2 * k), 0)
    lane = lax.broadcasted_iota(jnp.int32, (k, 2 * k), 1)

    if not scale_only:
        eliminate(work)
    value = work[...]
    diagonal = jnp.sum(jnp.where(lane == row, value, 0.0), axis=1, keepdims=True)
    work[...] = (jnp.ones_like(value) if scale_only else value) * lax.rsqrt(diagonal)
    yield


def eliminate(work, width=4):
    k = work.shape[0]
    row = lax.broadcasted_iota(jnp.int32, (k, 1), 0)
    lane = lax.broadcasted_iota(jnp.int32, work.shape, 1)

    def lane_sum(value, at):
        return jnp.sum(jnp.where(lane[: value.shape[0]] == at, value, 0.0), axis=1, keepdims=True)

    @pl.loop(0, k // width)
    def _(i):
        at = i * width
        value = work[...]
        rows = [work[pl.ds(at + a, 1), :] for a in range(width)]
        columns = [lane_sum(value, at + a) for a in range(width)]
        block = [[lane_sum(rows[a], at + b) for b in range(width)] for a in range(width)]
        for a in range(width):
            inverse = 1.0 / block[a][a]
            left = columns[a] * inverse
            for b in range(a + 1, width):
                factor = block[a][b] * inverse
                rows[b] = rows[b] - factor * rows[a]
                columns[b] = columns[b] - left * block[a][b]
                for d in range(b, width):
                    block[b][d] = block[b][d] - factor * block[a][d]
            value = value - jnp.where(row > at + a, left, 0.0) * rows[a]
        work[...] = value


def apply_inverse(work, value, first=0):
    k = work.shape[0]
    rows = work[first:, k:] if first else work[: value.shape[0], k : k + value.shape[0]]
    return jnp.dot(rows, value, precision=HIGHEST, preferred_element_type=F32)


def slots_of(grid, value):
    return value // (grid.z * grid.c), (value // grid.c) % grid.z, value % grid.c


def work_out_tables(here, tiles, notes, serves, column_table, item_table):
    grid = here.grid
    group = grid.c * grid.y
    n = group * tiles
    owners = grid.c * grid.z * grid.y
    side = notes.shape[2]

    @pl.loop(0, owners)
    def _(i):
        serves[pl.ds(i, 1), :] = notes[i][2:3].astype(F32)

    row = lax.broadcasted_iota(jnp.int32, (n, side), 0)
    lane = lax.broadcasted_iota(jnp.int32, (n, side), 1)
    tile, member = row % tiles, row // tiles
    asked = []
    for core in range(grid.c):
        for y in range(grid.y):
            line = notes[(core * grid.z + here.z) * grid.y + y][3:4].astype(F32)
            asked.append(jnp.broadcast_to(line, (tiles, side)))
    asked = jnp.concatenate(asked, axis=0)

    def column(value):
        return jnp.sum(value, axis=1, keepdims=True)

    slot = column(jnp.where(lane == tile, asked, 0.0)).astype(jnp.int32)
    sy, sz, sc = slots_of(grid, slot)
    where = (sc * grid.z + sz) * grid.y + sy
    hot = jnp.where(lane == where, 1.0, 0.0).astype(BF)[:, :owners]
    served = jnp.dot(hot, serves[...].astype(BF), preferred_element_type=F32)
    asker = ((member % grid.y) * grid.z + here.z) * grid.c + member // grid.y
    pick = column(jnp.where(lane == asker, served, 0.0)).astype(jnp.int32)
    line_at = (sc * grid.z + sz) * 2 + pick
    ask = jnp.where(sy == here.y, line_at, 0)
    ids = where * 2 + pick
    across = jnp.broadcast_to(ids.astype(F32), (n, side)).T.astype(jnp.int32)[:n]
    square_lane, square_row = lane[:, :n], row[:, :n]
    same = (across == ids) & (square_lane // tiles == square_row // tiles) & (square_lane < square_row)
    before = jnp.max(jnp.where(same, square_lane % tiles + 1, 0).astype(F32), axis=1, keepdims=True)
    columns = jnp.where(
        lane == 0, ask.astype(F32), jnp.where(lane == 1, pick.astype(F32), jnp.where(lane == 2, before, 0.0))
    )
    column_table[...] = columns.T[:8].astype(jnp.int32)
    mine = jnp.where((sy == here.y) & (sc == here.c), sz * 2 + pick, -1)
    number = jnp.where(mine == lane, tile + 1, 0).astype(F32)
    for g in range(group):
        last = jnp.max(number[g * tiles : (g + 1) * tiles], axis=0, keepdims=True)
        item_table[g : g + 1, :] = last.astype(jnp.int32) + g * (tiles + 1)


def within(at, ref):
    return jnp.minimum(jnp.maximum(at, 0), ref.shape[0] - 1)


def work_out_users(tiles, x_notes, user_table):
    side = x_notes.shape[2]
    row = lax.broadcasted_iota(jnp.int32, (tiles, side), 0)
    lane = lax.broadcasted_iota(jnp.int32, (tiles, side), 1)
    for x in range(x_notes.shape[0]):
        line = jnp.broadcast_to(x_notes[x][4:5].astype(F32), (tiles, side))
        block = jnp.sum(jnp.where(lane == row, line, 0.0), axis=1, keepdims=True).astype(jnp.int32)
        number = jnp.where(block == lane, row + 1, 0).astype(F32)
        last = jnp.max(number, axis=0, keepdims=True).astype(jnp.int32)
        user_table[x : x + 1, :] = last + x * (tiles + 1)


def unpack_masks(observed, masks):
    side = masks.shape[1]

    @pl.loop(0, masks.shape[0])
    def _(t):
        words = observed[t]
        spread = jnp.broadcast_to(words[:, None, :], (words.shape[0], 8, side)).reshape(side, side)
        shift = lax.broadcasted_iota(jnp.int32, (side, side), 0) % 8
        masks[t] = ((spread >> shift) & 1).astype(F32).T.astype(BF)


def residual_tiles(tables, own, query, notes, users, ratings, masks, out, out_t):
    tiles = ratings.shape[0]

    @pl.loop(0, tiles, unroll=4)
    def _(t):
        meta = notes[tables.note_at[t]].astype(F32)
        line = lax.broadcasted_iota(jnp.int32, meta.shape, 0)
        pick = tables.column[1, own * tiles + t]
        weight = jnp.sum(jnp.where(line == pick, meta, 0.0), axis=0, keepdims=True)
        items = jnp.concatenate([part[tables.query_at[t]] for part in query], axis=0)
        guess = lax.dot_general(
            users[tables.user_at[t]], items, (((0,), (0,)), ((), ())), preferred_element_type=F32
        )
        value = masks[t].astype(F32) * weight * (ratings[t].astype(F32) - guess)
        out[t] = value.astype(BF)
        out_t[t] = value.T.astype(BF)


def main_kernel(grid, counts, tree, *refs):
    refs = list(refs)
    tables = Names()
    tables.user_at, tables.query_at, tables.note_at, tables.user_before = (refs.pop(0) for _ in range(4))
    facts, *given, user_out, item_out = (refs.pop(0) for _ in range(7))
    scratch = named(jax.tree.unflatten(tree, refs))
    here = Here(grid)
    item_start, user_start, ratings, observed = kept = (
        scratch.item_start,
        scratch.user_start,
        scratch.ratings,
        scratch.observed,
    )
    loads = [
        pltpu.make_async_copy(there, ref, scratch.load_sem.at[i])
        for i, (there, ref) in enumerate(zip(given, kept))
    ]
    for load in loads:
        load.start()
    tiles, side = ratings.shape[:2]
    per = user_out.shape[1] // side
    rank = user_out.shape[0]
    x, y, z, c = here.x, here.y, here.z, here.c
    half = rank // 2
    res, res_t = scratch.res, scratch.res_t
    near_rows = tiles + 1
    far = grid.z // 4

    line, notes, users = scratch.line, scratch.notes, scratch.users
    ends = []
    greeting = here.greet()
    next(greeting)

    for load in loads[:2]:
        load.wait()
    for b in range(2):
        line[(c * grid.z + z) * 2 + b] = item_start[:, b * side : (b + 1) * side]
    for j in range(per):
        users[x * per + j] = user_start[:, j * side : (j + 1) * side]
    facts_f = facts[...].astype(F32)
    weight = (LEVELS + 1.0) / (facts_f + 1.0)
    facts_row = lax.broadcasted_iota(jnp.int32, facts.shape, 0)
    note_at = (c * grid.z + z) * grid.y + y
    first_rows = jnp.where(facts_row < 2, weight, facts_f)
    notes[note_at] = jnp.concatenate([first_rows, jnp.zeros_like(first_rows)], axis=0).astype(BF)
    for h in range(2):
        scratch.sums[h][0] = jnp.zeros((half, side), F32)
        for it in range(ITERS):
            near = scratch.half[it][h].near
            for s in range(grid.c * grid.y):
                near[s * near_rows] = jnp.zeros((half, side), BF)
            for s in range(grid.x):
                scratch.half[it][h].got_x[s * near_rows] = jnp.zeros((half, side), BF)
    scratch.x_notes[x] = notes[note_at]
    for load in loads[2:]:
        load.wait()
    unpack_masks(observed, scratch.masks)
    next(greeting)
    mine = notes.at[note_at]
    note_y = exchange(
        grid.y,
        y,
        here.along_y,
        lambda to: mine,
        lambda slot: notes.at[(c * grid.z + z) * grid.y + slot],
        *scratch.note_y,
    )
    note_x = exchange(
        grid.x, x, here.along_x, lambda to: mine, lambda slot: scratch.x_notes.at[slot], *scratch.note_x
    )
    items = spread_z(here, line, 2, *scratch.line_z)
    people = spread_x(here, users, per, *scratch.users_x)
    note_z = spread_z(here, notes, grid.y, *scratch.note_z)
    next(note_y)
    next(items)
    next(note_x)
    next(people)
    next(note_y)
    next(note_z)
    next(note_z)
    next(items)
    next(note_z)
    next(items)
    next(note_z)
    next(note_x)
    work_out_users(tiles, scratch.x_notes, scratch.user_v)
    work_out_tables(here, tiles, notes, scratch.serves, scratch.column_v, scratch.item_v)
    copies = [
        pltpu.make_async_copy(scratch.column_v, scratch.column_s, scratch.table_sem.at[0]),
        pltpu.make_async_copy(scratch.item_v, scratch.item_s, scratch.table_sem.at[1]),
        pltpu.make_async_copy(scratch.user_v, scratch.user_s, scratch.table_sem.at[2]),
    ]
    for copy in copies:
        copy.start()
    for copy in copies:
        copy.wait()
    tables.column = scratch.column_s
    own = c * grid.y + y
    next(items)
    next(people)
    ends += [note_x, note_y, items, people, note_z]

    def chain(h):
        rows = slice(h * half, (h + 1) * half)
        sums = scratch.sums[h]
        for it in range(ITERS):
            mine, low = scratch.half[it][h], scratch.half[it][0]
            sel, query, got_x, raw_u = mine.sel, mine.query, mine.got_x, mine.raw_u
            new_users, near, stage, got, fars, got_far, pre_i, raw_i = (
                mine.users,
                mine.near,
                mine.stage,
                mine.got,
                mine.fars,
                mine.got_far,
                mine.pre_i,
                mine.raw_i,
            )
            for i in range(grid.y):
                to = (y + i) % grid.y

                @pl.loop(0, tiles, unroll=4)
                def _(t):
                    at = tables.column[0, (c * grid.y + to) * tiles + t]
                    if it:
                        block = scratch.lines[h][within(at, line)]
                    else:
                        block = line[within(at, line)][rows]
                    sel[to * tiles + t] = block

            asked = exchange(
                grid.y,
                y,
                here.along_y,
                lambda to, sel=sel: sel.at[pl.ds(to * tiles, tiles)],
                lambda slot, query=query: query.at[pl.ds(slot * tiles, tiles)],
                *mine.ysel,
            )
            next(asked)
            query[pl.ds(y * tiles, tiles)] = sel[pl.ds(y * tiles, tiles)]
            yield
            next(asked)
            ends.append(asked)
            if it == 0:
                yield

            @pl.loop(0, tiles, unroll=4)
            def _(t):
                product = jnp.dot(query[tables.query_at[t]], res_t[t], preferred_element_type=F32)
                total = product + sums[tables.user_before[t]]
                sums[t + 1] = total
                got_x[x * near_rows + 1 + t] = total.astype(BF)

            def sums_from(slot, got_x=got_x):
                return got_x.at[pl.ds(slot * near_rows + 1, tiles)]

            parts = exchange(
                grid.x, x, here.along_x, lambda to, f=sums_from: f(x), lambda slot, f=sums_from: f(slot), *mine.xsum
            )
            next(parts)
            yield
            next(parts)
            ends.append(parts)

            def user_sum(block):
                total = None
                for s in range(grid.x):
                    value = got_x[within(scratch.user_s[s, block], got_x)].astype(F32)
                    total = value if total is None else total + value
                return total * scratch.gram_item[it - 1][-1][rows] if it else total

            @pl.loop(0, grid.x * per, unroll=4)
            def _(j):
                new_users[j] = user_sum(j).astype(BF)

            @pl.loop(0, per, unroll=4)
            def _(j):
                raw_u[j] = user_sum(x * per + j)

            yield

            @pl.loop(0, tiles, unroll=4)
            def _(t):
                product = jnp.dot(new_users[tables.user_at[t]], res[t], preferred_element_type=F32)
                total = product + sums[within(tables.column[2, own * tiles + t], sums)]
                sums[t + 1] = total
                near[own * near_rows + 1 + t] = total.astype(BF)

            def rows_of(core, slot, near=near):
                return near.at[pl.ds((core * grid.y + slot) * near_rows + 1, tiles)]

            along = exchange(
                grid.y, y, here.along_y, lambda to, f=rows_of: f(c, y), lambda slot, f=rows_of: f(c, slot), *mine.ynear
            )
            next(along)
            c_send, c_recv = mine.cnear

            def c_copy(core, slot):
                block = rows_of(core, slot)
                return remote(block, block, c_send.at[slot], c_recv.at[slot], here.other_core())

            c_copy(c, y).start()
            yield
            next(along)
            ends.append(along)
            for i in range(1, grid.y):
                c_copy(c, (y + i) % grid.y).start()
            yield
            for i in range(grid.y):
                c_copy(1 - c, (y + i) % grid.y).wait_recv()

            def gathered(zz, b):
                total = None
                for s in range(grid.c * grid.y):
                    at = scratch.item_s[s, zz * 2 + b]
                    value = near[within(at, near)].astype(F32)
                    total = value if total is None else total + value
                return total

            z_send, z_recv = mine.znear
            ways = [(1, (0, 1)), (-1, (0, 1)), (-2, (0,)), (2, (1,))]
            starts = [0, 2 * far, 4 * far, 5 * far]

            def near_z(way, arrival=False):
                by, parts_ = ways[way]
                count = len(parts_) * far
                to = here.along_z(here.z_off(-by if arrival else by))
                return remote(
                    stage.at[pl.ds(starts[way], count)],
                    got.at[pl.ds(starts[way], count)],
                    z_send.at[way],
                    z_recv.at[way],
                    to,
                )

            for way in (3, 2, 1, 0):
                by, parts_ = ways[way]

                @pl.loop(0, far)
                def _(k):
                    for j, b in enumerate(parts_):
                        zz = here.z_off(by + 4 * k)
                        stage[starts[way] + len(parts_) * k + j] = gathered(zz, b).astype(BF)

                near_z(way).start()

            @pl.loop(0, far)
            def _(k):
                for b in range(2):
                    fars[2 * k + b] = gathered(here.z_off(4 * k), b)

            yield
            for way in range(4):
                near_z(way, True).wait_recv()
            f_send, f_recv = mine.zfar
            far_stage = mine.far_stage

            def far_copy(k):
                return remote(
                    far_stage.at[pl.ds(2 * k, 2)],
                    got_far.at[pl.ds(2 * k, 2)],
                    f_send.at[k],
                    f_recv.at[k],
                    here.along_z(here.z_off(4 * k)),
                )

            for k in list(range(1, far)) + [0]:
                for b in range(2):
                    total = (
                        fars[2 * k + b]
                        + got[starts[0] + 2 * k + b].astype(F32)
                        + got[starts[1] + 2 * k + b].astype(F32)
                        + got[starts[2 + b] + k].astype(F32)
                    )
                    if k:
                        far_stage[2 * k + b] = total.astype(BF)
                    else:
                        pre_i[b] = total
                if k:
                    far_copy(k).start()
            yield
            for k in range(1, far):
                far_copy(k).wait_recv()
            work = scratch.gram_user[it][-1]
            for b in range(2):
                total = pre_i[b]
                for k in range(1, far):
                    total = total + got_far[2 * k + b].astype(F32)
                pre_i[b] = total
                if h:
                    raw_i[b] = apply_inverse(
                        work, jnp.concatenate([low.pre_i[b], total], axis=0), half
                    )
                else:
                    raw_i[b] = apply_inverse(work, total)
            if it + 1 < ITERS:
                next_line = scratch.lines[h]
                for b in range(2):
                    next_line[(c * grid.z + z) * 2 + b] = raw_i[b].astype(BF)
                items = spread_z(here, next_line, 2, *mine.zall)
                ends.append(items)
                for _ in range(3):
                    next(items)
                    yield
                next(items)
            for i in range(grid.y):
                c_copy(c, (y + i) % grid.y).wait_send()
            for way in range(4):
                near_z(way).wait_send()
            for k in range(1, far):
                far_copy(k).wait_send()
        yield

    def whole_of(low, high):
        return lambda i: jnp.concatenate([low[i], high[i]], axis=0)

    chains = [chain(0), chain(1)]

    def step():
        for one in chains:
            next(one)

    gram_item = None
    for it in range(ITERS):
        if it == 0:
            step()
            step()
            query = [one.query for one in scratch.half[0]]
            residual_tiles(tables, own, query, notes, users, ratings, scratch.masks, res, res_t)
            step()
        else:
            step()
            next(gram_item)
            step()
            next(gram_item)
            next(gram_item)
        step()
        gram_user = gram_steps(here, whole_of(*(one.raw_u for one in scratch.half[it])), per, counts[0], scratch.gram_user[it])
        next(gram_user)
        step()
        next(gram_user)
        step()
        next(gram_user)
        step()
        next(gram_user)
        step()
        next(gram_user)
        next(gram_user)
        step()
        gram_item = gram_steps(
            here,
            whole_of(*(one.raw_i for one in scratch.half[it])),
            2,
            counts[1],
            scratch.gram_item[it],
            scale_only=it + 1 < ITERS,
        )
        next(gram_item)
        if it + 1 < ITERS:
            step()
            next(gram_item)
            step()
            next(gram_item)
    users_of = whole_of(*(one.raw_u for one in scratch.half[-1]))
    items_of = whole_of(*(one.raw_i for one in scratch.half[-1]))
    for j in range(per):
        user_out[:, j * side : (j + 1) * side] = apply_inverse(
            scratch.gram_user[ITERS - 1][-1], users_of(j)
        ).astype(BF)
    for _ in range(5):
        next(gram_item)
    for b in range(2):
        item_out[:, b * side : (b + 1) * side] = apply_inverse(
            scratch.gram_item[ITERS - 1][-1], items_of(b)
        ).astype(BF)
    for steps in ends:
        next(steps)


def main_scratch(grid, rank, side, tiles, per):
    far = grid.z // 4
    asked = grid.c * grid.y * tiles

    def vmem(n, kind=BF, rows=rank // 2):
        return pltpu.VMEM((n, rows, side), kind)

    def pair(n):
        return [sems(n), sems(n)]

    def half():
        return dict(
            sel=vmem(grid.y * tiles),
            query=vmem(grid.y * tiles),
            got_x=vmem(grid.x * (tiles + 1)),
            raw_u=vmem(per, F32),
            users=vmem(grid.x * per),
            near=vmem(grid.c * grid.y * (tiles + 1)),
            stage=vmem(6 * far),
            got=vmem(6 * far),
            fars=vmem(2 * far, F32),
            far_stage=vmem(2 * far),
            got_far=vmem(2 * far),
            pre_i=vmem(2, F32),
            raw_i=vmem(2, F32),
            ysel=pair(grid.y),
            xsum=pair(grid.x),
            ynear=pair(grid.y),
            cnear=pair(grid.y),
            znear=pair(4),
            zfar=pair(far),
            zall=spread_z_sems(grid),
        )

    return dict(
        ratings=pltpu.VMEM((tiles, side, side), BF),
        observed=pltpu.VMEM((tiles, side // 8, side), jnp.int32),
        item_start=pltpu.VMEM((rank, 2 * side), BF),
        user_start=pltpu.VMEM((rank, per * side), BF),
        load_sem=sems(4),
        x_notes=pltpu.VMEM((grid.x, 16, side), BF),
        user_v=pltpu.VMEM((grid.x, side), jnp.int32),
        user_s=pltpu.SMEM((grid.x, side), jnp.int32),
        note_x=pair(grid.x),
        res=pltpu.VMEM((tiles, side, side), BF),
        res_t=pltpu.VMEM((tiles, side, side), BF),
        sums=[vmem(tiles + 1, F32) for _ in range(2)],
        line=vmem(2 * grid.z * 2, BF, rank),
        lines=[vmem(2 * grid.z * 2) for _ in range(2)],
        users=vmem(grid.x * per, BF, rank),
        notes=pltpu.VMEM((2 * grid.z * grid.y, 16, side), BF),
        masks=pltpu.VMEM((tiles, side, side), BF),
        serves=pltpu.VMEM((2 * grid.z * grid.y, side), F32),
        column_v=pltpu.VMEM((8, asked), jnp.int32),
        column_s=pltpu.SMEM((8, asked), jnp.int32),
        item_v=pltpu.VMEM((grid.c * grid.y, side), jnp.int32),
        item_s=pltpu.SMEM((grid.c * grid.y, side), jnp.int32),
        table_sem=sems(3),
        note_y=pair(grid.y),
        users_x=pair(grid.x),
        line_z=spread_z_sems(grid),
        note_z=spread_z_sems(grid),
        half=[[half() for _ in range(2)] for _ in range(ITERS)],
        gram_user=[gram_scratch(grid, rank) for _ in range(ITERS)],
        gram_item=[gram_scratch(grid, rank) for _ in range(ITERS)],
    )


def main_call(grid, counts, tables, facts, item_start, user_start, ratings, observed):
    tiles, side = ratings.shape[:2]
    rank = item_start.shape[0]
    per = user_start.shape[1] // side
    scratch, tree = jax.tree.flatten(main_scratch(grid, rank, side, tiles, per))
    return pl.pallas_call(
        functools.partial(main_kernel, grid, counts, tree),
        out_shape=(
            jax.ShapeDtypeStruct((rank, per * side), BF),
            jax.ShapeDtypeStruct((rank, 2 * side), BF),
        ),
        in_specs=[pl.BlockSpec(memory_space=pltpu.SMEM)] * len(tables)
        + [pl.BlockSpec(memory_space=pltpu.VMEM)]
        + [pl.BlockSpec(memory_space=pltpu.HBM)] * 4,
        out_specs=(pl.BlockSpec(memory_space=pltpu.VMEM),) * 2,
        scratch_shapes=scratch,
        compiler_params=pltpu.CompilerParams(
            collective_id=1, has_side_effects=True, vmem_limit_bytes=VMEM_LIMIT
        ),
    )(*tables, facts, item_start, user_start, ratings, observed)


def links(ids):
    at = jnp.arange(ids.shape[0], dtype=jnp.int32)
    same = (ids[:, None] == ids[None, :]) & (at[None, :] < at[:, None])
    return jnp.max(jnp.where(same, at[None, :] + 1, 0), axis=1)


def local(grid, ratings, observed, user_start, item_start, exposure, serve_list, tile_slot, tile_user):
    side = ratings.shape[2]
    own_users = user_start.shape[1]
    tiles = ratings.shape[0]
    owners = grid.y * grid.z * grid.c
    counts = (own_users * owners * grid.x * 1.0, item_start.shape[1] * owners * grid.x * 1.0)
    per = own_users // side
    sy, sz, sc = slots_of(grid, tile_slot)
    tables = (
        tile_user,
        sy * tiles + jnp.arange(tiles, dtype=jnp.int32),
        (sc * grid.z + sz) * grid.y + sy,
        links(tile_user),
    )
    rows = [exposure] + [jnp.pad(value, (0, side - value.shape[0])) for value in (serve_list, tile_slot, tile_user)]
    facts = jnp.concatenate(rows + [jnp.zeros((3 * side,), jnp.int32)]).reshape(8, side)
    return main_call(grid, counts, tables, facts, item_start, user_start, ratings, observed)


def solution(mesh):
    grid = Grid(mesh.shape["rows"], mesh.shape["rep"])
    both = P(("rows", "rep"))
    second = P(None, ("rows", "rep"))
    return jax.shard_map(
        functools.partial(local, grid),
        mesh=mesh,
        in_specs=(both, both, second, second, both, both, both, both),
        out_specs=(second, second),
        check_vma=False,
    )
```

```python
import functools

import jax
import jax.numpy as jnp
from jax import lax
from jax.experimental import pallas as pl
from jax.experimental.pallas import tpu as pltpu
from jax.sharding import PartitionSpec as P

LEVELS = 16
ITERS = 2
MESH = pl.DeviceIdType.MESH
BF = jnp.bfloat16
F32 = jnp.float32
HIGHEST = lax.Precision.HIGHEST
VMEM_LIMIT = 48 * 1024 * 1024


class Grid:
    def __init__(self, rows, rep):
        self.c = 2
        self.x = rep
        self.y = 4
        self.z = rows // (self.c * self.y)


class Names:
    def __init__(self, **named):
        self.__dict__.update(named)


def named(tree):
    if isinstance(tree, dict):
        return Names(**{key: named(value) for key, value in tree.items()})
    return [named(value) for value in tree] if isinstance(tree, (list, tuple)) else tree


class Here:
    def __init__(self, grid):
        r = lax.axis_index("rows")
        self.grid = grid
        self.r = r
        self.x = lax.axis_index("rep")
        self.y = r // (grid.z * grid.c)
        self.z = (r // grid.c) % grid.z
        self.c = r % grid.c

    def along_x(self, to):
        return self.r, to

    def along_y(self, to):
        return (to * self.grid.z + self.z) * self.grid.c + self.c, self.x

    def along_z(self, to):
        return (self.y * self.grid.z + to) * self.grid.c + self.c, self.x

    def along_yc(self, to):
        y, c = to // self.grid.c, to % self.grid.c
        return (y * self.grid.z + self.z) * self.grid.c + c, self.x

    def other_core(self):
        return (self.y * self.grid.z + self.z) * self.grid.c + 1 - self.c, self.x

    def z_off(self, by):
        return (self.z + by + 2 * self.grid.z) % self.grid.z

    def greet(self):
        grid = self.grid
        targets = [self.along_x((self.x + i) % grid.x) for i in range(1, grid.x)]
        for i in range(grid.y):
            for j in range(grid.c):
                if i or j:
                    to = ((self.y + i) % grid.y) * grid.c + (self.c + j) % 2
                    targets.append(self.along_yc(to))
        targets += [self.along_z(self.z_off(o)) for o in range(1, grid.z)]
        barrier = pltpu.get_barrier_semaphore()
        for target in targets:
            pl.semaphore_signal(barrier, inc=1, device_id=target, device_id_type=MESH)
        yield
        pl.semaphore_wait(barrier, len(targets))
        yield


def remote(src, dst, send_sem, recv_sem, device):
    return pltpu.make_async_remote_copy(
        src_ref=src,
        dst_ref=dst,
        send_sem=send_sem,
        recv_sem=recv_sem,
        device_id=device,
        device_id_type=MESH,
    )


def sems(*shape):
    return pltpu.SemaphoreType.DMA(shape)


def spread_x(here, buf, per, send, recv):
    n = here.grid.x

    def copy(to, slot):
        block = buf.at[pl.ds(slot * per, per)]
        return remote(block, block, send.at[to], recv.at[slot], here.along_x(to))

    for i in sorted(range(1, n), key=lambda i: -min(i, n - i)):
        copy((here.x + i) % n, here.x).start()
    yield
    for i in range(1, n):
        copy((here.x + i) % n, (here.x + i) % n).wait_recv()
    yield
    for i in range(1, n):
        copy((here.x + i) % n, here.x).wait_send()
    yield


def spread_z_sems(grid):
    far = grid.z // 4
    return [sems(far), sems(far), sems(far, 4), sems(far, 4), sems(1), sems(1)]


def spread_z(here, buf, n, far_send, far_recv, near_send, near_recv, c_send, c_recv):
    grid = here.grid
    half = n // 2
    far = grid.z // 4

    def chunk(core, zz, start=0, count=n):
        return buf.at[pl.ds((core * grid.z + zz) * n + start, count)]

    def far_copy(k):
        block = chunk(here.c, here.z)
        return remote(block, block, far_send.at[k], far_recv.at[k], here.along_z(here.z_off(4 * k)))

    def far_arrival(k):
        block = chunk(here.c, here.z_off(-4 * k))
        return remote(block, block, far_send.at[k], far_recv.at[k], here.along_z(here.z_off(-4 * k)))

    ways = [(1, 0, n), (-1, 0, n), (-2, 0, half), (2, half, half)]

    def near_copy(k, way):
        by, start, count = ways[way]
        block = chunk(here.c, here.z_off(-4 * k), start, count)
        return remote(
            block, block, near_send.at[k, way], near_recv.at[k, way], here.along_z(here.z_off(by))
        )

    def near_arrival(k, way):
        by, start, count = ways[way]
        block = chunk(here.c, here.z_off(-by - 4 * k), start, count)
        return remote(
            block, block, near_send.at[k, way], near_recv.at[k, way], here.along_z(here.z_off(-by))
        )

    for k in sorted(range(1, far), key=lambda k: -min(k, far - k)):
        far_copy(k).start()
    for way in (2, 3, 0, 1):
        near_copy(0, way).start()
    yield
    for k in range(1, far):
        far_arrival(k).wait_recv()
        for way in (2, 3, 0, 1):
            near_copy(k, way).start()
    yield
    for k in range(far):
        for way in range(4):
            near_arrival(k, way).wait_recv()
    line = buf.at[pl.ds(here.c * grid.z * n, grid.z * n)]
    swap = remote(line, line, c_send.at[0], c_recv.at[0], here.other_core())
    swap.start()
    yield
    line = buf.at[pl.ds((1 - here.c) * grid.z * n, grid.z * n)]
    remote(line, line, c_send.at[0], c_recv.at[0], here.other_core()).wait_recv()
    yield
    swap.wait_send()
    for k in range(far):
        if k:
            far_copy(k).wait_send()
        for way in range(4):
            near_copy(k, way).wait_send()
    yield


def exchange(n, me, device, put, take, send, recv):
    def copy(to):
        return remote(put(to), take(me), send.at[to], recv.at[me], device(to))

    def arrival(slot):
        return remote(put(slot), take(slot), send.at[slot], recv.at[slot], device(slot))

    for i in sorted(range(1, n), key=lambda i: -min(i, n - i)):
        copy((me + i) % n).start()
    yield
    for i in range(1, n):
        arrival((me + i) % n).wait_recv()
    yield
    for i in range(1, n):
        copy((me + i) % n).wait_send()
    yield


def add_up(ref, n):
    total = ref[0]
    for i in range(1, n):
        total = total + ref[i]
    return total


def gram_scratch(grid, rank):
    shape = (rank // grid.x // 2, 2 * rank)
    counts = [grid.x, grid.y * grid.c, grid.z, grid.x]
    buffers = [pltpu.VMEM((n,) + shape, F32) for n in [grid.x] + counts]
    return buffers + [sems(n) for n in counts for _ in range(2)] + [pltpu.VMEM((rank, 2 * rank), F32)]


def gram_steps(here, block, blocks, row_count, scratch):
    grid = here.grid
    part, first, second, third, whole = scratch[:5]
    pairs = [scratch[5 + 2 * i : 7 + 2 * i] for i in range(4)]
    work = scratch[-1]
    total = None
    for i in range(blocks):
        value = block(i)
        one = lax.dot_general(
            value, value, (((1,), (1,)), ((), ())), precision=HIGHEST, preferred_element_type=F32
        )
        total = one if total is None else total + one
    k = total.shape[0]
    rows = k // grid.x
    low = rows // 2
    for p in range(grid.x):
        part[p] = jnp.concatenate(
            [total[p * rows : p * rows + low], total[p * rows + low : (p + 1) * rows]], axis=1
        )
    x, z = here.x, here.z
    group = here.y * grid.c + here.c
    first[x] = part[x]
    ends = []

    def run(n, me, device, put, ref, pair):
        steps = exchange(n, me, device, put, lambda slot: ref.at[slot], *pair)
        next(steps)
        ends.append(steps)
        return steps

    steps = run(grid.x, x, here.along_x, lambda to: part.at[to], first, pairs[0])
    yield
    next(steps)
    second[group] = add_up(first, grid.x)
    mine = second.at[group]
    steps = run(grid.y * grid.c, group, here.along_yc, lambda to, mine=mine: mine, second, pairs[1])
    yield
    next(steps)
    third[z] = add_up(second, grid.y * grid.c)
    mine = third.at[z]
    steps = run(grid.z, z, here.along_z, lambda to, mine=mine: mine, third, pairs[2])
    yield
    next(steps)
    whole[x] = add_up(third, grid.z)
    mine = whole.at[x]
    steps = run(grid.x, x, here.along_x, lambda to, mine=mine: mine, whole, pairs[3])
    yield
    next(steps)
    row = lax.broadcasted_iota(jnp.int32, (low, k), 0)
    lane = lax.broadcasted_iota(jnp.int32, (low, k), 1)
    for p in range(grid.x):
        for h in range(2):
            at = p * rows + h * low
            unit = jnp.where(row + at == lane, 1.0, 0.0).astype(F32)
            value = whole[p][:, h * k : (h + 1) * k] * (1.0 / row_count)
            work[at : at + low, :] = jnp.concatenate([value, unit], axis=1)
    for steps in ends:
        next(steps)
    yield
    row = lax.broadcasted_iota(jnp.int32, (k, 2 * k), 0)
    lane = lax.broadcasted_iota(jnp.int32, (k, 2 * k), 1)

    eliminate(work)
    value = work[...]
    diagonal = jnp.sum(jnp.where(lane == row, value, 0.0), axis=1, keepdims=True)
    work[...] = value * lax.rsqrt(diagonal)
    yield


def eliminate(work, width=4):
    k = work.shape[0]
    row = lax.broadcasted_iota(jnp.int32, (k, 1), 0)
    lane = lax.broadcasted_iota(jnp.int32, work.shape, 1)

    def lane_sum(value, at):
        return jnp.sum(jnp.where(lane[: value.shape[0]] == at, value, 0.0), axis=1, keepdims=True)

    @pl.loop(0, k // width)
    def _(i):
        at = i * width
        value = work[...]
        rows = [work[pl.ds(at + a, 1), :] for a in range(width)]
        columns = [lane_sum(value, at + a) for a in range(width)]
        block = [[lane_sum(rows[a], at + b) for b in range(width)] for a in range(width)]
        for a in range(width):
            inverse = 1.0 / block[a][a]
            left = columns[a] * inverse
            for b in range(a + 1, width):
                factor = block[a][b] * inverse
                rows[b] = rows[b] - factor * rows[a]
                columns[b] = columns[b] - left * block[a][b]
                for d in range(b, width):
                    block[b][d] = block[b][d] - factor * block[a][d]
            value = value - jnp.where(row > at + a, left, 0.0) * rows[a]
        work[...] = value


def apply_inverse(work, value, first=0):
    k = work.shape[0]
    rows = work[first:, k:] if first else work[: value.shape[0], k : k + value.shape[0]]
    return jnp.dot(rows, value, precision=HIGHEST, preferred_element_type=F32)


def slots_of(grid, value):
    return value // (grid.z * grid.c), (value // grid.c) % grid.z, value % grid.c


def work_out_tables(here, tiles, notes, serves, column_table, item_table):
    grid = here.grid
    group = grid.c * grid.y
    n = group * tiles
    owners = grid.c * grid.z * grid.y
    side = notes.shape[2]

    @pl.loop(0, owners)
    def _(i):
        serves[pl.ds(i, 1), :] = notes[i][2:3].astype(F32)

    row = lax.broadcasted_iota(jnp.int32, (n, side), 0)
    lane = lax.broadcasted_iota(jnp.int32, (n, side), 1)
    tile, member = row % tiles, row // tiles
    asked = []
    for core in range(grid.c):
        for y in range(grid.y):
            line = notes[(core * grid.z + here.z) * grid.y + y][3:4].astype(F32)
            asked.append(jnp.broadcast_to(line, (tiles, side)))
    asked = jnp.concatenate(asked, axis=0)

    def column(value):
        return jnp.sum(value, axis=1, keepdims=True)

    slot = column(jnp.where(lane == tile, asked, 0.0)).astype(jnp.int32)
    sy, sz, sc = slots_of(grid, slot)
    where = (sc * grid.z + sz) * grid.y + sy
    hot = jnp.where(lane == where, 1.0, 0.0).astype(BF)[:, :owners]
    served = jnp.dot(hot, serves[...].astype(BF), preferred_element_type=F32)
    asker = ((member % grid.y) * grid.z + here.z) * grid.c + member // grid.y
    pick = column(jnp.where(lane == asker, served, 0.0)).astype(jnp.int32)
    line_at = (sc * grid.z + sz) * 2 + pick
    ask = jnp.where(sy == here.y, line_at, 0)
    ids = where * 2 + pick
    across = jnp.broadcast_to(ids.astype(F32), (n, side)).T.astype(jnp.int32)[:n]
    square_lane, square_row = lane[:, :n], row[:, :n]
    same = (across == ids) & (square_lane // tiles == square_row // tiles) & (square_lane < square_row)
    before = jnp.max(jnp.where(same, square_lane % tiles + 1, 0).astype(F32), axis=1, keepdims=True)
    columns = jnp.where(
        lane == 0, ask.astype(F32), jnp.where(lane == 1, pick.astype(F32), jnp.where(lane == 2, before, 0.0))
    )
    column_table[...] = columns.T[:8].astype(jnp.int32)
    mine = jnp.where((sy == here.y) & (sc == here.c), sz * 2 + pick, -1)
    number = jnp.where(mine == lane, tile + 1, 0).astype(F32)
    for g in range(group):
        last = jnp.max(number[g * tiles : (g + 1) * tiles], axis=0, keepdims=True)
        item_table[g : g + 1, :] = last.astype(jnp.int32) + g * (tiles + 1)


def within(at, ref):
    return jnp.minimum(jnp.maximum(at, 0), ref.shape[0] - 1)


def unpack_masks(observed, masks):
    side = masks.shape[1]

    @pl.loop(0, masks.shape[0])
    def _(t):
        words = observed[t]
        spread = jnp.broadcast_to(words[:, None, :], (words.shape[0], 8, side)).reshape(side, side)
        shift = lax.broadcasted_iota(jnp.int32, (side, side), 0) % 8
        masks[t] = ((spread >> shift) & 1).astype(F32).T.astype(BF)


def residual_tiles(tables, own, query, notes, users, ratings, masks, out, out_t):
    tiles = ratings.shape[0]

    @pl.loop(0, tiles, unroll=8)
    def _(t):
        meta = notes[tables.note_at[t]].astype(F32)
        line = lax.broadcasted_iota(jnp.int32, meta.shape, 0)
        pick = tables.column[1, own * tiles + t]
        weight = jnp.sum(jnp.where(line == pick, meta, 0.0), axis=0, keepdims=True)
        items = jnp.concatenate([part[tables.query_at[t]] for part in query], axis=0)
        guess = lax.dot_general(
            users[tables.user_at[t]], items, (((0,), (0,)), ((), ())), preferred_element_type=F32
        )
        value = masks[t].astype(F32) * weight * (ratings[t].astype(F32) - guess)
        out[t] = value.astype(BF)
        out_t[t] = value.T.astype(BF)


def main_kernel(grid, counts, tree, *refs):
    refs = list(refs)
    tables = Names()
    tables.user_at, tables.query_at, tables.note_at, tables.user_before, tables.user_last = (
        refs.pop(0) for _ in range(5)
    )
    facts, item_start, user_start, ratings_far, observed_far, user_out, item_out = (refs.pop(0) for _ in range(7))
    scratch = named(jax.tree.unflatten(tree, refs))
    here = Here(grid)
    ratings, observed = scratch.ratings, scratch.observed
    loads = [
        pltpu.make_async_copy(observed_far, observed, scratch.load_sem.at[0]),
        pltpu.make_async_copy(ratings_far, ratings, scratch.load_sem.at[1]),
    ]
    for load in loads:
        load.start()
    tiles, side = ratings.shape[:2]
    per = user_out.shape[1] // side
    rank = user_out.shape[0]
    x, y, z, c = here.x, here.y, here.z, here.c
    half = rank // 2
    res, res_t = scratch.res, scratch.res_t
    near_rows = tiles + 1
    far = grid.z // 4

    line, notes, users = scratch.line, scratch.notes, scratch.users
    ends = []
    greeting = here.greet()
    next(greeting)

    for b in range(2):
        line[(c * grid.z + z) * 2 + b] = item_start[:, b * side : (b + 1) * side]
    for j in range(per):
        users[x * per + j] = user_start[:, j * side : (j + 1) * side]
    facts_f = facts[...].astype(F32)
    weight = (LEVELS + 1.0) / (facts_f + 1.0)
    facts_row = lax.broadcasted_iota(jnp.int32, facts.shape, 0)
    note_at = (c * grid.z + z) * grid.y + y
    first_rows = jnp.where(facts_row < 2, weight, facts_f)
    notes[note_at] = jnp.concatenate([first_rows, jnp.zeros_like(first_rows)], axis=0).astype(BF)
    for h in range(2):
        scratch.sums[h][0] = jnp.zeros((half, side), F32)
        for it in range(ITERS):
            near = scratch.half[it][h].near
            for s in range(grid.c * grid.y):
                near[s * near_rows] = jnp.zeros((half, side), BF)
    for load in loads:
        load.wait()
    unpack_masks(observed, scratch.masks)
    next(greeting)
    mine = notes.at[note_at]
    note_y = exchange(
        grid.y,
        y,
        here.along_y,
        lambda to: mine,
        lambda slot: notes.at[(c * grid.z + z) * grid.y + slot],
        *scratch.note_y,
    )
    items = spread_z(here, line, 2, *scratch.line_z)
    people = spread_x(here, users, per, *scratch.users_x)
    note_z = spread_z(here, notes, grid.y, *scratch.note_z)
    next(note_y)
    next(items)
    next(people)
    next(note_y)
    next(note_z)
    next(note_z)
    next(items)
    next(note_z)
    next(items)
    next(note_z)
    work_out_tables(here, tiles, notes, scratch.serves, scratch.column_v, scratch.item_v)
    copies = [
        pltpu.make_async_copy(scratch.column_v, scratch.column_s, scratch.table_sem.at[0]),
        pltpu.make_async_copy(scratch.item_v, scratch.item_s, scratch.table_sem.at[1]),
    ]
    for copy in copies:
        copy.start()
    for copy in copies:
        copy.wait()
    tables.column = scratch.column_s
    own = c * grid.y + y
    next(items)
    next(people)
    ends += [note_y, items, people, note_z]

    def chain(h):
        rows = slice(h * half, (h + 1) * half)
        sums = scratch.sums[h]
        for it in range(ITERS):
            mine, low = scratch.half[it][h], scratch.half[it][0]
            sel, query, stage_x, got_x, pre_u, raw_u = (
                mine.sel,
                mine.query,
                mine.stage_x,
                mine.got_x,
                mine.pre_u,
                mine.raw_u,
            )
            new_users, near, stage, got, fars, got_far, pre_i, raw_i = (
                mine.users,
                mine.near,
                mine.stage,
                mine.got,
                mine.fars,
                mine.got_far,
                mine.pre_i,
                mine.raw_i,
            )
            for i in range(grid.y):
                to = (y + i) % grid.y

                @pl.loop(0, tiles, unroll=8)
                def _(t):
                    at = tables.column[0, (c * grid.y + to) * tiles + t]
                    if it:
                        block = scratch.lines[h][within(at, line)]
                    else:
                        block = line[within(at, line)][rows]
                    sel[to * tiles + t] = block

            asked = exchange(
                grid.y,
                y,
                here.along_y,
                lambda to, sel=sel: sel.at[pl.ds(to * tiles, tiles)],
                lambda slot, query=query: query.at[pl.ds(slot * tiles, tiles)],
                *mine.ysel,
            )
            next(asked)
            query[pl.ds(y * tiles, tiles)] = sel[pl.ds(y * tiles, tiles)]
            yield
            next(asked)
            ends.append(asked)
            if it == 0:
                yield

            @pl.loop(0, tiles, unroll=8)
            def _(t):
                product = jnp.dot(query[tables.query_at[t]], res_t[t], preferred_element_type=F32)
                sums[t + 1] = product + sums[tables.user_before[t]]

            for i in range(1, grid.x + 1):
                to = (x + i) % grid.x

                @pl.loop(0, per, unroll=4)
                def _(j):
                    total = sums[tables.user_last[to * per + j]]
                    if i < grid.x:
                        stage_x[to * per + j] = total.astype(BF)
                    else:
                        pre_u[j] = total

            parts = exchange(
                grid.x,
                x,
                here.along_x,
                lambda to, stage_x=stage_x: stage_x.at[pl.ds(to * per, per)],
                lambda slot, got_x=got_x: got_x.at[pl.ds(slot * per, per)],
                *mine.xsum,
            )
            next(parts)
            yield
            next(parts)
            ends.append(parts)

            @pl.loop(0, per, unroll=4)
            def _(j):
                total = pre_u[j]
                for i in range(1, grid.x):
                    total = total + got_x[((x + i) % grid.x) * per + j].astype(F32)
                if it:
                    pre_u[j] = total
                    work = scratch.gram_item[it - 1][-1]
                    if h:
                        total = apply_inverse(
                            work, jnp.concatenate([low.pre_u[j], total], axis=0), half
                        )
                    else:
                        total = apply_inverse(work, total)
                raw_u[j] = total
                new_users[x * per + j] = total.astype(BF)

            people = spread_x(here, new_users, per, *mine.xall)
            next(people)
            yield
            next(people)
            ends.append(people)

            @pl.loop(0, tiles, unroll=8)
            def _(t):
                product = jnp.dot(new_users[tables.user_at[t]], res[t], preferred_element_type=F32)
                total = product + sums[within(tables.column[2, own * tiles + t], sums)]
                sums[t + 1] = total
                near[own * near_rows + 1 + t] = total.astype(BF)

            def rows_of(core, slot, near=near):
                return near.at[pl.ds((core * grid.y + slot) * near_rows + 1, tiles)]

            along = exchange(
                grid.y, y, here.along_y, lambda to, f=rows_of: f(c, y), lambda slot, f=rows_of: f(c, slot), *mine.ynear
            )
            next(along)
            c_send, c_recv = mine.cnear

            def c_copy(core, slot):
                block = rows_of(core, slot)
                return remote(block, block, c_send.at[slot], c_recv.at[slot], here.other_core())

            c_copy(c, y).start()
            yield
            next(along)
            ends.append(along)
            for i in range(1, grid.y):
                c_copy(c, (y + i) % grid.y).start()
            yield
            for i in range(grid.y):
                c_copy(1 - c, (y + i) % grid.y).wait_recv()

            def gathered(zz, b):
                total = None
                for s in range(grid.c * grid.y):
                    at = scratch.item_s[s, zz * 2 + b]
                    value = near[within(at, near)].astype(F32)
                    total = value if total is None else total + value
                return total

            z_send, z_recv = mine.znear
            ways = [(1, (0, 1)), (-1, (0, 1)), (-2, (0,)), (2, (1,))]
            starts = [0, 2 * far, 4 * far, 5 * far]

            def near_z(way, arrival=False):
                by, parts_ = ways[way]
                count = len(parts_) * far
                to = here.along_z(here.z_off(-by if arrival else by))
                return remote(
                    stage.at[pl.ds(starts[way], count)],
                    got.at[pl.ds(starts[way], count)],
                    z_send.at[way],
                    z_recv.at[way],
                    to,
                )

            for way in (3, 2, 1, 0):
                by, parts_ = ways[way]

                @pl.loop(0, far)
                def _(k):
                    for j, b in enumerate(parts_):
                        zz = here.z_off(by + 4 * k)
                        stage[starts[way] + len(parts_) * k + j] = gathered(zz, b).astype(BF)

                near_z(way).start()

            @pl.loop(0, far)
            def _(k):
                for b in range(2):
                    fars[2 * k + b] = gathered(here.z_off(4 * k), b)

            yield
            for way in range(4):
                near_z(way, True).wait_recv()
            f_send, f_recv = mine.zfar
            far_stage = mine.far_stage

            def far_copy(k):
                return remote(
                    far_stage.at[pl.ds(2 * k, 2)],
                    got_far.at[pl.ds(2 * k, 2)],
                    f_send.at[k],
                    f_recv.at[k],
                    here.along_z(here.z_off(4 * k)),
                )

            for k in sorted(range(1, far), key=lambda k: -min(k, far - k)) + [0]:
                for b in range(2):
                    total = (
                        fars[2 * k + b]
                        + got[starts[0] + 2 * k + b].astype(F32)
                        + got[starts[1] + 2 * k + b].astype(F32)
                        + got[starts[2 + b] + k].astype(F32)
                    )
                    if k:
                        far_stage[2 * k + b] = total.astype(BF)
                    else:
                        pre_i[b] = total
                if k:
                    far_copy(k).start()
            yield
            for k in range(1, far):
                far_copy(k).wait_recv()
            work = scratch.gram_user[it][-1]
            for b in range(2):
                total = pre_i[b]
                for k in range(1, far):
                    total = total + got_far[2 * k + b].astype(F32)
                pre_i[b] = total
                if h:
                    raw_i[b] = apply_inverse(
                        work, jnp.concatenate([low.pre_i[b], total], axis=0), half
                    )
                else:
                    raw_i[b] = apply_inverse(work, total)
            if it + 1 < ITERS:
                next_line = scratch.lines[h]
                for b in range(2):
                    next_line[(c * grid.z + z) * 2 + b] = raw_i[b].astype(BF)
                items = spread_z(here, next_line, 2, *mine.zall)
                ends.append(items)
                for _ in range(3):
                    next(items)
                    yield
                next(items)
            for i in range(grid.y):
                c_copy(c, (y + i) % grid.y).wait_send()
            for way in range(4):
                near_z(way).wait_send()
            for k in range(1, far):
                far_copy(k).wait_send()
        yield

    def whole_of(low, high):
        return lambda i: jnp.concatenate([low[i], high[i]], axis=0)

    chains = [chain(0), chain(1)]

    def step():
        for one in chains:
            next(one)

    gram_item = None
    for it in range(ITERS):
        if it == 0:
            step()
            step()
            query = [one.query for one in scratch.half[0]]
            residual_tiles(tables, own, query, notes, users, ratings, scratch.masks, res, res_t)
            step()
        else:
            step()
            next(gram_item)
            step()
            next(gram_item)
            next(gram_item)
        step()
        gram_user = gram_steps(here, whole_of(*(one.raw_u for one in scratch.half[it])), per, counts[0], scratch.gram_user[it])
        next(gram_user)
        step()
        next(gram_user)
        step()
        next(gram_user)
        step()
        next(gram_user)
        step()
        next(gram_user)
        next(gram_user)
        step()
        gram_item = gram_steps(here, whole_of(*(one.raw_i for one in scratch.half[it])), 2, counts[1], scratch.gram_item[it])
        next(gram_item)
        if it + 1 < ITERS:
            step()
            next(gram_item)
            step()
            next(gram_item)
    users_of = whole_of(*(one.raw_u for one in scratch.half[-1]))
    items_of = whole_of(*(one.raw_i for one in scratch.half[-1]))
    for j in range(per):
        user_out[:, j * side : (j + 1) * side] = apply_inverse(
            scratch.gram_user[ITERS - 1][-1], users_of(j)
        ).astype(BF)
    for _ in range(5):
        next(gram_item)
    for b in range(2):
        item_out[:, b * side : (b + 1) * side] = apply_inverse(
            scratch.gram_item[ITERS - 1][-1], items_of(b)
        ).astype(BF)
    for steps in ends:
        next(steps)


def main_scratch(grid, rank, side, tiles, per):
    far = grid.z // 4
    asked = grid.c * grid.y * tiles

    def vmem(n, kind=BF, rows=rank // 2):
        return pltpu.VMEM((n, rows, side), kind)

    def pair(n):
        return [sems(n), sems(n)]

    def half():
        return dict(
            sel=vmem(grid.y * tiles),
            query=vmem(grid.y * tiles),
            stage_x=vmem(grid.x * per),
            got_x=vmem(grid.x * per),
            pre_u=vmem(per, F32),
            raw_u=vmem(per, F32),
            users=vmem(grid.x * per),
            near=vmem(grid.c * grid.y * (tiles + 1)),
            stage=vmem(6 * far),
            got=vmem(6 * far),
            fars=vmem(2 * far, F32),
            far_stage=vmem(2 * far),
            got_far=vmem(2 * far),
            pre_i=vmem(2, F32),
            raw_i=vmem(2, F32),
            ysel=pair(grid.y),
            xsum=pair(grid.x),
            xall=pair(grid.x),
            ynear=pair(grid.y),
            cnear=pair(grid.y),
            znear=pair(4),
            zfar=pair(far),
            zall=spread_z_sems(grid),
        )

    return dict(
        ratings=pltpu.VMEM((tiles, side, side), BF),
        observed=pltpu.VMEM((tiles, side // 8, side), jnp.int32),
        load_sem=sems(2),
        res=pltpu.VMEM((tiles, side, side), BF),
        res_t=pltpu.VMEM((tiles, side, side), BF),
        sums=[vmem(tiles + 1, F32) for _ in range(2)],
        line=vmem(2 * grid.z * 2, BF, rank),
        lines=[vmem(2 * grid.z * 2) for _ in range(2)],
        users=vmem(grid.x * per, BF, rank),
        notes=pltpu.VMEM((2 * grid.z * grid.y, 16, side), BF),
        masks=pltpu.VMEM((tiles, side, side), BF),
        serves=pltpu.VMEM((2 * grid.z * grid.y, side), F32),
        column_v=pltpu.VMEM((8, asked), jnp.int32),
        column_s=pltpu.SMEM((8, asked), jnp.int32),
        item_v=pltpu.VMEM((grid.c * grid.y, side), jnp.int32),
        item_s=pltpu.SMEM((grid.c * grid.y, side), jnp.int32),
        table_sem=sems(2),
        note_y=pair(grid.y),
        users_x=pair(grid.x),
        line_z=spread_z_sems(grid),
        note_z=spread_z_sems(grid),
        half=[[half() for _ in range(2)] for _ in range(ITERS)],
        gram_user=[gram_scratch(grid, rank) for _ in range(ITERS)],
        gram_item=[gram_scratch(grid, rank) for _ in range(ITERS)],
    )


def main_call(grid, counts, tables, facts, item_start, user_start, ratings, observed):
    tiles, side = ratings.shape[:2]
    rank = item_start.shape[0]
    per = user_start.shape[1] // side
    scratch, tree = jax.tree.flatten(main_scratch(grid, rank, side, tiles, per))
    return pl.pallas_call(
        functools.partial(main_kernel, grid, counts, tree),
        out_shape=(
            jax.ShapeDtypeStruct((rank, per * side), BF),
            jax.ShapeDtypeStruct((rank, 2 * side), BF),
        ),
        in_specs=[pl.BlockSpec(memory_space=pltpu.SMEM)] * len(tables)
        + [pl.BlockSpec(memory_space=pltpu.VMEM)] * 3
        + [pl.BlockSpec(memory_space=pltpu.HBM)] * 2,
        out_specs=(pl.BlockSpec(memory_space=pltpu.VMEM),) * 2,
        scratch_shapes=scratch,
        compiler_params=pltpu.CompilerParams(
            collective_id=1, has_side_effects=True, vmem_limit_bytes=VMEM_LIMIT
        ),
    )(*tables, facts, item_start, user_start, ratings, observed)


def links(ids):
    at = jnp.arange(ids.shape[0], dtype=jnp.int32)
    same = (ids[:, None] == ids[None, :]) & (at[None, :] < at[:, None])
    return jnp.max(jnp.where(same, at[None, :] + 1, 0), axis=1)


def lasts(ids, n):
    tiles = ids.shape[-1]
    same = ids[..., None, :] == jnp.arange(n, dtype=jnp.int32)[:, None]
    return jnp.max(jnp.where(same, jnp.arange(1, tiles + 1, dtype=jnp.int32), 0), axis=-1)


def local(grid, ratings, observed, user_start, item_start, exposure, serve_list, tile_slot, tile_user):
    side = ratings.shape[2]
    own_users = user_start.shape[1]
    tiles = ratings.shape[0]
    owners = grid.y * grid.z * grid.c
    counts = (own_users * owners * grid.x * 1.0, item_start.shape[1] * owners * grid.x * 1.0)
    per = own_users // side
    sy, sz, sc = slots_of(grid, tile_slot)
    tables = (
        tile_user,
        sy * tiles + jnp.arange(tiles, dtype=jnp.int32),
        (sc * grid.z + sz) * grid.y + sy,
        links(tile_user),
        lasts(tile_user, grid.x * per),
    )
    rows = [exposure, jnp.pad(serve_list, (0, side - owners)), jnp.pad(tile_slot, (0, side - tiles))]
    facts = jnp.concatenate(rows + [jnp.zeros((4 * side,), jnp.int32)]).reshape(8, side)
    return main_call(grid, counts, tables, facts, item_start, user_start, ratings, observed)


def solution(mesh):
    grid = Grid(mesh.shape["rows"], mesh.shape["rep"])
    both = P(("rows", "rep"))
    second = P(None, ("rows", "rep"))
    return jax.shard_map(
        functools.partial(local, grid),
        mesh=mesh,
        in_specs=(both, both, second, second, both, both, both, both),
        out_specs=(second, second),
        check_vma=False,
    )
```

```python
import functools

import jax
import jax.numpy as jnp
from jax import lax
from jax.experimental import pallas as pl
from jax.experimental.pallas import tpu as pltpu
from jax.sharding import PartitionSpec as P

LEVELS = 16
ITERS = 2
MESH = pl.DeviceIdType.MESH
BF = jnp.bfloat16
F32 = jnp.float32
HIGHEST = lax.Precision.HIGHEST
VMEM_LIMIT = 48 * 1024 * 1024


class Grid:
    def __init__(self, rows, rep):
        self.c = 2
        self.x = rep
        self.y = 4
        self.z = rows // (self.c * self.y)


class Names:
    def __init__(self, **named):
        self.__dict__.update(named)


def named(tree):
    if isinstance(tree, dict):
        return Names(**{key: named(value) for key, value in tree.items()})
    return [named(value) for value in tree] if isinstance(tree, (list, tuple)) else tree


class Here:
    def __init__(self, grid):
        r = lax.axis_index("rows")
        self.grid = grid
        self.r = r
        self.x = lax.axis_index("rep")
        self.y = r // (grid.z * grid.c)
        self.z = (r // grid.c) % grid.z
        self.c = r % grid.c

    def along_x(self, to):
        return self.r, to

    def along_y(self, to):
        return (to * self.grid.z + self.z) * self.grid.c + self.c, self.x

    def along_z(self, to):
        return (self.y * self.grid.z + to) * self.grid.c + self.c, self.x

    def along_yc(self, to):
        y, c = to // self.grid.c, to % self.grid.c
        return (y * self.grid.z + self.z) * self.grid.c + c, self.x

    def other_core(self):
        return (self.y * self.grid.z + self.z) * self.grid.c + 1 - self.c, self.x

    def z_off(self, by):
        return (self.z + by + 2 * self.grid.z) % self.grid.z

    def greet(self):
        grid = self.grid
        targets = [self.along_x((self.x + i) % grid.x) for i in range(1, grid.x)]
        for i in range(grid.y):
            for j in range(grid.c):
                if i or j:
                    to = ((self.y + i) % grid.y) * grid.c + (self.c + j) % 2
                    targets.append(self.along_yc(to))
        targets += [self.along_z(self.z_off(o)) for o in range(1, grid.z)]
        barrier = pltpu.get_barrier_semaphore()
        for target in targets:
            pl.semaphore_signal(barrier, inc=1, device_id=target, device_id_type=MESH)
        yield
        pl.semaphore_wait(barrier, len(targets))
        yield


def remote(src, dst, send_sem, recv_sem, device):
    return pltpu.make_async_remote_copy(
        src_ref=src,
        dst_ref=dst,
        send_sem=send_sem,
        recv_sem=recv_sem,
        device_id=device,
        device_id_type=MESH,
    )


def sems(*shape):
    return pltpu.SemaphoreType.DMA(shape)


def spread_x(here, buf, per, send, recv):
    n = here.grid.x

    def copy(to, slot):
        block = buf.at[pl.ds(slot * per, per)]
        return remote(block, block, send.at[to], recv.at[slot], here.along_x(to))

    for i in sorted(range(1, n), key=lambda i: -min(i, n - i)):
        copy((here.x + i) % n, here.x).start()
    yield
    for i in range(1, n):
        copy((here.x + i) % n, (here.x + i) % n).wait_recv()
    yield
    for i in range(1, n):
        copy((here.x + i) % n, here.x).wait_send()
    yield


def spread_z_sems(grid):
    far = grid.z // 4
    return [sems(far), sems(far), sems(far, 4), sems(far, 4), sems(1), sems(1)]


def spread_z(here, buf, n, far_send, far_recv, near_send, near_recv, c_send, c_recv):
    grid = here.grid
    half = n // 2
    far = grid.z // 4

    def chunk(core, zz, start=0, count=n):
        return buf.at[pl.ds((core * grid.z + zz) * n + start, count)]

    def far_copy(k):
        block = chunk(here.c, here.z)
        return remote(block, block, far_send.at[k], far_recv.at[k], here.along_z(here.z_off(4 * k)))

    def far_arrival(k):
        block = chunk(here.c, here.z_off(-4 * k))
        return remote(block, block, far_send.at[k], far_recv.at[k], here.along_z(here.z_off(-4 * k)))

    ways = [(1, 0, n), (-1, 0, n), (-2, 0, half), (2, half, half)]

    def near_copy(k, way):
        by, start, count = ways[way]
        block = chunk(here.c, here.z_off(-4 * k), start, count)
        return remote(
            block, block, near_send.at[k, way], near_recv.at[k, way], here.along_z(here.z_off(by))
        )

    def near_arrival(k, way):
        by, start, count = ways[way]
        block = chunk(here.c, here.z_off(-by - 4 * k), start, count)
        return remote(
            block, block, near_send.at[k, way], near_recv.at[k, way], here.along_z(here.z_off(-by))
        )

    for k in sorted(range(1, far), key=lambda k: -min(k, far - k)):
        far_copy(k).start()
    for way in (2, 3, 0, 1):
        near_copy(0, way).start()
    yield
    for k in range(1, far):
        far_arrival(k).wait_recv()
        for way in (2, 3, 0, 1):
            near_copy(k, way).start()
    yield
    for k in range(far):
        for way in range(4):
            near_arrival(k, way).wait_recv()
    line = buf.at[pl.ds(here.c * grid.z * n, grid.z * n)]
    swap = remote(line, line, c_send.at[0], c_recv.at[0], here.other_core())
    swap.start()
    yield
    line = buf.at[pl.ds((1 - here.c) * grid.z * n, grid.z * n)]
    remote(line, line, c_send.at[0], c_recv.at[0], here.other_core()).wait_recv()
    yield
    swap.wait_send()
    for k in range(far):
        if k:
            far_copy(k).wait_send()
        for way in range(4):
            near_copy(k, way).wait_send()
    yield


def exchange(n, me, device, put, take, send, recv, prepare=None):
    def copy(to):
        return remote(put(to), take(me), send.at[to], recv.at[me], device(to))

    def arrival(slot):
        return remote(put(slot), take(slot), send.at[slot], recv.at[slot], device(slot))

    for i in sorted(range(1, n), key=lambda i: -min(i, n - i)):
        if prepare is not None:
            prepare((me + i) % n)
        copy((me + i) % n).start()
    yield
    for i in range(1, n):
        arrival((me + i) % n).wait_recv()
    yield
    for i in range(1, n):
        copy((me + i) % n).wait_send()
    yield


def add_up(ref, n):
    total = ref[0]
    for i in range(1, n):
        total = total + ref[i]
    return total


def gram_scratch(grid, rank):
    shape = (rank // grid.x // 2, 2 * rank)
    counts = [grid.x, grid.y * grid.c, grid.z, grid.x]
    buffers = [pltpu.VMEM((n,) + shape, F32) for n in [grid.x] + counts]
    return buffers + [sems(n) for n in counts for _ in range(2)] + [pltpu.VMEM((rank, 2 * rank), F32)]


def gram_steps(here, block, blocks, row_count, scratch):
    grid = here.grid
    part, first, second, third, whole = scratch[:5]
    pairs = [scratch[5 + 2 * i : 7 + 2 * i] for i in range(4)]
    work = scratch[-1]
    total = None
    for i in range(blocks):
        value = block(i)
        one = lax.dot_general(
            value, value, (((1,), (1,)), ((), ())), precision=HIGHEST, preferred_element_type=F32
        )
        total = one if total is None else total + one
    k = total.shape[0]
    rows = k // grid.x
    low = rows // 2
    for p in range(grid.x):
        part[p] = jnp.concatenate(
            [total[p * rows : p * rows + low], total[p * rows + low : (p + 1) * rows]], axis=1
        )
    x, z = here.x, here.z
    group = here.y * grid.c + here.c
    first[x] = part[x]
    ends = []

    def run(n, me, device, put, ref, pair):
        steps = exchange(n, me, device, put, lambda slot: ref.at[slot], *pair)
        next(steps)
        ends.append(steps)
        return steps

    steps = run(grid.x, x, here.along_x, lambda to: part.at[to], first, pairs[0])
    yield
    next(steps)
    second[group] = add_up(first, grid.x)
    mine = second.at[group]
    steps = run(grid.y * grid.c, group, here.along_yc, lambda to, mine=mine: mine, second, pairs[1])
    yield
    next(steps)
    third[z] = add_up(second, grid.y * grid.c)
    mine = third.at[z]
    steps = run(grid.z, z, here.along_z, lambda to, mine=mine: mine, third, pairs[2])
    yield
    next(steps)
    whole[x] = add_up(third, grid.z)
    mine = whole.at[x]
    steps = run(grid.x, x, here.along_x, lambda to, mine=mine: mine, whole, pairs[3])
    yield
    next(steps)
    row = lax.broadcasted_iota(jnp.int32, (low, k), 0)
    lane = lax.broadcasted_iota(jnp.int32, (low, k), 1)
    for p in range(grid.x):
        for h in range(2):
            at = p * rows + h * low
            unit = jnp.where(row + at == lane, 1.0, 0.0).astype(F32)
            value = whole[p][:, h * k : (h + 1) * k] * (1.0 / row_count)
            work[at : at + low, :] = jnp.concatenate([value, unit], axis=1)
    for steps in ends:
        next(steps)
    yield
    row = lax.broadcasted_iota(jnp.int32, (k, 2 * k), 0)
    lane = lax.broadcasted_iota(jnp.int32, (k, 2 * k), 1)

    eliminate(work)
    value = work[...]
    diagonal = jnp.sum(jnp.where(lane == row, value, 0.0), axis=1, keepdims=True)
    work[...] = value * lax.rsqrt(diagonal)
    yield


def eliminate(work, width=4):
    k = work.shape[0]
    row = lax.broadcasted_iota(jnp.int32, (k, 1), 0)
    lane = lax.broadcasted_iota(jnp.int32, work.shape, 1)

    def lane_sum(value, at):
        return jnp.sum(jnp.where(lane[: value.shape[0]] == at, value, 0.0), axis=1, keepdims=True)

    @pl.loop(0, k // width)
    def _(i):
        at = i * width
        value = work[...]
        rows = [work[pl.ds(at + a, 1), :] for a in range(width)]
        columns = [lane_sum(value, at + a) for a in range(width)]
        block = [[lane_sum(rows[a], at + b) for b in range(width)] for a in range(width)]
        for a in range(width):
            inverse = 1.0 / block[a][a]
            left = columns[a] * inverse
            for b in range(a + 1, width):
                factor = block[a][b] * inverse
                rows[b] = rows[b] - factor * rows[a]
                columns[b] = columns[b] - left * block[a][b]
                for d in range(b, width):
                    block[b][d] = block[b][d] - factor * block[a][d]
            value = value - jnp.where(row > at + a, left, 0.0) * rows[a]
        work[...] = value


def apply_inverse(work, value, first=0):
    k = work.shape[0]
    rows = work[first:, k:] if first else work[: value.shape[0], k : k + value.shape[0]]
    return jnp.dot(rows, value, precision=HIGHEST, preferred_element_type=F32)


def slots_of(grid, value):
    return value // (grid.z * grid.c), (value // grid.c) % grid.z, value % grid.c


def work_out_tables(here, tiles, notes, serves, column_table, item_table):
    grid = here.grid
    group = grid.c * grid.y
    n = group * tiles
    owners = grid.c * grid.z * grid.y
    side = notes.shape[2]

    @pl.loop(0, owners)
    def _(i):
        serves[pl.ds(i, 1), :] = notes[i][2:3].astype(F32)

    row = lax.broadcasted_iota(jnp.int32, (n, side), 0)
    lane = lax.broadcasted_iota(jnp.int32, (n, side), 1)
    tile, member = row % tiles, row // tiles
    asked = []
    for core in range(grid.c):
        for y in range(grid.y):
            line = notes[(core * grid.z + here.z) * grid.y + y][3:4].astype(F32)
            asked.append(jnp.broadcast_to(line, (tiles, side)))
    asked = jnp.concatenate(asked, axis=0)

    def column(value):
        return jnp.sum(value, axis=1, keepdims=True)

    slot = column(jnp.where(lane == tile, asked, 0.0)).astype(jnp.int32)
    sy, sz, sc = slots_of(grid, slot)
    where = (sc * grid.z + sz) * grid.y + sy
    hot = jnp.where(lane == where, 1.0, 0.0).astype(BF)[:, :owners]
    served = jnp.dot(hot, serves[...].astype(BF), preferred_element_type=F32)
    asker = ((member % grid.y) * grid.z + here.z) * grid.c + member // grid.y
    pick = column(jnp.where(lane == asker, served, 0.0)).astype(jnp.int32)
    line_at = (sc * grid.z + sz) * 2 + pick
    ask = jnp.where(sy == here.y, line_at, 0)
    ids = where * 2 + pick
    across = jnp.broadcast_to(ids.astype(F32), (n, side)).T.astype(jnp.int32)[:n]
    square_lane, square_row = lane[:, :n], row[:, :n]
    same = (across == ids) & (square_lane // tiles == square_row // tiles) & (square_lane < square_row)
    before = jnp.max(jnp.where(same, square_lane % tiles + 1, 0).astype(F32), axis=1, keepdims=True)
    columns = jnp.where(
        lane == 0, ask.astype(F32), jnp.where(lane == 1, pick.astype(F32), jnp.where(lane == 2, before, 0.0))
    )
    column_table[...] = columns.T[:8].astype(jnp.int32)
    mine = jnp.where((sy == here.y) & (sc == here.c), sz * 2 + pick, -1)
    number = jnp.where(mine == lane, tile + 1, 0).astype(F32)
    for g in range(group):
        last = jnp.max(number[g * tiles : (g + 1) * tiles], axis=0, keepdims=True)
        item_table[g : g + 1, :] = last.astype(jnp.int32) + g * (tiles + 1)


def within(at, ref):
    return jnp.minimum(jnp.maximum(at, 0), ref.shape[0] - 1)


def unpack_masks(observed, masks):
    side = masks.shape[1]

    @pl.loop(0, masks.shape[0])
    def _(t):
        words = observed[t]
        spread = jnp.broadcast_to(words[:, None, :], (words.shape[0], 8, side)).reshape(side, side)
        shift = lax.broadcasted_iota(jnp.int32, (side, side), 0) % 8
        masks[t] = ((spread >> shift) & 1).astype(F32).T.astype(BF)


def residual_tiles(tables, own, query, notes, users, ratings, masks, out, out_t):
    tiles = ratings.shape[0]

    @pl.loop(0, tiles, unroll=8)
    def _(t):
        meta = notes[tables.note_at[t]].astype(F32)
        line = lax.broadcasted_iota(jnp.int32, meta.shape, 0)
        pick = tables.column[1, own * tiles + t]
        weight = jnp.sum(jnp.where(line == pick, meta, 0.0), axis=0, keepdims=True)
        items = jnp.concatenate([part[tables.query_at[t]] for part in query], axis=0)
        guess = lax.dot_general(
            users[tables.user_at[t]], items, (((0,), (0,)), ((), ())), preferred_element_type=F32
        )
        value = masks[t].astype(F32) * weight * (ratings[t].astype(F32) - guess)
        out[t] = value.astype(BF)
        out_t[t] = value.T.astype(BF)


def main_kernel(grid, counts, tree, *refs):
    refs = list(refs)
    tables = Names()
    tables.user_at, tables.query_at, tables.note_at, tables.user_before, tables.user_last = (
        refs.pop(0) for _ in range(5)
    )
    facts, item_start, user_start, ratings_far, observed_far, user_out, item_out = (refs.pop(0) for _ in range(7))
    scratch = named(jax.tree.unflatten(tree, refs))
    here = Here(grid)
    ratings, observed = scratch.ratings, scratch.observed
    loads = [
        pltpu.make_async_copy(observed_far, observed, scratch.load_sem.at[0]),
        pltpu.make_async_copy(ratings_far, ratings, scratch.load_sem.at[1]),
    ]
    for load in loads:
        load.start()
    tiles, side = ratings.shape[:2]
    per = user_out.shape[1] // side
    rank = user_out.shape[0]
    x, y, z, c = here.x, here.y, here.z, here.c
    half = rank // 2
    res, res_t = scratch.res, scratch.res_t
    near_rows = tiles + 1
    far = grid.z // 4

    line, notes, users = scratch.line, scratch.notes, scratch.users
    ends = []
    greeting = here.greet()
    next(greeting)

    for b in range(2):
        line[(c * grid.z + z) * 2 + b] = item_start[:, b * side : (b + 1) * side]
    for j in range(per):
        users[x * per + j] = user_start[:, j * side : (j + 1) * side]
    facts_f = facts[...].astype(F32)
    weight = (LEVELS + 1.0) / (facts_f + 1.0)
    facts_row = lax.broadcasted_iota(jnp.int32, facts.shape, 0)
    note_at = (c * grid.z + z) * grid.y + y
    first_rows = jnp.where(facts_row < 2, weight, facts_f)
    notes[note_at] = jnp.concatenate([first_rows, jnp.zeros_like(first_rows)], axis=0).astype(BF)
    for h in range(2):
        scratch.sums[h][0] = jnp.zeros((half, side), F32)
        for it in range(ITERS):
            near = scratch.half[it][h].near
            for s in range(grid.c * grid.y):
                near[s * near_rows] = jnp.zeros((half, side), BF)
    for load in loads:
        load.wait()
    unpack_masks(observed, scratch.masks)
    next(greeting)
    mine = notes.at[note_at]
    note_y = exchange(
        grid.y,
        y,
        here.along_y,
        lambda to: mine,
        lambda slot: notes.at[(c * grid.z + z) * grid.y + slot],
        *scratch.note_y,
    )
    items = spread_z(here, line, 2, *scratch.line_z)
    people = spread_x(here, users, per, *scratch.users_x)
    note_z = spread_z(here, notes, grid.y, *scratch.note_z)
    next(note_y)
    next(items)
    next(people)
    next(note_y)
    next(note_z)
    next(note_z)
    next(items)
    next(note_z)
    next(items)
    next(note_z)
    work_out_tables(here, tiles, notes, scratch.serves, scratch.column_v, scratch.item_v)
    copies = [
        pltpu.make_async_copy(scratch.column_v, scratch.column_s, scratch.table_sem.at[0]),
        pltpu.make_async_copy(scratch.item_v, scratch.item_s, scratch.table_sem.at[1]),
    ]
    for copy in copies:
        copy.start()
    for copy in copies:
        copy.wait()
    tables.column = scratch.column_s
    own = c * grid.y + y
    next(items)
    next(people)
    ends += [note_y, items, people, note_z]

    def chain(h):
        rows = slice(h * half, (h + 1) * half)
        sums = scratch.sums[h]
        for it in range(ITERS):
            mine, low = scratch.half[it][h], scratch.half[it][0]
            sel, query, stage_x, got_x, pre_u, raw_u = (
                mine.sel,
                mine.query,
                mine.stage_x,
                mine.got_x,
                mine.pre_u,
                mine.raw_u,
            )
            new_users, near, stage, got, fars, got_far, pre_i, raw_i = (
                mine.users,
                mine.near,
                mine.stage,
                mine.got,
                mine.fars,
                mine.got_far,
                mine.pre_i,
                mine.raw_i,
            )
            def select(to, sel=sel):
                @pl.loop(0, tiles, unroll=8)
                def _(t):
                    at = tables.column[0, (c * grid.y + to) * tiles + t]
                    if it:
                        block = scratch.lines[h][within(at, line)]
                    else:
                        block = line[within(at, line)][rows]
                    sel[to * tiles + t] = block

            asked = exchange(
                grid.y,
                y,
                here.along_y,
                lambda to, sel=sel: sel.at[pl.ds(to * tiles, tiles)],
                lambda slot, query=query: query.at[pl.ds(slot * tiles, tiles)],
                *mine.ysel,
                prepare=select,
            )
            next(asked)
            select(y)
            query[pl.ds(y * tiles, tiles)] = sel[pl.ds(y * tiles, tiles)]
            yield
            next(asked)
            ends.append(asked)
            if it == 0:
                yield

            @pl.loop(0, tiles, unroll=8)
            def _(t):
                product = jnp.dot(query[tables.query_at[t]], res_t[t], preferred_element_type=F32)
                sums[t + 1] = product + sums[tables.user_before[t]]

            for i in range(1, grid.x + 1):
                to = (x + i) % grid.x

                @pl.loop(0, per, unroll=4)
                def _(j):
                    total = sums[tables.user_last[to * per + j]]
                    if i < grid.x:
                        stage_x[to * per + j] = total.astype(BF)
                    else:
                        pre_u[j] = total

            parts = exchange(
                grid.x,
                x,
                here.along_x,
                lambda to, stage_x=stage_x: stage_x.at[pl.ds(to * per, per)],
                lambda slot, got_x=got_x: got_x.at[pl.ds(slot * per, per)],
                *mine.xsum,
            )
            next(parts)
            yield
            next(parts)
            ends.append(parts)

            @pl.loop(0, per, unroll=4)
            def _(j):
                total = pre_u[j]
                for i in range(1, grid.x):
                    total = total + got_x[((x + i) % grid.x) * per + j].astype(F32)
                if it:
                    pre_u[j] = total
                    work = scratch.gram_item[it - 1][-1]
                    if h:
                        total = apply_inverse(
                            work, jnp.concatenate([low.pre_u[j], total], axis=0), half
                        )
                    else:
                        total = apply_inverse(work, total)
                raw_u[j] = total
                new_users[x * per + j] = total.astype(BF)

            people = spread_x(here, new_users, per, *mine.xall)
            next(people)
            yield
            next(people)
            ends.append(people)

            @pl.loop(0, tiles, unroll=8)
            def _(t):
                product = jnp.dot(new_users[tables.user_at[t]], res[t], preferred_element_type=F32)
                total = product + sums[within(tables.column[2, own * tiles + t], sums)]
                sums[t + 1] = total
                near[own * near_rows + 1 + t] = total.astype(BF)

            def rows_of(core, slot, near=near):
                return near.at[pl.ds((core * grid.y + slot) * near_rows + 1, tiles)]

            along = exchange(
                grid.y, y, here.along_y, lambda to, f=rows_of: f(c, y), lambda slot, f=rows_of: f(c, slot), *mine.ynear
            )
            next(along)
            c_send, c_recv = mine.cnear

            def c_copy(core, slot):
                block = rows_of(core, slot)
                return remote(block, block, c_send.at[slot], c_recv.at[slot], here.other_core())

            c_copy(c, y).start()
            yield
            next(along)
            ends.append(along)
            for i in range(1, grid.y):
                c_copy(c, (y + i) % grid.y).start()
            yield
            for i in range(grid.y):
                c_copy(1 - c, (y + i) % grid.y).wait_recv()

            def gathered(zz, b):
                total = None
                for s in range(grid.c * grid.y):
                    at = scratch.item_s[s, zz * 2 + b]
                    value = near[within(at, near)].astype(F32)
                    total = value if total is None else total + value
                return total

            z_send, z_recv = mine.znear
            ways = [(1, (0, 1)), (-1, (0, 1)), (-2, (0,)), (2, (1,))]
            starts = [0, 2 * far, 4 * far, 5 * far]

            def near_z(way, arrival=False):
                by, parts_ = ways[way]
                count = len(parts_) * far
                to = here.along_z(here.z_off(-by if arrival else by))
                return remote(
                    stage.at[pl.ds(starts[way], count)],
                    got.at[pl.ds(starts[way], count)],
                    z_send.at[way],
                    z_recv.at[way],
                    to,
                )

            for way in (3, 2, 1, 0):
                by, parts_ = ways[way]

                @pl.loop(0, far)
                def _(k):
                    for j, b in enumerate(parts_):
                        zz = here.z_off(by + 4 * k)
                        stage[starts[way] + len(parts_) * k + j] = gathered(zz, b).astype(BF)

                near_z(way).start()

            @pl.loop(0, far)
            def _(k):
                for b in range(2):
                    fars[2 * k + b] = gathered(here.z_off(4 * k), b)

            yield
            for way in range(4):
                near_z(way, True).wait_recv()
            f_send, f_recv = mine.zfar
            far_stage = mine.far_stage

            def far_copy(k):
                return remote(
                    far_stage.at[pl.ds(2 * k, 2)],
                    got_far.at[pl.ds(2 * k, 2)],
                    f_send.at[k],
                    f_recv.at[k],
                    here.along_z(here.z_off(4 * k)),
                )

            for k in sorted(range(1, far), key=lambda k: -min(k, far - k)) + [0]:
                for b in range(2):
                    total = (
                        fars[2 * k + b]
                        + got[starts[0] + 2 * k + b].astype(F32)
                        + got[starts[1] + 2 * k + b].astype(F32)
                        + got[starts[2 + b] + k].astype(F32)
                    )
                    if k:
                        far_stage[2 * k + b] = total.astype(BF)
                    else:
                        pre_i[b] = total
                if k:
                    far_copy(k).start()
            yield
            for k in range(1, far):
                far_copy(k).wait_recv()
            work = scratch.gram_user[it][-1]
            for b in range(2):
                total = pre_i[b]
                for k in range(1, far):
                    total = total + got_far[2 * k + b].astype(F32)
                pre_i[b] = total
                if h:
                    raw_i[b] = apply_inverse(
                        work, jnp.concatenate([low.pre_i[b], total], axis=0), half
                    )
                else:
                    raw_i[b] = apply_inverse(work, total)
            if it + 1 < ITERS:
                next_line = scratch.lines[h]
                for b in range(2):
                    next_line[(c * grid.z + z) * 2 + b] = raw_i[b].astype(BF)
                items = spread_z(here, next_line, 2, *mine.zall)
                ends.append(items)
                for _ in range(3):
                    next(items)
                    yield
                next(items)
            for i in range(grid.y):
                c_copy(c, (y + i) % grid.y).wait_send()
            for way in range(4):
                near_z(way).wait_send()
            for k in range(1, far):
                far_copy(k).wait_send()
        yield

    def whole_of(low, high):
        return lambda i: jnp.concatenate([low[i], high[i]], axis=0)

    chains = [chain(0), chain(1)]

    def step():
        for one in chains:
            next(one)

    gram_item = None
    for it in range(ITERS):
        if it == 0:
            step()
            step()
            query = [one.query for one in scratch.half[0]]
            residual_tiles(tables, own, query, notes, users, ratings, scratch.masks, res, res_t)
            step()
        else:
            step()
            next(gram_item)
            step()
            next(gram_item)
            next(gram_item)
        step()
        gram_user = gram_steps(here, whole_of(*(one.raw_u for one in scratch.half[it])), per, counts[0], scratch.gram_user[it])
        next(gram_user)
        step()
        next(gram_user)
        step()
        next(gram_user)
        step()
        next(gram_user)
        step()
        next(gram_user)
        next(gram_user)
        step()
        gram_item = gram_steps(here, whole_of(*(one.raw_i for one in scratch.half[it])), 2, counts[1], scratch.gram_item[it])
        next(gram_item)
        if it + 1 < ITERS:
            step()
            next(gram_item)
            step()
            next(gram_item)
    users_of = whole_of(*(one.raw_u for one in scratch.half[-1]))
    items_of = whole_of(*(one.raw_i for one in scratch.half[-1]))
    for j in range(per):
        user_out[:, j * side : (j + 1) * side] = apply_inverse(
            scratch.gram_user[ITERS - 1][-1], users_of(j)
        ).astype(BF)
    for _ in range(5):
        next(gram_item)
    for b in range(2):
        item_out[:, b * side : (b + 1) * side] = apply_inverse(
            scratch.gram_item[ITERS - 1][-1], items_of(b)
        ).astype(BF)
    for steps in ends:
        next(steps)


def main_scratch(grid, rank, side, tiles, per):
    far = grid.z // 4
    asked = grid.c * grid.y * tiles

    def vmem(n, kind=BF, rows=rank // 2):
        return pltpu.VMEM((n, rows, side), kind)

    def pair(n):
        return [sems(n), sems(n)]

    def half():
        return dict(
            sel=vmem(grid.y * tiles),
            query=vmem(grid.y * tiles),
            stage_x=vmem(grid.x * per),
            got_x=vmem(grid.x * per),
            pre_u=vmem(per, F32),
            raw_u=vmem(per, F32),
            users=vmem(grid.x * per),
            near=vmem(grid.c * grid.y * (tiles + 1)),
            stage=vmem(6 * far),
            got=vmem(6 * far),
            fars=vmem(2 * far, F32),
            far_stage=vmem(2 * far),
            got_far=vmem(2 * far),
            pre_i=vmem(2, F32),
            raw_i=vmem(2, F32),
            ysel=pair(grid.y),
            xsum=pair(grid.x),
            xall=pair(grid.x),
            ynear=pair(grid.y),
            cnear=pair(grid.y),
            znear=pair(4),
            zfar=pair(far),
            zall=spread_z_sems(grid),
        )

    return dict(
        ratings=pltpu.VMEM((tiles, side, side), BF),
        observed=pltpu.VMEM((tiles, side // 8, side), jnp.int32),
        load_sem=sems(2),
        res=pltpu.VMEM((tiles, side, side), BF),
        res_t=pltpu.VMEM((tiles, side, side), BF),
        sums=[vmem(tiles + 1, F32) for _ in range(2)],
        line=vmem(2 * grid.z * 2, BF, rank),
        lines=[vmem(2 * grid.z * 2) for _ in range(2)],
        users=vmem(grid.x * per, BF, rank),
        notes=pltpu.VMEM((2 * grid.z * grid.y, 16, side), BF),
        masks=pltpu.VMEM((tiles, side, side), BF),
        serves=pltpu.VMEM((2 * grid.z * grid.y, side), F32),
        column_v=pltpu.VMEM((8, asked), jnp.int32),
        column_s=pltpu.SMEM((8, asked), jnp.int32),
        item_v=pltpu.VMEM((grid.c * grid.y, side), jnp.int32),
        item_s=pltpu.SMEM((grid.c * grid.y, side), jnp.int32),
        table_sem=sems(2),
        note_y=pair(grid.y),
        users_x=pair(grid.x),
        line_z=spread_z_sems(grid),
        note_z=spread_z_sems(grid),
        half=[[half() for _ in range(2)] for _ in range(ITERS)],
        gram_user=[gram_scratch(grid, rank) for _ in range(ITERS)],
        gram_item=[gram_scratch(grid, rank) for _ in range(ITERS)],
    )


def main_call(grid, counts, tables, facts, item_start, user_start, ratings, observed):
    tiles, side = ratings.shape[:2]
    rank = item_start.shape[0]
    per = user_start.shape[1] // side
    scratch, tree = jax.tree.flatten(main_scratch(grid, rank, side, tiles, per))
    return pl.pallas_call(
        functools.partial(main_kernel, grid, counts, tree),
        out_shape=(
            jax.ShapeDtypeStruct((rank, per * side), BF),
            jax.ShapeDtypeStruct((rank, 2 * side), BF),
        ),
        in_specs=[pl.BlockSpec(memory_space=pltpu.SMEM)] * len(tables)
        + [pl.BlockSpec(memory_space=pltpu.VMEM)] * 3
        + [pl.BlockSpec(memory_space=pltpu.HBM)] * 2,
        out_specs=(pl.BlockSpec(memory_space=pltpu.VMEM),) * 2,
        scratch_shapes=scratch,
        compiler_params=pltpu.CompilerParams(
            collective_id=1, has_side_effects=True, vmem_limit_bytes=VMEM_LIMIT
        ),
    )(*tables, facts, item_start, user_start, ratings, observed)


def links(ids):
    at = jnp.arange(ids.shape[0], dtype=jnp.int32)
    same = (ids[:, None] == ids[None, :]) & (at[None, :] < at[:, None])
    return jnp.max(jnp.where(same, at[None, :] + 1, 0), axis=1)


def lasts(ids, n):
    tiles = ids.shape[-1]
    same = ids[..., None, :] == jnp.arange(n, dtype=jnp.int32)[:, None]
    return jnp.max(jnp.where(same, jnp.arange(1, tiles + 1, dtype=jnp.int32), 0), axis=-1)


def local(grid, ratings, observed, user_start, item_start, exposure, serve_list, tile_slot, tile_user):
    side = ratings.shape[2]
    own_users = user_start.shape[1]
    tiles = ratings.shape[0]
    owners = grid.y * grid.z * grid.c
    counts = (own_users * owners * grid.x * 1.0, item_start.shape[1] * owners * grid.x * 1.0)
    per = own_users // side
    sy, sz, sc = slots_of(grid, tile_slot)
    tables = (
        tile_user,
        sy * tiles + jnp.arange(tiles, dtype=jnp.int32),
        (sc * grid.z + sz) * grid.y + sy,
        links(tile_user),
        lasts(tile_user, grid.x * per),
    )
    rows = [exposure, jnp.pad(serve_list, (0, side - owners)), jnp.pad(tile_slot, (0, side - tiles))]
    facts = jnp.concatenate(rows + [jnp.zeros((4 * side,), jnp.int32)]).reshape(8, side)
    return main_call(grid, counts, tables, facts, item_start, user_start, ratings, observed)


def solution(mesh):
    grid = Grid(mesh.shape["rows"], mesh.shape["rep"])
    both = P(("rows", "rep"))
    second = P(None, ("rows", "rep"))
    return jax.shard_map(
        functools.partial(local, grid),
        mesh=mesh,
        in_specs=(both, both, second, second, both, both, both, both),
        out_specs=(second, second),
        check_vma=False,
    )
```
